32 devices in a mesh: grp: 2 (over x), tm: 4 (over y, core), tile: 4 (over z).
Axes of the slice: x: 2, y: 2, z: 4, core: 2. Of those that a mesh axis runs over, the one named last changes fastest.
Arguments:
- frames: bfloat16 [64, 1024, 1024], P(('grp', 'tm'), 'tile'), parts along dimension 0, may hold values from -3 to 3
- inverse_taps: float32 [48], replicated, may hold values from -3 to 3
- mode_rate: float32 [1024, 1024], P(None, 'tile'), may hold values from 0.00625 to 0.2
- frame_factor: float32 [64], P(('grp', 'tm')), parts along dimension 0, may hold values from 0.5 to 1
Outputs:
- superheat: bfloat16 [64, 1024, 1024], P(('grp', 'tm'), 'tile'), parts along dimension 0
The draws below stay inside these ranges and needn't reach their ends.
There are 2 independent parts, one for each index of `grp`. The reference program is written for one: setup_inputs(seed, part) draws one part's arguments, and reference() takes and returns one part's arrays. A program takes and returns all parts, laid end to end along the dimension named above; an argument that names none is the same for every part. Nothing has to cross between parts.
All inputs are finite; a program needn't handle non-finite values.
Results may differ from the reference program's by a relative error of at most 0.0097.
Values may be sent and summed in bfloat16 or wider, within the bound.
No kernel may reach another device: no remote copies, remote signals or barrier semaphores. Data moves between devices by JAX's collectives and lax.ppermute only.
A program may use at most 128 MiB of HBM per device.

```python
import math
import jax
import jax.numpy as jnp
from jax import lax

FRAME = 1024
TAPS = 48
SPAN_SNAPSHOTS = 32


def draw_frame_factor(key, part):
    option_selector = jax.random.fold_in(key, 11)
    level_key = jax.random.fold_in(key, 23)
    sample_bunches = jax.random.randint(option_selector, (SPAN_SNAPSHOTS,), 0, 12)
    tier_sequence = jax.random.uniform(level_key, (SPAN_SNAPSHOTS,), jnp.float32, 0.5, 0.8)
    return jnp.where(sample_bunches == 0, tier_sequence, jnp.float32(1.0)).astype(jnp.float32)


def level_of(key, dims, split, low, top_value):
    loudness, own = 1.0, jax.random.fold_in(key, 6)
    for dim, blocks in split:
        draws = jnp.exp(jax.random.uniform(jax.random.fold_in(own, dim), (blocks,), jnp.float32, low / len(split), top_value / len(split)))
        loudness = loudness * jnp.repeat(draws, dims[dim] // blocks).reshape([-1 if axis == dim else 1 for axis in range(len(dims))])
    return loudness


def scatter_about(rng, dims, scale, reach, pieces=(), kind=jnp.bfloat16):
    values = scale * jax.random.normal(rng, dims, jnp.float32)
    if pieces:
        values = values * level_of(rng, dims, pieces, -0.22, 0.18)
    return jnp.clip(values, -reach, reach).astype(kind)


def setup_inputs(seed: int = 0, part: int = 0) -> dict:
    streams_of = jax.random.split(jax.random.key(seed), 5)
    own_keys = jax.random.split(jax.random.fold_in(streams_of[4], part), 5)
    return {
        "frames": scatter_about(own_keys[0], (SPAN_SNAPSHOTS, FRAME, FRAME), 0.5, 3.0, ((0, 4), (1, 4))),
        "inverse_taps": scatter_about(streams_of[1], (TAPS,), 0.5, 3.0, (), jnp.float32),
        "mode_rate": jnp.clip(jnp.exp(math.log(0.2) - 3.465736 * jax.random.uniform(streams_of[2], (FRAME, FRAME), jnp.float32) ** level_of(streams_of[2], (FRAME, FRAME), ((1, 4),), -0.2, 0.2)), 0.00625, 0.2),
        "frame_factor": draw_frame_factor(jax.random.fold_in(jax.random.fold_in(streams_of[4], part), 71), part),
    }


def cosine_matrix(points):
    freq_idx = jnp.arange(points, dtype=jnp.int32)[:, None]
    cell_idx = jnp.arange(points, dtype=jnp.int32)[None, :]
    phase = (2 * cell_idx + 1) * freq_idx % (4 * points)
    angle = jnp.pi * phase.astype(jnp.float32) / (2.0 * points)
    values = jnp.cos(angle) * jnp.sqrt(2.0 / points)
    values = jnp.where(freq_idx == 0, values / jnp.sqrt(2.0), values)
    return values.astype(jnp.bfloat16)

def reference(frames, inverse_taps, mode_rate, frame_factor):
    frame_count = frames.shape[0]
    frame_side = frames.shape[1]
    tap_count = inverse_taps.shape[0]
    taps_b = inverse_taps.astype(jnp.bfloat16).astype(jnp.float32)
    padded = jnp.concatenate([jnp.zeros((tap_count - 1, frame_side, frame_side), jnp.bfloat16), frames], axis=0)
    wall_heat_flux = jnp.zeros((frame_count, frame_side, frame_side), jnp.float32)
    for lag_index in range(tap_count):
        start = tap_count - 1 - lag_index
        wall_heat_flux = wall_heat_flux + taps_b[lag_index] * padded[start:start + frame_count].astype(jnp.float32)
    wall_heat_flux = wall_heat_flux.astype(jnp.bfloat16)
    basis = cosine_matrix(frame_side)

    def forward(frame_now):
        column_pass = jnp.dot(frame_now, basis.T, preferred_element_type=jnp.float32).astype(jnp.bfloat16)
        return jnp.dot(basis, column_pass, preferred_element_type=jnp.float32)
    spectra = lax.map(forward, wall_heat_flux)
    retain = jnp.exp(-mode_rate)

    def advance(running, inputs):
        spectrum, factor = inputs
        running = retain * factor * running + spectrum
        return (running, running.astype(jnp.bfloat16))
    _, running_b = lax.scan(advance, jnp.zeros((frame_side, frame_side), jnp.float32), (spectra, frame_factor))

    def inverse(state_now):
        row_pass = jnp.dot(basis.T, state_now, preferred_element_type=jnp.float32).astype(jnp.bfloat16)
        return jnp.dot(row_pass, basis, preferred_element_type=jnp.float32).astype(jnp.bfloat16)
    return lax.map(inverse, running_b)
```

```python
import functools

import jax
import jax.numpy as jnp
from jax import lax
from jax.experimental import pallas as pl
from jax.experimental.pallas import tpu as pltpu
from jax.sharding import PartitionSpec as P

F32 = jnp.float32
BF16 = jnp.bfloat16
VMEM_LIMIT = 48 * 1024 * 1024


def cosine_matrix(points):
    freq_idx = jnp.arange(points, dtype=jnp.int32)[:, None]
    cell_idx = jnp.arange(points, dtype=jnp.int32)[None, :]
    phase = (2 * cell_idx + 1) * freq_idx % (4 * points)
    angle = jnp.pi * phase.astype(jnp.float32) / (2.0 * points)
    values = jnp.cos(angle) * jnp.sqrt(2.0 / points)
    values = jnp.where(freq_idx == 0, values / jnp.sqrt(2.0), values)
    return values.astype(jnp.bfloat16)


def dot(a, b, a_dim, b_dim):
    return lax.dot_general(a, b, (((a_dim,), (b_dim,)), ((), ())), preferred_element_type=F32)


def columns_kernel(frames_ref, basis_ref, out_ref):
    owners, _, own_modes, rows = out_ref.shape
    modes = dot(basis_ref[...], frames_ref[0], 1, 1)
    out_ref[...] = modes.astype(BF16).reshape(owners, 1, own_modes, rows)


def forward_columns(frames, basis, owners):
    span, rows, side = frames.shape
    own_modes = side // owners
    return pl.pallas_call(
        columns_kernel,
        grid=(span,),
        in_specs=[
            pl.BlockSpec((1, rows, side), lambda f: (f, 0, 0)),
            pl.BlockSpec((side, side), lambda f: (0, 0)),
        ],
        out_specs=pl.BlockSpec((owners, 1, own_modes, rows), lambda f: (0, f, 0, 0)),
        out_shape=jax.ShapeDtypeStruct((owners, span, own_modes, rows), BF16),
        compiler_params=pltpu.CompilerParams(vmem_limit_bytes=VMEM_LIMIT),
        cost_estimate=pl.CostEstimate(
            flops=2 * span * rows * side * side,
            bytes_accessed=4 * span * rows * side + 2 * side * side,
            transcendentals=0,
        ),
        name="columns",
    )(frames, basis)


def modes_kernel(tiles, factor_ref, in_ref, filter_ref, rate_ref, basis_ref, out_ref, spectra_ref, running_ref):
    owners, span, batch, rows = in_ref.shape
    blocks = owners // tiles
    frames = blocks * span
    filtered = []
    for tile in range(tiles):
        piece = in_ref[tile * blocks:(tile + 1) * blocks].reshape(frames * batch, rows)
        filtered.append(dot(filter_ref[...], piece, 1, 0).astype(BF16))
    column_pass = jnp.concatenate(filtered, axis=1)
    spectra_ref[...] = dot(column_pass, basis_ref[...], 1, 1)
    retain = jnp.exp(-rate_ref[...])
    state = jnp.zeros_like(retain)
    for frame in range(frames):
        at = slice(frame * batch, (frame + 1) * batch)
        state = retain * factor_ref[frame] * state + spectra_ref[at]
        running_ref[at] = state.astype(BF16)
    row_pass = dot(running_ref[...], basis_ref[...], 1, 0).astype(BF16)
    for tile in range(tiles):
        out_ref[tile * blocks:(tile + 1) * blocks] = row_pass[:, tile * rows:(tile + 1) * rows].reshape(
            blocks, span, batch, rows
        )


def in_modes(received, factors, filter_matrix, rate, basis, tiles, batch):
    owners, span, own_modes, rows = received.shape
    side = basis.shape[0]
    frames = owners // tiles * span
    block = pl.BlockSpec((owners, span, batch, rows), lambda k: (0, 0, k, 0))
    return pl.pallas_call(
        functools.partial(modes_kernel, tiles),
        grid=(own_modes // batch,),
        in_specs=[
            pl.BlockSpec(memory_space=pltpu.SMEM),
            block,
            pl.BlockSpec(filter_matrix.shape, lambda k: (0, 0)),
            pl.BlockSpec((batch, side), lambda k: (k, 0)),
            pl.BlockSpec((side, side), lambda k: (0, 0)),
        ],
        out_specs=block,
        out_shape=jax.ShapeDtypeStruct(received.shape, BF16),
        scratch_shapes=[
            pltpu.VMEM((frames * batch, side), F32),
            pltpu.VMEM((frames * batch, side), BF16),
        ],
        compiler_params=pltpu.CompilerParams(vmem_limit_bytes=VMEM_LIMIT),
        cost_estimate=pl.CostEstimate(
            flops=4 * frames * own_modes * side * side,
            bytes_accessed=4 * frames * own_modes * side + 2 * side * side,
            transcendentals=own_modes * side,
        ),
        name="in_modes",
    )(factors, received, filter_matrix, rate, basis)


def back_kernel(in_ref, basis_ref, out_ref):
    owners, _, own_modes, rows = in_ref.shape
    row_pass = in_ref[...].reshape(owners * own_modes, rows)
    out_ref[0] = dot(row_pass, basis_ref[...], 0, 0).astype(BF16)


def back_columns(received, basis):
    owners, span, own_modes, rows = received.shape
    side = basis.shape[0]
    return pl.pallas_call(
        back_kernel,
        grid=(span,),
        in_specs=[
            pl.BlockSpec((owners, 1, own_modes, rows), lambda f: (0, f, 0, 0)),
            pl.BlockSpec((side, side), lambda f: (0, 0)),
        ],
        out_specs=pl.BlockSpec((1, rows, side), lambda f: (f, 0, 0)),
        out_shape=jax.ShapeDtypeStruct((span, rows, side), BF16),
        compiler_params=pltpu.CompilerParams(vmem_limit_bytes=VMEM_LIMIT),
        cost_estimate=pl.CostEstimate(
            flops=2 * span * rows * side * side,
            bytes_accessed=4 * span * rows * side + 2 * side * side,
            transcendentals=0,
        ),
        name="back_columns",
    )(received, basis)


def filter_over(taps_b, frames, batch):
    tap_count = taps_b.shape[0]
    lag = jnp.arange(frames)[:, None] - jnp.arange(frames)[None, :]
    onehot = lag[:, :, None] == jnp.arange(tap_count)[None, None, :]
    toeplitz = jnp.sum(jnp.where(onehot, taps_b[None, None, :], 0.0), axis=2).astype(BF16)
    same = jnp.eye(batch, dtype=BF16)
    return (toeplitz[:, None, :, None] * same[None, :, None, :]).reshape(frames * batch, frames * batch)


def on_device(frames, inverse_taps, mode_rate, frame_factor):
    span, rows, side = frames.shape
    blocks, tiles = lax.axis_size("tm"), lax.axis_size("tile")
    owners = blocks * tiles
    own_modes = side // owners
    batch = min(16, own_modes)
    basis = cosine_matrix(side)
    taps_b = inverse_taps.astype(BF16).astype(F32)
    filter_matrix = filter_over(taps_b, blocks * span, batch)
    factors = lax.all_gather(frame_factor, "tm", tiled=True)
    rate = lax.dynamic_slice_in_dim(mode_rate, lax.axis_index("tm") * own_modes, own_modes, 1).T

    def exchange(block):
        return lax.all_to_all(block, ("tile", "tm"), split_axis=0, concat_axis=0, tiled=True)

    received = exchange(forward_columns(frames, basis, owners))
    returned = exchange(in_modes(received, factors, filter_matrix, rate, basis, tiles, batch))
    return back_columns(returned, basis)


def solution(mesh):
    return jax.shard_map(
        on_device,
        mesh=mesh,
        in_specs=(P(("grp", "tm"), "tile", None), P(), P(None, "tile"), P(("grp", "tm"))),
        out_specs=P(("grp", "tm"), "tile", None),
        check_vma=False,
    )
```

```python
import functools

import jax
import jax.numpy as jnp
import numpy as np
from jax import lax
from jax.experimental import pallas as pl
from jax.experimental.pallas import tpu as pltpu
from jax.sharding import PartitionSpec as P

F32 = jnp.float32
BF16 = jnp.bfloat16
VMEM_LIMIT = 48 * 1024 * 1024


def cosine_matrix(points):
    freq_idx = np.arange(points)[:, None]
    cell_idx = np.arange(points)[None, :]
    phase = (2 * cell_idx + 1) * freq_idx % (4 * points)
    values = np.cos(np.pi * phase / (2.0 * points)) * np.sqrt(2.0 / points)
    values = np.where(freq_idx == 0, values / np.sqrt(2.0), values)
    return values.astype(np.float32).astype(BF16)


def dot(a, b, a_dim, b_dim):
    return lax.dot_general(a, b, (((a_dim,), (b_dim,)), ((), ())), preferred_element_type=F32)


def cost(flops, bytes_accessed):
    return pl.CostEstimate(flops=flops, bytes_accessed=bytes_accessed, transcendentals=0)


PARAMS = pltpu.CompilerParams(vmem_limit_bytes=VMEM_LIMIT)


def columns_kernel(frames_ref, basis_ref, out_ref):
    modes = dot(basis_ref[...], frames_ref[0], 1, 1)
    out_ref[...] = modes.astype(BF16).reshape(out_ref.shape)


def forward_columns(frames, basis, owners):
    span, rows, side = frames.shape
    count = basis.shape[0]
    own_modes = count // owners
    return pl.pallas_call(
        columns_kernel,
        grid=(span,),
        in_specs=[
            pl.BlockSpec((1, rows, side), lambda f: (f, 0, 0)),
            pl.BlockSpec((count, side), lambda f: (0, 0)),
        ],
        out_specs=pl.BlockSpec((owners, 1, own_modes, rows), lambda f: (0, f, 0, 0)),
        out_shape=jax.ShapeDtypeStruct((owners, span, own_modes, rows), BF16),
        compiler_params=PARAMS,
        cost_estimate=cost(2 * span * rows * side * count, 2 * span * rows * (side + count) + 2 * side * count),
        name="columns",
    )(frames, basis)


def modes_kernel(tiles, out_count, factor_ref, in_ref, filter_ref, rate_ref, basis_ref, *refs):
    out_refs, (spectra_ref, running_ref) = refs[:out_count], refs[out_count:]
    owners, span, batch, rows = in_ref.shape
    blocks = owners // tiles
    frames = blocks * span
    filtered = []
    for tile in range(tiles):
        piece = in_ref[tile * blocks:(tile + 1) * blocks].reshape(frames * batch, rows)
        filtered.append(dot(filter_ref[...], piece, 1, 0).astype(BF16))
    column_pass = jnp.concatenate(filtered, axis=1)
    spectra_ref[...] = dot(column_pass, basis_ref[...], 1, 1)
    retain = jnp.exp(-rate_ref[...])
    state = jnp.zeros_like(retain)
    for frame in range(frames):
        at = slice(frame * batch, (frame + 1) * batch)
        state = retain * factor_ref[frame] * state + spectra_ref[at]
        running_ref[at] = state.astype(BF16)
    row_pass = dot(running_ref[...], basis_ref[...], 1, 0).astype(BF16)
    part = span // out_count
    for tile in range(tiles):
        piece = row_pass[:, tile * rows:(tile + 1) * rows].reshape(blocks, span, batch, rows)
        for i, out_ref in enumerate(out_refs):
            out_ref[tile * blocks:(tile + 1) * blocks] = piece[:, i * part:(i + 1) * part]


def in_modes(received, factors, filter_matrix, rate, basis, tiles, batch, out_count):
    owners, span, own_modes, rows = received.shape
    side = basis.shape[0]
    frames = owners // tiles * span
    part = span // out_count
    return pl.pallas_call(
        functools.partial(modes_kernel, tiles, out_count),
        grid=(own_modes // batch,),
        in_specs=[
            pl.BlockSpec(memory_space=pltpu.SMEM),
            pl.BlockSpec((owners, span, batch, rows), lambda k: (0, 0, k, 0)),
            pl.BlockSpec(filter_matrix.shape, lambda k: (0, 0)),
            pl.BlockSpec((batch, side), lambda k: (k, 0)),
            pl.BlockSpec((side, side), lambda k: (0, 0)),
        ],
        out_specs=[pl.BlockSpec((owners, part, batch, rows), lambda k: (0, 0, k, 0))] * out_count,
        out_shape=[jax.ShapeDtypeStruct((owners, part, own_modes, rows), BF16)] * out_count,
        scratch_shapes=[
            pltpu.VMEM((frames * batch, side), F32),
            pltpu.VMEM((frames * batch, side), BF16),
        ],
        compiler_params=PARAMS,
        cost_estimate=cost(5 * frames * own_modes * side * side, 4 * frames * own_modes * side + 2 * side * side),
        name="in_modes",
    )(factors, received, filter_matrix, rate, basis)


def back_kernel(count, *refs):
    in_refs, basis_refs, out_ref = refs[:count], refs[count:2 * count], refs[-1]
    total = 0.0
    for in_ref, basis_ref in zip(in_refs, basis_refs):
        row_pass = in_ref[...].reshape(basis_ref.shape[0], in_ref.shape[-1])
        total = total + dot(row_pass, basis_ref[...], 0, 0)
    out_ref[0] = total.astype(BF16)


def back_columns(pieces, bases, first, frames, span, earlier):
    side = bases[0].shape[1]
    rows = pieces[0][0].shape[-1]
    count = len(pieces)
    in_specs = []
    for array, start in pieces:
        owners, _, own_modes, _ = array.shape
        in_specs.append(pl.BlockSpec((owners, 1, own_modes, rows), lambda f, start=start: (0, f + start, 0, 0)))
    in_specs += [pl.BlockSpec(basis.shape, lambda f: (0, 0)) for basis in bases]
    operands = [array for array, _ in pieces] + list(bases)
    aliases = {}
    body = functools.partial(back_kernel, count)
    if earlier is not None:
        in_specs.append(pl.BlockSpec(memory_space=pl.ANY))
        aliases = {len(operands): 0}
        operands.append(earlier)
    return pl.pallas_call(
        body,
        grid=(frames,),
        in_specs=in_specs,
        out_specs=pl.BlockSpec((1, rows, side), lambda f: (f + first, 0, 0)),
        out_shape=jax.ShapeDtypeStruct((span, rows, side), BF16),
        input_output_aliases=aliases,
        compiler_params=PARAMS,
        cost_estimate=cost(2 * frames * rows * side * side, 4 * frames * rows * side + 2 * side * side),
        name="back_columns",
    )(*operands)


def filter_over(taps_b, frames, batch):
    tap_count = taps_b.shape[0]
    lag = np.arange(frames)[:, None] - np.arange(frames)[None, :]
    onehot = lag[:, :, None] == np.arange(tap_count)
    toeplitz = jnp.sum(jnp.where(onehot, taps_b[None, None, :], 0.0), axis=2).astype(BF16)
    index = np.arange(frames * batch)
    spread = (index[:, None] // batch == np.arange(frames)[None, :]).astype(BF16)
    over_rows = dot(spread, toeplitz, 1, 0).astype(BF16)
    over_both = dot(over_rows, spread, 1, 1).astype(BF16)
    same_mode = index[:, None] % batch == index[None, :] % batch
    return jnp.where(same_mode, over_both, jnp.zeros((), BF16))


def on_device(frames, inverse_taps, mode_rate, frame_factor):
    span, rows, side = frames.shape
    blocks, tiles = lax.axis_size("tm"), lax.axis_size("tile")
    owners = blocks * tiles
    own_modes = side // owners
    batch = min(16, own_modes)
    chunks = 2 if own_modes // batch % 2 == 0 else 1
    chunk_modes = own_modes // chunks

    matrix = cosine_matrix(side)
    by_chunk = matrix.reshape(owners, chunks, chunk_modes, side).swapaxes(0, 1)
    bases = [jnp.asarray(by_chunk[c].reshape(owners * chunk_modes, side)) for c in range(chunks)]
    basis = jnp.asarray(matrix)

    taps_b = inverse_taps.astype(BF16).astype(F32)
    filter_matrix = filter_over(taps_b, blocks * span, batch)
    factors = lax.all_gather(frame_factor, "tm", tiled=True)
    rate = lax.dynamic_slice_in_dim(mode_rate, lax.axis_index("tm") * own_modes, own_modes, 1).T

    def exchange(block):
        return lax.all_to_all(block, ("tile", "tm"), split_axis=0, concat_axis=0, tiled=True)

    received = [exchange(forward_columns(frames, bases[c], owners)) for c in range(chunks)]
    halves = 2 if span % 2 == 0 else 1
    returned = []
    for c in range(chunks):
        out_count = halves if c == chunks - 1 else 1
        own_rate = rate[c * chunk_modes:(c + 1) * chunk_modes]
        outs = in_modes(received[c], factors, filter_matrix, own_rate, basis, tiles, batch, out_count)
        returned.append([exchange(out) for out in outs])
    part = span // halves
    result = None
    for half in range(halves):
        pieces = [(arrays[0], half * part) for arrays in returned[:-1]] + [(returned[-1][half], 0)]
        result = back_columns(pieces, bases, half * part, part, span, result)
    return result


def solution(mesh):
    return jax.shard_map(
        on_device,
        mesh=mesh,
        in_specs=(P(("grp", "tm"), "tile", None), P(), P(None, "tile"), P(("grp", "tm"))),
        out_specs=P(("grp", "tm"), "tile", None),
        check_vma=False,
    )
```

```python
import functools

import jax
import jax.numpy as jnp
import numpy as np
from jax import lax
from jax.experimental import pallas as pl
from jax.experimental.pallas import tpu as pltpu
from jax.sharding import PartitionSpec as P

F32 = jnp.float32
BF16 = jnp.bfloat16
MIB = 1024 * 1024
GROUP = ("tile", "tm")
MOST_MESSAGES = 16


def cosine_matrix(points):
    freq_idx = np.arange(points)[:, None]
    cell_idx = np.arange(points)[None, :]
    phase = (2 * cell_idx + 1) * freq_idx % (4 * points)
    values = np.cos(np.pi * phase / (2.0 * points)) * np.sqrt(2.0 / points)
    values = np.where(freq_idx == 0, values / np.sqrt(2.0), values)
    return values.astype(np.float32).astype(BF16)


def dot(a, b, a_dim, b_dim):
    return lax.dot_general(a, b, (((a_dim,), (b_dim,)), ((), ())), preferred_element_type=F32)


def cost(flops, bytes_accessed):
    return pl.CostEstimate(flops=flops, bytes_accessed=bytes_accessed, transcendentals=0)


SMEM = pl.BlockSpec(memory_space=pltpu.SMEM)


def whole(array):
    return pl.BlockSpec(array.shape, lambda step: (0,) * array.ndim)


def gathered(refs, first, count):
    each = refs[0].shape[0]
    if len(refs) == 1:
        return refs[0][first:first + count]
    return jnp.concatenate([refs[i][...] for i in range(first // each, (first + count) // each)], axis=0)


def permute_row_blocks(flip, source_ref, target_ref, blocks):
    size = source_ref.shape[0] // blocks
    for d in range(blocks):
        at = pl.ds(pl.multiple_of((d ^ flip) * size, size), size)
        target_ref[d * size:(d + 1) * size] = source_ref[at]


def columns_kernel(owners, flip_ref, frames_ref, basis_ref, *refs):
    out_refs, ordered_ref = refs[:-1], refs[-1]

    @pl.when(pl.program_id(0) == 0)
    def _():
        permute_row_blocks(flip_ref[2], basis_ref, ordered_ref, owners)

    modes = dot(ordered_ref[...], frames_ref[0], 1, 1).astype(BF16)
    size = modes.shape[0] // len(out_refs)
    for i, out_ref in enumerate(out_refs):
        out_ref[...] = modes[i * size:(i + 1) * size].reshape(out_ref.shape)


def forward_columns(flip, frames, basis, owners, messages):
    span, rows, side = frames.shape
    own_modes = side // owners
    each = owners // messages
    return pl.pallas_call(
        functools.partial(columns_kernel, owners),
        grid=(span,),
        in_specs=[SMEM, pl.BlockSpec((1, rows, side), lambda f: (f, 0, 0)), whole(basis)],
        out_specs=[pl.BlockSpec((each, 1, own_modes, rows), lambda f: (0, f, 0, 0))] * messages,
        out_shape=[jax.ShapeDtypeStruct((each, span, own_modes, rows), BF16)] * messages,
        scratch_shapes=[pltpu.VMEM(basis.shape, BF16)],
        compiler_params=pltpu.CompilerParams(vmem_limit_bytes=20 * MIB),
        cost_estimate=cost(2 * span * rows * side * side, 4 * span * rows * side + 2 * side * side),
        name="columns",
    )(flip, frames, basis)


def modes_kernel(tiles, messages, flip_ref, factor_ref, *refs):
    in_refs = refs[:messages]
    filter_ref, rate_ref, basis_ref = refs[messages:messages + 3]
    out_refs = refs[messages + 3:2 * messages + 3]
    ordered_ref, spectra_ref, running_ref = refs[2 * messages + 3:]
    each, span, batch, rows = in_refs[0].shape
    owners = each * messages
    blocks = owners // tiles
    frames = blocks * span
    flip_tile, flip_block = flip_ref[0], flip_ref[1]

    @pl.when(pl.program_id(0) == 0)
    def _():
        for d in range(tiles):
            at = pl.ds(pl.multiple_of((d ^ flip_tile) * rows, rows), rows)
            ordered_ref[:, d * rows:(d + 1) * rows] = basis_ref[:, at]

    filtered = []
    for d in range(tiles):
        piece = gathered(in_refs, d * blocks, blocks).reshape(frames * batch, rows)
        filtered.append(dot(filter_ref[...], piece, 1, 0).astype(BF16))
    column_pass = jnp.concatenate(filtered, axis=1)
    spectra_ref[...] = dot(column_pass, ordered_ref[...], 1, 1)
    retain = jnp.exp(-rate_ref[...])
    state = jnp.zeros_like(retain)
    for frame in range(frames):
        state = retain * factor_ref[frame] * state + spectra_ref[frame * batch:(frame + 1) * batch]
        if messages == 1:
            at = slice(frame * batch, (frame + 1) * batch)
        else:
            place = ((frame // span) ^ flip_block) * span + frame % span
            at = pl.ds(pl.multiple_of(place * batch, batch), batch)
        running_ref[at] = state.astype(BF16)
    row_pass = dot(running_ref[...], ordered_ref[...], 1, 0).astype(BF16)
    for d in range(tiles):
        piece = row_pass[:, d * rows:(d + 1) * rows].reshape(blocks, span, batch, rows)
        if messages == 1:
            out_refs[0][d * blocks:(d + 1) * blocks] = piece
        else:
            for i in range(0, blocks, each):
                out_refs[(d * blocks + i) // each][...] = piece[i:i + each]


def in_modes(flip, received, factors, filter_matrix, rate, basis, tiles, batch):
    each, span, own_modes, rows = received[0].shape
    messages = len(received)
    side = basis.shape[0]
    frames = each * messages // tiles * span
    block = pl.BlockSpec((each, span, batch, rows), lambda k: (0, 0, k, 0))
    return pl.pallas_call(
        functools.partial(modes_kernel, tiles, messages),
        grid=(own_modes // batch,),
        in_specs=[SMEM, SMEM]
        + [block] * messages
        + [whole(filter_matrix), pl.BlockSpec((batch, side), lambda k: (k, 0)), whole(basis)],
        out_specs=[block] * messages,
        out_shape=[jax.ShapeDtypeStruct(received[0].shape, BF16)] * messages,
        scratch_shapes=[
            pltpu.VMEM(basis.shape, BF16),
            pltpu.VMEM((frames * batch, side), F32),
            pltpu.VMEM((frames * batch, side), BF16),
        ],
        compiler_params=pltpu.CompilerParams(vmem_limit_bytes=36 * MIB),
        cost_estimate=cost(5 * frames * own_modes * side * side, 4 * frames * own_modes * side + 2 * side * side),
        name="in_modes",
    )(flip, factors, *received, filter_matrix, rate, basis)


def back_kernel(owners, flip_ref, *refs):
    in_refs, (basis_ref, out_ref, ordered_ref) = refs[:-3], refs[-3:]

    @pl.when(pl.program_id(0) == 0)
    def _():
        permute_row_blocks(flip_ref[2], basis_ref, ordered_ref, owners)

    row_pass = gathered(in_refs, 0, owners).reshape(basis_ref.shape[0], in_refs[0].shape[-1])
    out_ref[0] = dot(row_pass, ordered_ref[...], 0, 0).astype(BF16)


def back_columns(flip, received, basis):
    each, span, own_modes, rows = received[0].shape
    side = basis.shape[1]
    return pl.pallas_call(
        functools.partial(back_kernel, each * len(received)),
        grid=(span,),
        in_specs=[SMEM]
        + [pl.BlockSpec((each, 1, own_modes, rows), lambda f: (0, f, 0, 0))] * len(received)
        + [whole(basis)],
        out_specs=pl.BlockSpec((1, rows, side), lambda f: (f, 0, 0)),
        out_shape=jax.ShapeDtypeStruct((span, rows, side), BF16),
        scratch_shapes=[pltpu.VMEM(basis.shape, BF16)],
        compiler_params=pltpu.CompilerParams(vmem_limit_bytes=20 * MIB),
        cost_estimate=cost(2 * span * rows * side * side, 4 * span * rows * side + 2 * side * side),
        name="back_columns",
    )(flip, *received, basis)


def filter_over(taps_b, blocks, span, batch, flip_block):
    tap_count = taps_b.shape[0]
    frames = blocks * span
    place = np.arange(frames)
    source = (place // span ^ flip_block) * span + place % span
    lag = np.arange(frames)[:, None] - source[None, :]
    onehot = lag[:, :, None] == np.arange(tap_count)
    toeplitz = jnp.sum(jnp.where(onehot, taps_b[None, None, :], 0.0), axis=2).astype(BF16)
    index = np.arange(frames * batch)
    spread = (index[:, None] // batch == np.arange(frames)[None, :]).astype(BF16)
    over_rows = dot(spread, toeplitz, 1, 0).astype(BF16)
    over_both = dot(over_rows, spread, 1, 1).astype(BF16)
    same_mode = index[:, None] % batch == index[None, :] % batch
    return jnp.where(same_mode, over_both, jnp.zeros((), BF16))


def exchange(blocks):
    if len(blocks) == 1:
        return [lax.all_to_all(blocks[0], GROUP, split_axis=0, concat_axis=0, tiled=True)]
    tiles, times = lax.axis_size("tile"), lax.axis_size("tm")
    index = [[time * tiles + tile for time in range(times)] for tile in range(tiles)]
    arrived = list(blocks)
    order = sorted(range(1, len(blocks)), key=lambda d: (-(d % times * 5 + d // times * 3) % len(blocks), d))
    for d in order:
        off_tile, off_time = d // times, d % times
        route = [
            (index[tile][time], index[tile ^ off_tile][time ^ off_time])
            for tile in range(tiles)
            for time in range(times)
        ]
        arrived[d] = lax.ppermute(blocks[d], ("tm", "tile"), route)
    return arrived


def on_device(frames, inverse_taps, mode_rate, frame_factor):
    span, rows, side = frames.shape
    blocks, tiles = lax.axis_size("tm"), lax.axis_size("tile")
    owners = blocks * tiles
    own_modes = side // owners
    batch = min(16, own_modes)
    by_pairs = owners <= MOST_MESSAGES and owners & (owners - 1) == 0
    messages = owners if by_pairs else 1
    own_block, own_tile = lax.axis_index("tm"), lax.axis_index("tile")
    flip = jnp.stack([own_tile, own_block, own_tile * blocks + own_block]).astype(jnp.int32)
    if not by_pairs:
        flip = jnp.zeros_like(flip)

    basis = jnp.asarray(cosine_matrix(side))
    taps_b = inverse_taps.astype(BF16).astype(F32)
    filter_matrix = filter_over(taps_b, blocks, span, batch, flip[1])
    factors = lax.all_gather(frame_factor, "tm", tiled=True)
    rate = lax.dynamic_slice_in_dim(mode_rate, own_block * own_modes, own_modes, 1).T

    received = exchange(forward_columns(flip, frames, basis, owners, messages))
    returned = exchange(in_modes(flip, received, factors, filter_matrix, rate, basis, tiles, batch))
    return back_columns(flip, returned, basis)


def solution(mesh):
    return jax.shard_map(
        on_device,
        mesh=mesh,
        in_specs=(P(("grp", "tm"), "tile", None), P(), P(None, "tile"), P(("grp", "tm"))),
        out_specs=P(("grp", "tm"), "tile", None),
        check_vma=False,
    )
```

```python
import functools

import jax
import jax.numpy as jnp
import numpy as np
from jax import lax
from jax.experimental import pallas as pl
from jax.experimental.pallas import tpu as pltpu
from jax.sharding import PartitionSpec as P

F32 = jnp.float32
BF16 = jnp.bfloat16
MIB = 1024 * 1024
GROUP = ("tile", "tm")
MOST_MESSAGES = 16


def cosine_matrix(points):
    freq_idx = np.arange(points)[:, None]
    cell_idx = np.arange(points)[None, :]
    phase = (2 * cell_idx + 1) * freq_idx % (4 * points)
    values = np.cos(np.pi * phase / (2.0 * points)) * np.sqrt(2.0 / points)
    values = np.where(freq_idx == 0, values / np.sqrt(2.0), values)
    return values.astype(np.float32).astype(BF16)


def dot(a, b, a_dim, b_dim):
    return lax.dot_general(a, b, (((a_dim,), (b_dim,)), ((), ())), preferred_element_type=F32)


def cost(flops, bytes_accessed):
    return pl.CostEstimate(flops=flops, bytes_accessed=bytes_accessed, transcendentals=0)


SMEM = pl.BlockSpec(memory_space=pltpu.SMEM)


def whole(array):
    return pl.BlockSpec(array.shape, lambda step: (0,) * array.ndim)


def gathered(refs, first, count):
    each = refs[0].shape[0]
    if len(refs) == 1:
        return refs[0][first:first + count]
    return jnp.concatenate([refs[i][...] for i in range(first // each, (first + count) // each)], axis=0)


def permute_row_blocks(flip, source_ref, target_ref, blocks):
    size = source_ref.shape[0] // blocks
    for d in range(blocks):
        at = pl.ds(pl.multiple_of((d ^ flip) * size, size), size)
        target_ref[d * size:(d + 1) * size] = source_ref[at]


def columns_kernel(owners, flip_ref, frames_ref, basis_ref, *refs):
    out_refs, ordered_ref = refs[:-1], refs[-1]

    @pl.when(pl.program_id(0) == 0)
    def _():
        permute_row_blocks(flip_ref[2], basis_ref, ordered_ref, owners)

    modes = dot(ordered_ref[...], frames_ref[0], 1, 1).astype(BF16)
    size = modes.shape[0] // len(out_refs)
    for i, out_ref in enumerate(out_refs):
        out_ref[...] = modes[i * size:(i + 1) * size].reshape(out_ref.shape)


def forward_columns(flip, frames, basis, owners, messages):
    span, rows, side = frames.shape
    own_modes = side // owners
    each = owners // messages
    return pl.pallas_call(
        functools.partial(columns_kernel, owners),
        grid=(span,),
        in_specs=[SMEM, pl.BlockSpec((1, rows, side), lambda f: (f, 0, 0)), whole(basis)],
        out_specs=[pl.BlockSpec((each, 1, own_modes, rows), lambda f: (0, f, 0, 0))] * messages,
        out_shape=[jax.ShapeDtypeStruct((each, span, own_modes, rows), BF16)] * messages,
        scratch_shapes=[pltpu.VMEM(basis.shape, BF16)],
        compiler_params=pltpu.CompilerParams(vmem_limit_bytes=60 * MIB),
        cost_estimate=cost(2 * span * rows * side * side, 4 * span * rows * side + 2 * side * side),
        name="columns",
    )(flip, frames, basis)


def modes_kernel(tiles, messages, flip_ref, factor_ref, *refs):
    in_refs = refs[:messages]
    filter_ref, rate_ref, basis_ref = refs[messages:messages + 3]
    out_refs = refs[messages + 3:2 * messages + 3]
    ordered_ref, spectra_ref, running_ref = refs[2 * messages + 3:]
    each, span, batch, rows = in_refs[0].shape
    owners = each * messages
    blocks = owners // tiles
    frames = blocks * span
    flip_tile, flip_block = flip_ref[0], flip_ref[1]

    @pl.when(pl.program_id(0) == 0)
    def _():
        for d in range(tiles):
            at = pl.ds(pl.multiple_of((d ^ flip_tile) * rows, rows), rows)
            ordered_ref[:, d * rows:(d + 1) * rows] = basis_ref[:, at]

    filtered = []
    for d in range(tiles):
        piece = gathered(in_refs, d * blocks, blocks).reshape(frames * batch, rows)
        filtered.append(dot(filter_ref[...], piece, 1, 0).astype(BF16))
    column_pass = jnp.concatenate(filtered, axis=1)
    spectra_ref[...] = dot(column_pass, ordered_ref[...], 1, 1)
    retain = jnp.exp(-rate_ref[...])
    state = jnp.zeros_like(retain)
    for frame in range(frames):
        here = slice(frame * batch, (frame + 1) * batch)
        place, there = frame, here
        if messages > 1:
            place = ((frame // span) ^ flip_block) * span + frame % span
            there = pl.ds(pl.multiple_of(place * batch, batch), batch)
        state = retain * factor_ref[place] * state + spectra_ref[here]
        running_ref[there] = state.astype(BF16)
    row_pass = dot(running_ref[...], ordered_ref[...], 1, 0).astype(BF16)
    for d in range(tiles):
        piece = row_pass[:, d * rows:(d + 1) * rows].reshape(blocks, span, batch, rows)
        if messages == 1:
            out_refs[0][d * blocks:(d + 1) * blocks] = piece
        else:
            for i in range(0, blocks, each):
                out_refs[(d * blocks + i) // each][...] = piece[i:i + each]


def in_modes(flip, received, factors, filter_matrix, rate, basis, tiles, batch):
    each, span, own_modes, rows = received[0].shape
    messages = len(received)
    side = basis.shape[0]
    frames = each * messages // tiles * span
    block = pl.BlockSpec((each, span, batch, rows), lambda k: (0, 0, k, 0))
    return pl.pallas_call(
        functools.partial(modes_kernel, tiles, messages),
        grid=(own_modes // batch,),
        in_specs=[SMEM, SMEM]
        + [block] * messages
        + [whole(filter_matrix), pl.BlockSpec((batch, side), lambda k: (k, 0)), whole(basis)],
        out_specs=[block] * messages,
        out_shape=[jax.ShapeDtypeStruct(received[0].shape, BF16)] * messages,
        scratch_shapes=[
            pltpu.VMEM(basis.shape, BF16),
            pltpu.VMEM((frames * batch, side), F32),
            pltpu.VMEM((frames * batch, side), BF16),
        ],
        compiler_params=pltpu.CompilerParams(vmem_limit_bytes=60 * MIB),
        cost_estimate=cost(5 * frames * own_modes * side * side, 4 * frames * own_modes * side + 2 * side * side),
        name="in_modes",
    )(flip, factors, *received, filter_matrix, rate, basis)


def back_kernel(owners, flip_ref, *refs):
    in_refs, (basis_ref, out_ref, ordered_ref) = refs[:-3], refs[-3:]

    @pl.when(pl.program_id(0) == 0)
    def _():
        permute_row_blocks(flip_ref[2], basis_ref, ordered_ref, owners)

    row_pass = gathered(in_refs, 0, owners).reshape(basis_ref.shape[0], in_refs[0].shape[-1])
    out_ref[0] = dot(row_pass, ordered_ref[...], 0, 0).astype(BF16)


def back_columns(flip, received, basis):
    each, span, own_modes, rows = received[0].shape
    side = basis.shape[1]
    return pl.pallas_call(
        functools.partial(back_kernel, each * len(received)),
        grid=(span,),
        in_specs=[SMEM]
        + [pl.BlockSpec((each, 1, own_modes, rows), lambda f: (0, f, 0, 0))] * len(received)
        + [whole(basis)],
        out_specs=pl.BlockSpec((1, rows, side), lambda f: (f, 0, 0)),
        out_shape=jax.ShapeDtypeStruct((span, rows, side), BF16),
        scratch_shapes=[pltpu.VMEM(basis.shape, BF16)],
        compiler_params=pltpu.CompilerParams(vmem_limit_bytes=60 * MIB),
        cost_estimate=cost(2 * span * rows * side * side, 4 * span * rows * side + 2 * side * side),
        name="back_columns",
    )(flip, *received, basis)


def filter_over(taps_b, blocks, span, batch, flip_block):
    tap_count = taps_b.shape[0]
    frames = blocks * span
    place = np.arange(frames)
    source = (place // span ^ flip_block) * span + place % span
    lag = np.arange(frames)[:, None] - source[None, :]
    onehot = lag[:, :, None] == np.arange(tap_count)
    toeplitz = jnp.sum(jnp.where(onehot, taps_b[None, None, :], 0.0), axis=2).astype(BF16)
    index = np.arange(frames * batch)
    spread = (index[:, None] // batch == np.arange(frames)[None, :]).astype(BF16)
    over_rows = dot(spread, toeplitz, 1, 0).astype(BF16)
    over_both = dot(over_rows, spread, 1, 1).astype(BF16)
    same_mode = index[:, None] % batch == index[None, :] % batch
    return jnp.where(same_mode, over_both, jnp.zeros((), BF16))


def send(block, move):
    tiles, times = lax.axis_size("tile"), lax.axis_size("tm")
    route = []
    for time in range(times):
        for tile in range(tiles):
            to_tile, to_time = move(tile, time)
            route.append((time * tiles + tile, to_time * tiles + to_tile))
    return lax.ppermute(block, ("tm", "tile"), route)


def exchange(blocks):
    if len(blocks) == 1:
        return [lax.all_to_all(blocks[0], GROUP, split_axis=0, concat_axis=0, tiled=True)]
    tiles, times = lax.axis_size("tile"), lax.axis_size("tm")
    far = tiles // 2

    def direct(d_tile, d_time):
        block = blocks[d_tile * times + d_time]
        arrived[d_tile, d_time] = send(block, lambda tile, time: (tile ^ d_tile, time ^ d_time))

    def set_out(d_time):
        arrived[far, d_time] = send(blocks[far * times + d_time], lambda tile, time: ((tile - 1) % tiles, time))

    def go_on(d_time):
        arrived[far, d_time] = send(arrived[far, d_time], lambda tile, time: ((tile - 1) % tiles, time ^ d_time))

    relayed = list(range(times // 2, times)) if tiles == 4 else []
    arrived = {(0, 0): blocks[0]}
    for d_time in reversed(range(times)):
        if d_time in relayed:
            set_out(d_time)
            direct(0, d_time)
        else:
            direct(far, d_time)
    near = [d_tile for d_tile in range(1, tiles) if d_tile != far]
    for d_time in reversed(range(times)):
        for d_tile in near:
            direct(d_tile, d_time)
        if d_time in relayed:
            go_on(d_time)
    for d_time in range(1, times):
        if d_time not in relayed:
            direct(0, d_time)
    return [arrived[d // times, d % times] for d in range(len(blocks))]


def on_device(frames, inverse_taps, mode_rate, frame_factor):
    span, rows, side = frames.shape
    blocks, tiles = lax.axis_size("tm"), lax.axis_size("tile")
    owners = blocks * tiles
    own_modes = side // owners
    batch = min(16, own_modes)
    by_pairs = owners <= MOST_MESSAGES and owners & (owners - 1) == 0
    messages = owners if by_pairs else 1
    own_block, own_tile = lax.axis_index("tm"), lax.axis_index("tile")
    flip = jnp.stack([own_tile, own_block, own_tile * blocks + own_block]).astype(jnp.int32)
    if not by_pairs:
        flip = jnp.zeros_like(flip)

    basis = jnp.asarray(cosine_matrix(side))
    taps_b = inverse_taps.astype(BF16).astype(F32)
    filter_matrix = filter_over(taps_b, blocks, span, batch, flip[1])
    if by_pairs:
        around = [send(frame_factor, lambda tile, time: (tile, time ^ d)) for d in range(1, blocks)]
        factors = jnp.concatenate([frame_factor] + around)
    else:
        factors = lax.all_gather(frame_factor, "tm", tiled=True)
    rate = lax.dynamic_slice_in_dim(mode_rate, own_block * own_modes, own_modes, 1).T

    received = exchange(forward_columns(flip, frames, basis, owners, messages))
    returned = exchange(in_modes(flip, received, factors, filter_matrix, rate, basis, tiles, batch))
    return back_columns(flip, returned, basis)


def solution(mesh):
    return jax.shard_map(
        on_device,
        mesh=mesh,
        in_specs=(P(("grp", "tm"), "tile", None), P(), P(None, "tile"), P(("grp", "tm"))),
        out_specs=P(("grp", "tm"), "tile", None),
        check_vma=False,
    )
```

```python
import functools

import jax
import jax.numpy as jnp
import numpy as np
from jax import lax
from jax.experimental import pallas as pl
from jax.experimental.pallas import tpu as pltpu
from jax.sharding import PartitionSpec as P

F32 = jnp.float32
BF16 = jnp.bfloat16
PARAMS = pltpu.CompilerParams(vmem_limit_bytes=60 * 1024 * 1024)
SMEM = pl.BlockSpec(memory_space=pltpu.SMEM)


def cosine_matrix(points):
    freq_idx = np.arange(points)[:, None]
    cell_idx = np.arange(points)[None, :]
    phase = (2 * cell_idx + 1) * freq_idx % (4 * points)
    values = np.cos(np.pi * phase / (2.0 * points)) * np.sqrt(2.0 / points)
    values = np.where(freq_idx == 0, values / np.sqrt(2.0), values)
    return values.astype(np.float32).astype(BF16)


def dot(a, b, a_dim, b_dim):
    return lax.dot_general(a, b, (((a_dim,), (b_dim,)), ((), ())), preferred_element_type=F32)


def cost(flops, bytes_accessed):
    return pl.CostEstimate(flops=flops, bytes_accessed=bytes_accessed, transcendentals=0)


def whole(array):
    return pl.BlockSpec(array.shape, lambda step: (0,) * array.ndim)


def columns_kernel(joined, own_ref, frames_ref, basis_ref, *refs):
    out_refs, ordered_ref = refs[:-1], refs[-1]
    tiles, blocks, modes, side = basis_ref.shape

    @pl.when(pl.program_id(0) == 0)
    def _():
        for tile in range(tiles):
            for d in range(blocks):
                at = (tile * blocks + d if joined else d * tiles + tile) * modes
                ordered_ref[at:at + modes] = basis_ref[tile, d ^ own_ref[0]]

    out = dot(ordered_ref[...], frames_ref[0], 1, 1).astype(BF16)
    size = out.shape[0] // len(out_refs)
    for i, out_ref in enumerate(out_refs):
        out_ref[...] = out[i * size:(i + 1) * size].reshape(out_ref.shape)


def forward_columns(own, frames, basis, joined):
    span, rows, side = frames.shape
    tiles, blocks, modes, _ = basis.shape
    count, each = (1, blocks) if joined else (blocks, 1)
    total = tiles * blocks * modes
    return pl.pallas_call(
        functools.partial(columns_kernel, joined),
        grid=(span,),
        in_specs=[SMEM, pl.BlockSpec((1, rows, side), lambda f: (f, 0, 0)), whole(basis)],
        out_specs=[pl.BlockSpec((tiles, each, 1, modes, rows), lambda f: (0, 0, f, 0, 0))] * count,
        out_shape=[jax.ShapeDtypeStruct((tiles, each, span, modes, rows), BF16)] * count,
        scratch_shapes=[pltpu.VMEM((total, side), BF16)],
        compiler_params=PARAMS,
        cost_estimate=cost(2 * span * rows * side * total, 2 * span * rows * (side + total) + 2 * side * total),
        name="columns",
    )(own, frames, basis)


def gathered(refs, tile=None):
    pick = slice(None) if tile is None else tile
    parts = [ref[pick] for ref in refs]
    return parts[0] if len(parts) == 1 else jnp.concatenate(parts, axis=parts[0].ndim - 4)


def modes_kernel(in_count, own_ref, factor_ref, *refs):
    in_refs, (filter_ref, rate_ref, basis_ref) = refs[:in_count], refs[in_count:in_count + 3]
    out_refs, (spectra_ref, running_ref) = refs[in_count + 3:-2], refs[-2:]
    tiles, _, span, batch, rows = in_refs[0].shape
    frames = spectra_ref.shape[0] // batch
    blocks = frames // span
    filtered = []
    for tile in range(tiles):
        piece = gathered(in_refs, tile).reshape(frames * batch, rows)
        filtered.append(dot(filter_ref[...], piece, 1, 0).astype(BF16))
    column_pass = jnp.concatenate(filtered, axis=1)
    spectra_ref[...] = dot(column_pass, basis_ref[...], 1, 1)
    retain = jnp.exp(-rate_ref[...])
    state = jnp.zeros_like(retain)
    for block in range(blocks):
        place = block ^ own_ref[0]
        states = []
        for step in range(span):
            at = (block * span + step) * batch
            state = retain * factor_ref[place * span + step] * state + spectra_ref[at:at + batch]
            if batch % 16 == 0:
                start = pl.multiple_of((place * span + step) * batch, batch)
                running_ref[pl.ds(start, batch)] = state.astype(BF16)
            else:
                states.append(state)
        if states:
            start = pl.multiple_of(place * span * batch, span * batch)
            running_ref[pl.ds(start, span * batch)] = jnp.concatenate(states, axis=0).astype(BF16)
    row_pass = dot(running_ref[...], basis_ref[...], 1, 0).astype(BF16)
    for tile in range(tiles):
        piece = row_pass[:, tile * rows:(tile + 1) * rows].reshape(blocks, span, batch, rows)
        for i, out_ref in enumerate(out_refs):
            each = blocks // len(out_refs)
            out_ref[tile] = piece[i * each:(i + 1) * each]


def in_modes(own, received, factors, filter_matrix, rate, basis, batch, joined):
    side = basis.shape[0]
    tiles, _, span, modes, rows = received[0][0].shape
    frames = factors.shape[0]
    blocks = frames // span
    out_count, each = (1, blocks) if joined else (blocks, 1)

    def block(count):
        return pl.BlockSpec((tiles, count, span, batch, rows), lambda k: (0, 0, 0, k, 0))

    return pl.pallas_call(
        functools.partial(modes_kernel, len(received)),
        grid=(modes // batch,),
        in_specs=[SMEM, SMEM]
        + [block(count) for _, count in received]
        + [whole(filter_matrix), pl.BlockSpec((batch, side), lambda k: (k, 0)), whole(basis)],
        out_specs=[block(each)] * out_count,
        out_shape=[jax.ShapeDtypeStruct((tiles, each, span, modes, rows), BF16)] * out_count,
        scratch_shapes=[pltpu.VMEM((frames * batch, side), F32), pltpu.VMEM((frames * batch, side), BF16)],
        compiler_params=PARAMS,
        cost_estimate=cost(5 * frames * modes * side * side, 4 * frames * modes * side + 2 * side * side),
        name="in_modes",
    )(own, factors, *[array for array, _ in received], filter_matrix, rate, basis)


def back_kernel(counts, own_ref, *refs):
    in_refs, basis_refs = refs[:sum(counts)], refs[sum(counts):sum(counts) + len(counts)]
    out_ref, ordered_refs = refs[sum(counts) + len(counts)], refs[sum(counts) + len(counts) + 1:]

    @pl.when(pl.program_id(0) == 0)
    def _():
        for basis_ref, ordered_ref in zip(basis_refs, ordered_refs):
            tiles, blocks, modes, _ = basis_ref.shape
            for tile in range(tiles):
                for d in range(blocks):
                    at = (tile * blocks + d) * modes
                    ordered_ref[at:at + modes] = basis_ref[tile, d ^ own_ref[0]]

    total = 0.0
    for count, ordered_ref in zip(counts, ordered_refs):
        row_pass = gathered(in_refs[:count]).reshape(ordered_ref.shape[0], in_refs[0].shape[-1])
        in_refs = in_refs[count:]
        total = total + dot(row_pass, ordered_ref[...], 0, 0)
    out_ref[0] = total.astype(BF16)


def back_columns(own, streams, bases):
    tiles, _, span, modes, rows = streams[0][0][0].shape
    side = bases[0].shape[-1]
    pieces = [piece for stream in streams for piece in stream]
    return pl.pallas_call(
        functools.partial(back_kernel, [len(stream) for stream in streams]),
        grid=(span,),
        in_specs=[SMEM]
        + [pl.BlockSpec((tiles, count, 1, modes, rows), lambda f: (0, 0, f, 0, 0)) for _, count in pieces]
        + [whole(basis) for basis in bases],
        out_specs=pl.BlockSpec((1, rows, side), lambda f: (f, 0, 0)),
        out_shape=jax.ShapeDtypeStruct((span, rows, side), BF16),
        scratch_shapes=[pltpu.VMEM((basis.size // side, side), BF16) for basis in bases],
        compiler_params=PARAMS,
        cost_estimate=cost(2 * span * rows * side * side, 4 * span * rows * side + 2 * side * side),
        name="back_columns",
    )(own, *[array for array, _ in pieces], *bases)


def filter_over(taps_b, blocks, span, batch, own):
    tap_count = taps_b.shape[0]
    frames = blocks * span
    place = np.arange(frames)
    source = (place // span ^ own) * span + place % span
    lag = np.arange(frames)[:, None] - source[None, :]
    onehot = lag[:, :, None] == np.arange(tap_count)
    toeplitz = jnp.sum(jnp.where(onehot, taps_b[None, None, :], 0.0), axis=2).astype(BF16)
    index = np.arange(frames * batch)
    spread = (index[:, None] // batch == np.arange(frames)[None, :]).astype(BF16)
    over_rows = dot(spread, toeplitz, 1, 0).astype(BF16)
    over_both = dot(over_rows, spread, 1, 1).astype(BF16)
    same_mode = index[:, None] % batch == index[None, :] % batch
    return jnp.where(same_mode, over_both, jnp.zeros((), BF16))


def over_time(array, d):
    return lax.ppermute(array, "tm", [(i, i ^ d) for i in range(lax.axis_size("tm"))])


def over_tiles(array):
    return lax.all_to_all(array, "tile", split_axis=0, concat_axis=0, tiled=True)


def parted_over_time(arrays):
    return [array if d == 0 else over_time(array, d) for d, array in enumerate(arrays)]


def joined_over_time(array):
    parts = [over_time(array[:, d:d + 1], d) for d in range(1, array.shape[1])]
    return [(array, 1)] + [(part, 1) for part in parts]


def on_device(frames, inverse_taps, mode_rate, frame_factor):
    span, rows, side = frames.shape
    blocks, tiles = lax.axis_size("tm"), lax.axis_size("tile")
    own_modes = side // (blocks * tiles)
    batch = min(16, own_modes)
    streams = 2 if own_modes // batch % 2 == 0 else 1
    modes = own_modes // streams
    own_block = lax.axis_index("tm")
    own = own_block.astype(jnp.int32).reshape(1)

    matrix = cosine_matrix(side)
    by_stream = np.moveaxis(matrix.reshape(tiles, blocks, streams, modes, side), 2, 0)
    bases = [jnp.asarray(by_stream[i]) for i in range(streams)]
    basis = jnp.asarray(matrix)
    taps_b = inverse_taps.astype(BF16).astype(F32)
    filter_matrix = filter_over(taps_b, blocks, span, batch, own_block)
    factors = jnp.concatenate(parted_over_time([frame_factor] * blocks))
    rate = lax.dynamic_slice_in_dim(mode_rate, own_block * own_modes, own_modes, 1).T
    rates = [rate[i * modes:(i + 1) * modes] for i in range(streams)]

    def middle(i, received, joined):
        return in_modes(own, received, factors, filter_matrix, rates[i], basis, batch, joined)

    crossed = over_tiles(forward_columns(own, frames, bases[0], True)[0])
    if streams == 2:
        turned = parted_over_time(forward_columns(own, frames, bases[1], False))
        arrived = over_tiles(jnp.concatenate(turned, axis=1))
    inverted = parted_over_time(middle(0, joined_over_time(crossed), False))
    result = []
    if streams == 2:
        returned = over_tiles(middle(1, [(arrived, blocks)], True)[0])
        result = [joined_over_time(returned)]
    result = [[(over_tiles(jnp.concatenate(inverted, axis=1)), blocks)]] + result
    return back_columns(own, result, bases)


def solution(mesh):
    return jax.shard_map(
        on_device,
        mesh=mesh,
        in_specs=(P(("grp", "tm"), "tile", None), P(), P(None, "tile"), P(("grp", "tm"))),
        out_specs=P(("grp", "tm"), "tile", None),
        check_vma=False,
    )
```

```python
import functools

import jax
import jax.numpy as jnp
import numpy as np
from jax import lax
from jax.experimental import pallas as pl
from jax.experimental.pallas import tpu as pltpu
from jax.sharding import PartitionSpec as P

F32 = jnp.float32
BF16 = jnp.bfloat16
VMEM_LIMIT = 48 * 1024 * 1024


def cosine_matrix(points):
    freq_idx = np.arange(points)[:, None]
    cell_idx = np.arange(points)[None, :]
    phase = (2 * cell_idx + 1) * freq_idx % (4 * points)
    values = np.cos(np.pi * phase / (2.0 * points)) * np.sqrt(2.0 / points)
    values = np.where(freq_idx == 0, values / np.sqrt(2.0), values)
    return values.astype(np.float32).astype(BF16)


def dot(a, b, a_dim, b_dim):
    return lax.dot_general(a, b, (((a_dim,), (b_dim,)), ((), ())), preferred_element_type=F32)


def cost(flops, bytes_accessed):
    return pl.CostEstimate(flops=flops, bytes_accessed=bytes_accessed, transcendentals=0)


PARAMS = pltpu.CompilerParams(vmem_limit_bytes=VMEM_LIMIT)


def columns_kernel(frames_ref, basis_ref, out_ref):
    modes = dot(basis_ref[...], frames_ref[0], 1, 1)
    out_ref[...] = modes.astype(BF16).reshape(out_ref.shape)


def forward_columns(frames, basis, owners):
    span, rows, side = frames.shape
    count = basis.shape[0]
    own_modes = count // owners
    return pl.pallas_call(
        columns_kernel,
        grid=(span,),
        in_specs=[
            pl.BlockSpec((1, rows, side), lambda f: (f, 0, 0)),
            pl.BlockSpec((count, side), lambda f: (0, 0)),
        ],
        out_specs=pl.BlockSpec((owners, 1, own_modes, rows), lambda f: (0, f, 0, 0)),
        out_shape=jax.ShapeDtypeStruct((owners, span, own_modes, rows), BF16),
        compiler_params=PARAMS,
        cost_estimate=cost(2 * span * rows * side * count, 2 * span * rows * (side + count) + 2 * side * count),
        name="columns",
    )(frames, basis)


def modes_kernel(tiles, out_count, factor_ref, in_ref, filter_ref, rate_ref, basis_ref, *refs):
    out_refs, (spectra_ref, running_ref) = refs[:out_count], refs[out_count:]
    owners, span, batch, rows = in_ref.shape
    blocks = owners // tiles
    frames = blocks * span
    filtered = []
    for tile in range(tiles):
        piece = in_ref[tile * blocks:(tile + 1) * blocks].reshape(frames * batch, rows)
        filtered.append(dot(filter_ref[...], piece, 1, 0).astype(BF16))
    column_pass = jnp.concatenate(filtered, axis=1)
    spectra_ref[...] = dot(column_pass, basis_ref[...], 1, 1)
    retain = jnp.exp(-rate_ref[...])
    state = jnp.zeros_like(retain)
    for frame in range(frames):
        at = slice(frame * batch, (frame + 1) * batch)
        state = retain * factor_ref[frame] * state + spectra_ref[at]
        running_ref[at] = state.astype(BF16)
    row_pass = dot(running_ref[...], basis_ref[...], 1, 0).astype(BF16)
    part = span // out_count
    for tile in range(tiles):
        piece = row_pass[:, tile * rows:(tile + 1) * rows].reshape(blocks, span, batch, rows)
        for i, out_ref in enumerate(out_refs):
            out_ref[tile * blocks:(tile + 1) * blocks] = piece[:, i * part:(i + 1) * part]


def in_modes(received, factors, filter_matrix, rate, basis, tiles, batch, out_count):
    owners, span, own_modes, rows = received.shape
    side = basis.shape[0]
    frames = owners // tiles * span
    part = span // out_count
    return pl.pallas_call(
        functools.partial(modes_kernel, tiles, out_count),
        grid=(own_modes // batch,),
        in_specs=[
            pl.BlockSpec(memory_space=pltpu.SMEM),
            pl.BlockSpec((owners, span, batch, rows), lambda k: (0, 0, k, 0)),
            pl.BlockSpec(filter_matrix.shape, lambda k: (0, 0)),
            pl.BlockSpec((batch, side), lambda k: (k, 0)),
            pl.BlockSpec((side, side), lambda k: (0, 0)),
        ],
        out_specs=[pl.BlockSpec((owners, part, batch, rows), lambda k: (0, 0, k, 0))] * out_count,
        out_shape=[jax.ShapeDtypeStruct((owners, part, own_modes, rows), BF16)] * out_count,
        scratch_shapes=[
            pltpu.VMEM((frames * batch, side), F32),
            pltpu.VMEM((frames * batch, side), BF16),
        ],
        compiler_params=PARAMS,
        cost_estimate=cost(5 * frames * own_modes * side * side, 4 * frames * own_modes * side + 2 * side * side),
        name="in_modes",
    )(factors, received, filter_matrix, rate, basis)


def back_kernel(count, *refs):
    in_refs, basis_refs, out_ref = refs[:count], refs[count:2 * count], refs[-1]
    total = 0.0
    for in_ref, basis_ref in zip(in_refs, basis_refs):
        row_pass = in_ref[...].reshape(basis_ref.shape[0], in_ref.shape[-1])
        total = total + dot(row_pass, basis_ref[...], 0, 0)
    out_ref[0] = total.astype(BF16)


def back_columns(pieces, bases, first, frames, span, earlier):
    side = bases[0].shape[1]
    rows = pieces[0][0].shape[-1]
    count = len(pieces)
    in_specs = []
    for array, start in pieces:
        owners, _, own_modes, _ = array.shape
        in_specs.append(pl.BlockSpec((owners, 1, own_modes, rows), lambda f, start=start: (0, f + start, 0, 0)))
    in_specs += [pl.BlockSpec(basis.shape, lambda f: (0, 0)) for basis in bases]
    operands = [array for array, _ in pieces] + list(bases)
    aliases = {}
    body = functools.partial(back_kernel, count)
    if earlier is not None:
        in_specs.append(pl.BlockSpec(memory_space=pl.ANY))
        aliases = {len(operands): 0}
        operands.append(earlier)
    return pl.pallas_call(
        body,
        grid=(frames,),
        in_specs=in_specs,
        out_specs=pl.BlockSpec((1, rows, side), lambda f: (f + first, 0, 0)),
        out_shape=jax.ShapeDtypeStruct((span, rows, side), BF16),
        input_output_aliases=aliases,
        compiler_params=PARAMS,
        cost_estimate=cost(2 * frames * rows * side * side, 4 * frames * rows * side + 2 * side * side),
        name="back_columns",
    )(*operands)


def filter_over(taps_b, frames, batch):
    tap_count = taps_b.shape[0]
    lag = np.arange(frames)[:, None] - np.arange(frames)[None, :]
    onehot = lag[:, :, None] == np.arange(tap_count)
    toeplitz = jnp.sum(jnp.where(onehot, taps_b[None, None, :], 0.0), axis=2).astype(BF16)
    index = np.arange(frames * batch)
    spread = (index[:, None] // batch == np.arange(frames)[None, :]).astype(BF16)
    over_rows = dot(spread, toeplitz, 1, 0).astype(BF16)
    over_both = dot(over_rows, spread, 1, 1).astype(BF16)
    same_mode = index[:, None] % batch == index[None, :] % batch
    return jnp.where(same_mode, over_both, jnp.zeros((), BF16))


def on_device(frames, inverse_taps, mode_rate, frame_factor):
    span, rows, side = frames.shape
    blocks, tiles = lax.axis_size("tm"), lax.axis_size("tile")
    owners = blocks * tiles
    own_modes = side // owners
    batch = min(16, own_modes)
    chunks = 2 if own_modes // batch % 2 == 0 else 1
    chunk_modes = own_modes // chunks

    matrix = cosine_matrix(side)
    by_chunk = matrix.reshape(owners, chunks, chunk_modes, side).swapaxes(0, 1)
    bases = [jnp.asarray(by_chunk[c].reshape(owners * chunk_modes, side)) for c in range(chunks)]
    basis = jnp.asarray(matrix)

    taps_b = inverse_taps.astype(BF16).astype(F32)
    filter_matrix = filter_over(taps_b, blocks * span, batch)
    factors = lax.all_gather(frame_factor, "tm", tiled=True)
    rate = lax.dynamic_slice_in_dim(mode_rate, lax.axis_index("tm") * own_modes, own_modes, 1).T

    def exchange(block):
        flat = block.reshape(-1, rows)
        flat = lax.all_to_all(flat, ("tile", "tm"), split_axis=0, concat_axis=0, tiled=True)
        return flat.reshape(block.shape)

    received = [exchange(forward_columns(frames, bases[c], owners)) for c in range(chunks)]
    halves = 2 if span % 2 == 0 else 1
    returned = []
    for c in range(chunks):
        out_count = halves if c == chunks - 1 else 1
        own_rate = rate[c * chunk_modes:(c + 1) * chunk_modes]
        outs = in_modes(received[c], factors, filter_matrix, own_rate, basis, tiles, batch, out_count)
        returned.append([exchange(out) for out in outs])
    part = span // halves
    result = None
    for half in range(halves):
        pieces = [(arrays[0], half * part) for arrays in returned[:-1]] + [(returned[-1][half], 0)]
        result = back_columns(pieces, bases, half * part, part, span, result)
    return result


def solution(mesh):
    return jax.shard_map(
        on_device,
        mesh=mesh,
        in_specs=(P(("grp", "tm"), "tile", None), P(), P(None, "tile"), P(("grp", "tm"))),
        out_specs=P(("grp", "tm"), "tile", None),
        check_vma=False,
    )
```

```python
import functools
import math

import jax
import jax.numpy as jnp
import numpy as np
from jax import lax
from jax.experimental import pallas as pl
from jax.experimental.pallas import tpu as pltpu
from jax.sharding import PartitionSpec as P

F32 = jnp.float32
BF16 = jnp.bfloat16
PARAMS = pltpu.CompilerParams(vmem_limit_bytes=60 * 1024 * 1024)
SMEM = pl.BlockSpec(memory_space=pltpu.SMEM)


def tile_layout(tiles, blocks):
    times = range(blocks)
    if tiles == 4 and blocks % 2 == 0:
        near, far = times[:blocks // 2], times[blocks // 2:]
        return [
            [(0, d) for d in times],
            [(1, d) for d in times] + [(2, d) for d in near],
            [(3, d) for d in times] + [(2, d) for d in far],
        ]
    return [[(e, d) for d in times] for e in range(tiles)]


def time_layout(tiles, blocks):
    return [[(e, d) for e in range(tiles)] for d in range(blocks)]


def send_tile(array, e):
    tiles = lax.axis_size("tile")
    return lax.ppermute(array, "tile", [(i, (i + e) % tiles) for i in range(tiles)])


def over_tiles(arrays, layout):
    if len(layout) == lax.axis_size("tile"):
        return [(send_tile(a, e) if e else a, labels) for e, (a, labels) in enumerate(zip(arrays, layout))]
    blocks = len(layout[0])
    forth, back = send_tile(arrays[1], 1), send_tile(arrays[2], -1)
    forth_on, back_on = send_tile(forth[blocks:], 1), send_tile(back[blocks:], -1)
    return [
        (arrays[0], layout[0]),
        (forth, layout[1][:blocks]),
        (back, layout[2][:blocks]),
        (forth_on, layout[1][blocks:]),
        (back_on, layout[2][blocks:]),
    ]


def over_time(arrays, layout):
    sent = [
        lax.ppermute(a, "tm", [(i, i ^ d) for i in range(lax.axis_size("tm"))]) if d else a
        for d, a in enumerate(arrays)
    ]
    return list(zip(sent, layout))


def runs(pieces, wanted):
    where = {label: (i, j) for i, (_, labels) in enumerate(pieces) for j, label in enumerate(labels)}
    found = []
    for label in wanted:
        i, j = where[label]
        if found and found[-1][0] == i and sum(found[-1][1:]) == j:
            found[-1] = (i, found[-1][1], found[-1][2] + 1)
        else:
            found.append((i, j, 1))
    return found


def arrange_kernel(moves, count, *refs):
    sems = refs[-1]
    copies = []
    for n, (source, first, target, at, length) in enumerate(moves):
        from_ref, to_ref = refs[source].at[first:first + length], refs[count + target].at[at:at + length]
        copies.append(pltpu.make_async_copy(from_ref, to_ref, sems.at[n]))
    for copy in copies:
        copy.start()
    for copy in copies:
        copy.wait()


def arranged(pieces, layout):
    moves = []
    for target, labels in enumerate(layout):
        at = 0
        for source, first, length in runs(pieces, labels):
            moves.append((source, first, target, at, length))
            at += length
    block = pieces[0][0].shape[1:]
    total = sum(len(labels) for labels in layout)
    return pl.pallas_call(
        functools.partial(arrange_kernel, moves, len(pieces)),
        in_specs=[pl.BlockSpec(memory_space=pl.ANY)] * len(pieces),
        out_specs=[pl.BlockSpec(memory_space=pl.ANY)] * len(layout),
        out_shape=[jax.ShapeDtypeStruct((len(labels), *block), BF16) for labels in layout],
        scratch_shapes=[pltpu.SemaphoreType.DMA((len(moves),))],
        compiler_params=PARAMS,
        cost_estimate=cost(0, 4 * total * math.prod(block)),
        name="arrange",
    )(*[array for array, _ in pieces])


def cosine_matrix(points):
    freq_idx = np.arange(points)[:, None]
    cell_idx = np.arange(points)[None, :]
    phase = (2 * cell_idx + 1) * freq_idx % (4 * points)
    values = np.cos(np.pi * phase / (2.0 * points)) * np.sqrt(2.0 / points)
    values = np.where(freq_idx == 0, values / np.sqrt(2.0), values)
    return values.astype(np.float32).astype(BF16)


def dot(a, b, a_dim, b_dim):
    return lax.dot_general(a, b, (((a_dim,), (b_dim,)), ((), ())), preferred_element_type=F32)


def cost(flops, bytes_accessed):
    return pl.CostEstimate(flops=flops, bytes_accessed=bytes_accessed, transcendentals=0)


def whole(array):
    return pl.BlockSpec(array.shape, lambda step: (0,) * array.ndim)


def order_rows(own_ref, basis_ref, ordered_ref, labels, sign):
    tiles, _, modes, _ = basis_ref.shape
    for i, (e, d) in enumerate(labels):
        tile = lax.rem(own_ref[0] + sign * e + tiles, tiles)
        ordered_ref[i * modes:(i + 1) * modes] = basis_ref[tile, own_ref[1] ^ d]


def gathered(refs, pieces, wanted):
    parts = [refs[i][j:j + count] for i, j, count in runs(pieces, wanted)]
    return parts[0] if len(parts) == 1 else jnp.concatenate(parts, axis=0)


def columns_kernel(layout, own_ref, frames_ref, basis_ref, *refs):
    out_refs, ordered_ref = refs[-len(layout) - 1:-1], refs[-1]

    @pl.when(pl.program_id(0) == 0)
    def _():
        order_rows(own_ref, basis_ref, ordered_ref, sum(layout, []), 1)

    out = dot(ordered_ref[...], frames_ref[0], 1, 1).astype(BF16)
    for out_ref in out_refs:
        size = out_ref.shape[0] * out_ref.shape[2]
        out_ref[...] = out[:size].reshape(out_ref.shape)
        out = out[size:]


def forward_columns(own, frames, basis, layout, after):
    span, rows, side = frames.shape
    tiles, blocks, modes, _ = basis.shape
    total = tiles * blocks * modes
    return pl.pallas_call(
        functools.partial(columns_kernel, layout),
        grid=(span,),
        in_specs=[SMEM, pl.BlockSpec((1, rows, side), lambda f: (f, 0, 0)), whole(basis)]
        + [pl.BlockSpec(memory_space=pl.ANY)] * len(after),
        out_specs=[pl.BlockSpec((len(labels), 1, modes, rows), lambda f: (0, f, 0, 0)) for labels in layout],
        out_shape=[jax.ShapeDtypeStruct((len(labels), span, modes, rows), BF16) for labels in layout],
        scratch_shapes=[pltpu.VMEM((total, side), BF16)],
        compiler_params=PARAMS,
        cost_estimate=cost(2 * span * rows * side * total, 2 * span * rows * (side + total) + 2 * side * total),
        name="columns",
    )(own, frames, basis, *after)


def modes_kernel(labels, layout, own_ref, factor_ref, *refs):
    count = len(labels)
    in_refs, (filter_ref, rate_ref, basis_ref) = refs[:count], refs[count:count + 3]
    out_refs, (ordered_ref, spectra_ref, running_ref) = refs[count + 3:-3], refs[-3:]
    _, span, batch, rows = in_refs[0].shape
    frames = spectra_ref.shape[0] // batch
    blocks = frames // span
    tiles = basis_ref.shape[1] // rows

    @pl.when(pl.program_id(0) == 0)
    def _():
        for e in range(tiles):
            start = lax.rem(own_ref[0] - e + tiles, tiles) * rows
            ordered_ref[:, e * rows:(e + 1) * rows] = basis_ref[:, pl.ds(pl.multiple_of(start, rows), rows)]

    pieces = [(None, some) for some in labels]
    filtered = []
    for e in range(tiles):
        piece = gathered(in_refs, pieces, [(e, d) for d in range(blocks)]).reshape(frames * batch, rows)
        filtered.append(dot(filter_ref[...], piece, 1, 0).astype(BF16))
    column_pass = jnp.concatenate(filtered, axis=1)
    spectra_ref[...] = dot(column_pass, ordered_ref[...], 1, 1)
    retain = jnp.exp(-rate_ref[...])
    state = jnp.zeros_like(retain)
    for block in range(blocks):
        place = block ^ own_ref[1]
        states = []
        for step in range(span):
            at = (block * span + step) * batch
            state = retain * factor_ref[place * span + step] * state + spectra_ref[at:at + batch]
            if batch % 16 == 0:
                start = pl.multiple_of((place * span + step) * batch, batch)
                running_ref[pl.ds(start, batch)] = state.astype(BF16)
            else:
                states.append(state)
        if states:
            start = pl.multiple_of(place * span * batch, span * batch)
            running_ref[pl.ds(start, span * batch)] = jnp.concatenate(states, axis=0).astype(BF16)
    row_pass = dot(running_ref[...], ordered_ref[...], 1, 0).astype(BF16)
    for e in range(tiles):
        piece = row_pass[:, e * rows:(e + 1) * rows].reshape(blocks, span, batch, rows)
        for i, j, length, d in [
            (i, labels_out.index(((tiles - e) % tiles, d)), 1, d)
            for i, labels_out in enumerate(layout)
            for d in range(blocks)
            if ((tiles - e) % tiles, d) in labels_out
        ]:
            out_refs[i][j:j + length] = piece[d:d + length]


def in_modes(own, pieces, factors, filter_matrix, rate, basis, batch, layout):
    side = basis.shape[0]
    _, span, modes, rows = pieces[0][0].shape
    frames = factors.shape[0]

    def block(count):
        return pl.BlockSpec((count, span, batch, rows), lambda k: (0, 0, k, 0))

    return pl.pallas_call(
        functools.partial(modes_kernel, [labels for _, labels in pieces], layout),
        grid=(modes // batch,),
        in_specs=[SMEM, SMEM]
        + [block(len(labels)) for _, labels in pieces]
        + [whole(filter_matrix), pl.BlockSpec((batch, side), lambda k: (k, 0)), whole(basis)],
        out_specs=[block(len(labels)) for labels in layout],
        out_shape=[jax.ShapeDtypeStruct((len(labels), span, modes, rows), BF16) for labels in layout],
        scratch_shapes=[
            pltpu.VMEM((side, side), BF16),
            pltpu.VMEM((frames * batch, side), F32),
            pltpu.VMEM((frames * batch, side), BF16),
        ],
        compiler_params=PARAMS,
        cost_estimate=cost(5 * frames * modes * side * side, 4 * frames * modes * side + 2 * side * side),
        name="in_modes",
    )(own, factors, *[array for array, _ in pieces], filter_matrix, rate, basis)


def back_kernel(labels, own_ref, *refs):
    streams, arrays = len(labels), sum(len(stream) for stream in labels)
    in_refs, basis_refs = refs[:arrays], refs[arrays:arrays + streams]
    out_ref, ordered_refs = refs[arrays + streams], refs[arrays + streams + 1:]

    @pl.when(pl.program_id(0) == 0)
    def _():
        for stream, basis_ref, ordered_ref in zip(labels, basis_refs, ordered_refs):
            order_rows(own_ref, basis_ref, ordered_ref, sum(stream, []), -1)

    total = 0.0
    for stream, ordered_ref in zip(labels, ordered_refs):
        parts = [ref[...] for ref in in_refs[:len(stream)]]
        in_refs = in_refs[len(stream):]
        row_pass = jnp.concatenate(parts, axis=0).reshape(ordered_ref.shape[0], parts[0].shape[-1])
        total = total + dot(row_pass, ordered_ref[...], 0, 0)
    out_ref[0] = total.astype(BF16)


def back_columns(own, streams, bases):
    _, span, modes, rows = streams[0][0][0].shape
    side = bases[0].shape[-1]
    pieces = sum(streams, [])
    return pl.pallas_call(
        functools.partial(back_kernel, [[labels for _, labels in stream] for stream in streams]),
        grid=(span,),
        in_specs=[SMEM]
        + [pl.BlockSpec((len(labels), 1, modes, rows), lambda f: (0, f, 0, 0)) for _, labels in pieces]
        + [whole(basis) for basis in bases],
        out_specs=pl.BlockSpec((1, rows, side), lambda f: (f, 0, 0)),
        out_shape=jax.ShapeDtypeStruct((span, rows, side), BF16),
        scratch_shapes=[pltpu.VMEM((basis.size // side, side), BF16) for basis in bases],
        compiler_params=PARAMS,
        cost_estimate=cost(2 * span * rows * side * side, 4 * span * rows * side + 2 * side * side),
        name="back_columns",
    )(own, *[array for array, _ in pieces], *bases)


def filter_over(taps_b, blocks, span, batch, own):
    tap_count = taps_b.shape[0]
    frames = blocks * span
    place = np.arange(frames)
    source = (place // span ^ own) * span + place % span
    lag = np.arange(frames)[:, None] - source[None, :]
    onehot = lag[:, :, None] == np.arange(tap_count)
    toeplitz = jnp.sum(jnp.where(onehot, taps_b[None, None, :], 0.0), axis=2).astype(BF16)
    index = np.arange(frames * batch)
    spread = (index[:, None] // batch == np.arange(frames)[None, :]).astype(BF16)
    over_rows = dot(spread, toeplitz, 1, 0).astype(BF16)
    over_both = dot(over_rows, spread, 1, 1).astype(BF16)
    same_mode = index[:, None] % batch == index[None, :] % batch
    return jnp.where(same_mode, over_both, jnp.zeros((), BF16))


def on_device(frames, inverse_taps, mode_rate, frame_factor):
    span, rows, side = frames.shape
    blocks, tiles = lax.axis_size("tm"), lax.axis_size("tile")
    own_modes = side // (blocks * tiles)
    batch = min(16, own_modes)
    streams = 2 if own_modes // batch % 2 == 0 else 1
    modes = own_modes // streams
    own_block = lax.axis_index("tm")
    own = jnp.stack([lax.axis_index("tile"), own_block]).astype(jnp.int32)

    matrix = cosine_matrix(side)
    by_stream = np.moveaxis(matrix.reshape(tiles, blocks, streams, modes, side), 2, 0)
    bases = [jnp.asarray(by_stream[i]) for i in range(streams)]
    basis = jnp.asarray(matrix)
    taps_b = inverse_taps.astype(BF16).astype(F32)
    filter_matrix = filter_over(taps_b, blocks, span, batch, own_block)
    rate = lax.dynamic_slice_in_dim(mode_rate, own_block * own_modes, own_modes, 1).T
    rates = [rate[i * modes:(i + 1) * modes] for i in range(streams)]

    by_tile, by_time = tile_layout(tiles, blocks), time_layout(tiles, blocks)
    factors = jnp.concatenate([piece for piece, _ in over_time([frame_factor] * blocks, by_time)])

    def middle(i, pieces, layout):
        return in_modes(own, pieces, factors, filter_matrix, rates[i], basis, batch, layout)

    start = forward_columns(own, frames, bases[0], by_tile, [])
    first = over_tiles(start, by_tile)
    if streams == 2:
        second = over_time(forward_columns(own, frames, bases[1], by_time, [start[0], factors]), by_time)
        second = over_tiles(arranged(second, by_tile), by_tile)
    first = over_time(arranged(first, by_time), by_time)
    first = over_time(middle(0, first, by_time), by_time)
    done = []
    if streams == 2:
        second = over_tiles(middle(1, second, by_tile), by_tile)
        done = [over_time(arranged(second, by_time), by_time)]
    first = over_tiles(arranged(first, by_tile), by_tile)
    return back_columns(own, [first] + done, bases)


def solution(mesh):
    return jax.shard_map(
        on_device,
        mesh=mesh,
        in_specs=(P(("grp", "tm"), "tile", None), P(), P(None, "tile"), P(("grp", "tm"))),
        out_specs=P(("grp", "tm"), "tile", None),
        check_vma=False,
    )
```

```python
import functools

import jax
import jax.numpy as jnp
import numpy as np
from jax import lax
from jax.experimental import pallas as pl
from jax.experimental.pallas import tpu as pltpu
from jax.sharding import PartitionSpec as P

F32 = jnp.float32
BF16 = jnp.bfloat16
PARAMS = pltpu.CompilerParams(vmem_limit_bytes=60 * 1024 * 1024)
SMEM = pl.BlockSpec(memory_space=pltpu.SMEM)


def tile_layout(tiles, blocks):
    return [[(e, d) for d in range(blocks)] for e in range(tiles)]


def time_layout(tiles, blocks):
    return [[(e, d) for e in range(tiles)] for d in range(blocks)]


def send_tile(array, e):
    tiles = lax.axis_size("tile")
    return lax.ppermute(array, "tile", [(i, (i + e) % tiles) for i in range(tiles)])


def over_tiles(arrays, layout):
    return [(send_tile(a, e) if e else a, labels) for e, (a, labels) in enumerate(zip(arrays, layout))]


def over_all(array, tiles, blocks):
    array = lax.all_to_all(array, ("tile", "tm"), split_axis=0, concat_axis=0, tiled=True)
    return [(array, [(-tile % tiles, time) for tile in range(tiles) for time in range(blocks)])]


def over_time(arrays, layout):
    sent = [
        lax.ppermute(a, "tm", [(i, i ^ d) for i in range(lax.axis_size("tm"))]) if d else a
        for d, a in enumerate(arrays)
    ]
    return list(zip(sent, layout))


def runs(pieces, wanted):
    where = {label: (i, j) for i, (_, labels) in enumerate(pieces) for j, label in enumerate(labels)}
    found = []
    for label in wanted:
        i, j = where[label]
        if found and found[-1][0] == i and sum(found[-1][1:]) == j:
            found[-1] = (i, found[-1][1], found[-1][2] + 1)
        else:
            found.append((i, j, 1))
    return found


def arrange_kernel(labels, layout, *refs):
    pieces = [(None, some) for some in labels]
    for out_ref, wanted in zip(refs[len(labels):], layout):
        at = 0
        for i, first, count in runs(pieces, wanted):
            out_ref[at:at + count] = refs[i][first:first + count]
            at += count


def arranged(pieces, layout):
    _, span, modes, rows = pieces[0][0].shape

    def block(labels):
        return pl.BlockSpec((len(labels), 1, modes, rows), lambda f: (0, f, 0, 0))

    total = sum(len(labels) for labels in layout) * span * modes * rows
    return pl.pallas_call(
        functools.partial(arrange_kernel, [labels for _, labels in pieces], layout),
        grid=(span,),
        in_specs=[block(labels) for _, labels in pieces],
        out_specs=[block(labels) for labels in layout],
        out_shape=[jax.ShapeDtypeStruct((len(labels), span, modes, rows), BF16) for labels in layout],
        compiler_params=PARAMS,
        cost_estimate=cost(0, 4 * total),
        name="arrange",
    )(*[array for array, _ in pieces])


def cosine_matrix(points):
    freq_idx = np.arange(points)[:, None]
    cell_idx = np.arange(points)[None, :]
    phase = (2 * cell_idx + 1) * freq_idx % (4 * points)
    values = np.cos(np.pi * phase / (2.0 * points)) * np.sqrt(2.0 / points)
    values = np.where(freq_idx == 0, values / np.sqrt(2.0), values)
    return values.astype(np.float32).astype(BF16)


def dot(a, b, a_dim, b_dim):
    return lax.dot_general(a, b, (((a_dim,), (b_dim,)), ((), ())), preferred_element_type=F32)


def cost(flops, bytes_accessed):
    return pl.CostEstimate(flops=flops, bytes_accessed=bytes_accessed, transcendentals=0)


def whole(array):
    return pl.BlockSpec(array.shape, lambda step: (0,) * array.ndim)


def order_rows(own_ref, basis_ref, ordered_ref, labels, sign):
    tiles, _, modes, _ = basis_ref.shape
    for i, (e, d) in enumerate(labels):
        tile = lax.rem(own_ref[0] + sign * e + tiles, tiles)
        ordered_ref[i * modes:(i + 1) * modes] = basis_ref[tile, own_ref[1] ^ d]


def gathered(refs, pieces, wanted):
    parts = [refs[i][j:j + count] for i, j, count in runs(pieces, wanted)]
    return parts[0] if len(parts) == 1 else jnp.concatenate(parts, axis=0)


def columns_kernel(layout, own_ref, frames_ref, basis_ref, *refs):
    out_refs, ordered_ref = refs[-len(layout) - 1:-1], refs[-1]

    @pl.when(pl.program_id(0) == 0)
    def _():
        order_rows(own_ref, basis_ref, ordered_ref, sum(layout, []), 1)

    out = dot(ordered_ref[...], frames_ref[0], 1, 1).astype(BF16)
    for out_ref in out_refs:
        size = out_ref.shape[0] * out_ref.shape[2]
        out_ref[...] = out[:size].reshape(out_ref.shape)
        out = out[size:]


def forward_columns(own, frames, basis, layout, after):
    span, rows, side = frames.shape
    tiles, blocks, modes, _ = basis.shape
    total = tiles * blocks * modes
    return pl.pallas_call(
        functools.partial(columns_kernel, layout),
        grid=(span,),
        in_specs=[SMEM, pl.BlockSpec((1, rows, side), lambda f: (f, 0, 0)), whole(basis)]
        + [pl.BlockSpec(memory_space=pl.ANY)] * len(after),
        out_specs=[pl.BlockSpec((len(labels), 1, modes, rows), lambda f: (0, f, 0, 0)) for labels in layout],
        out_shape=[jax.ShapeDtypeStruct((len(labels), span, modes, rows), BF16) for labels in layout],
        scratch_shapes=[pltpu.VMEM((total, side), BF16)],
        compiler_params=PARAMS,
        cost_estimate=cost(2 * span * rows * side * total, 2 * span * rows * (side + total) + 2 * side * total),
        name="columns",
    )(own, frames, basis, *after)


def modes_kernel(labels, layout, own_ref, factor_ref, *refs):
    count = len(labels)
    in_refs, (filter_ref, rate_ref, basis_ref) = refs[:count], refs[count:count + 3]
    out_refs, (ordered_ref, spectra_ref, running_ref) = refs[count + 3:-3], refs[-3:]
    _, span, batch, rows = in_refs[0].shape
    frames = spectra_ref.shape[0] // batch
    blocks = frames // span
    tiles = basis_ref.shape[1] // rows

    @pl.when(pl.program_id(0) == 0)
    def _():
        for e in range(tiles):
            start = lax.rem(own_ref[0] - e + tiles, tiles) * rows
            ordered_ref[:, e * rows:(e + 1) * rows] = basis_ref[:, pl.ds(pl.multiple_of(start, rows), rows)]

    pieces = [(None, some) for some in labels]
    filtered = []
    for e in range(tiles):
        piece = gathered(in_refs, pieces, [(e, d) for d in range(blocks)]).reshape(frames * batch, rows)
        filtered.append(dot(filter_ref[...], piece, 1, 0).astype(BF16))
    column_pass = jnp.concatenate(filtered, axis=1)
    spectra_ref[...] = dot(column_pass, ordered_ref[...], 1, 1)
    retain = jnp.exp(-rate_ref[...])
    state = jnp.zeros_like(retain)
    for block in range(blocks):
        place = block ^ own_ref[1]
        states = []
        for step in range(span):
            at = (block * span + step) * batch
            state = retain * factor_ref[block * span + step] * state + spectra_ref[at:at + batch]
            if batch % 16 == 0:
                start = pl.multiple_of((place * span + step) * batch, batch)
                running_ref[pl.ds(start, batch)] = state.astype(BF16)
            else:
                states.append(state)
        if states:
            start = pl.multiple_of(place * span * batch, span * batch)
            running_ref[pl.ds(start, span * batch)] = jnp.concatenate(states, axis=0).astype(BF16)
    row_pass = dot(running_ref[...], ordered_ref[...], 1, 0).astype(BF16)
    for e in range(tiles):
        piece = row_pass[:, e * rows:(e + 1) * rows].reshape(blocks, span, batch, rows)
        for i, j, length, d in [
            (i, labels_out.index(((tiles - e) % tiles, d)), 1, d)
            for i, labels_out in enumerate(layout)
            for d in range(blocks)
            if ((tiles - e) % tiles, d) in labels_out
        ]:
            out_refs[i][j:j + length] = piece[d:d + length]


def in_modes(own, pieces, factors, filter_matrix, rate, basis, batch, layout):
    side = basis.shape[0]
    _, span, modes, rows = pieces[0][0].shape
    frames = factors.shape[0]

    def block(count):
        return pl.BlockSpec((count, span, batch, rows), lambda k: (0, 0, k, 0))

    return pl.pallas_call(
        functools.partial(modes_kernel, [labels for _, labels in pieces], layout),
        grid=(modes // batch,),
        in_specs=[SMEM, SMEM]
        + [block(len(labels)) for _, labels in pieces]
        + [whole(filter_matrix), pl.BlockSpec((batch, side), lambda k: (k, 0)), whole(basis)],
        out_specs=[block(len(labels)) for labels in layout],
        out_shape=[jax.ShapeDtypeStruct((len(labels), span, modes, rows), BF16) for labels in layout],
        scratch_shapes=[
            pltpu.VMEM((side, side), BF16),
            pltpu.VMEM((frames * batch, side), F32),
            pltpu.VMEM((frames * batch, side), BF16),
        ],
        compiler_params=PARAMS,
        cost_estimate=cost(5 * frames * modes * side * side, 4 * frames * modes * side + 2 * side * side),
        name="in_modes",
    )(own, factors, *[array for array, _ in pieces], filter_matrix, rate, basis)


def back_kernel(labels, *refs):
    streams, arrays = len(labels), sum(len(stream) for stream in labels)
    own_refs, refs = refs[:streams], refs[streams:]
    in_refs, basis_refs = refs[:arrays], refs[arrays:arrays + streams]
    out_ref, ordered_refs = refs[arrays + streams], refs[arrays + streams + 1:]

    @pl.when(pl.program_id(0) == 0)
    def _():
        for stream, own_ref, basis_ref, ordered_ref in zip(labels, own_refs, basis_refs, ordered_refs):
            order_rows(own_ref, basis_ref, ordered_ref, sum(stream, []), -1)

    total = 0.0
    for stream, ordered_ref in zip(labels, ordered_refs):
        parts = [ref[...] for ref in in_refs[:len(stream)]]
        in_refs = in_refs[len(stream):]
        row_pass = jnp.concatenate(parts, axis=0).reshape(ordered_ref.shape[0], parts[0].shape[-1])
        total = total + dot(row_pass, ordered_ref[...], 0, 0)
    out_ref[0] = total.astype(BF16)


def back_columns(owns, shape, streams, bases):
    span, rows, side = shape
    modes = streams[0][0][0].shape[2]
    pieces = sum(streams, [])
    return pl.pallas_call(
        functools.partial(back_kernel, [[labels for _, labels in stream] for stream in streams]),
        grid=(span,),
        in_specs=[SMEM] * len(owns)
        + [pl.BlockSpec((len(labels), 1, modes, rows), lambda f: (0, f, 0, 0)) for _, labels in pieces]
        + [whole(basis) for basis in bases],
        out_specs=pl.BlockSpec((1, rows, side), lambda f: (f, 0, 0)),
        out_shape=jax.ShapeDtypeStruct(shape, BF16),
        scratch_shapes=[pltpu.VMEM((basis.size // side, side), BF16) for basis in bases],
        compiler_params=PARAMS,
        cost_estimate=cost(2 * span * rows * side * side, 4 * span * rows * side + 2 * side * side),
        name="back_columns",
    )(*owns, *[array for array, _ in pieces], *bases)


def filter_over(taps_b, blocks, span, batch, own):
    tap_count = taps_b.shape[0]
    frames = blocks * span
    place = np.arange(frames)
    source = (place // span ^ own) * span + place % span
    lag = np.arange(frames)[:, None] - source[None, :]
    onehot = lag[:, :, None] == np.arange(tap_count)
    toeplitz = jnp.sum(jnp.where(onehot, taps_b[None, None, :], 0.0), axis=2).astype(BF16)
    index = np.arange(frames * batch)
    spread = (index[:, None] // batch == np.arange(frames)[None, :]).astype(BF16)
    over_rows = dot(spread, toeplitz, 1, 0).astype(BF16)
    over_both = dot(over_rows, spread, 1, 1).astype(BF16)
    same_mode = index[:, None] % batch == index[None, :] % batch
    return jnp.where(same_mode, over_both, jnp.zeros((), BF16))


def on_device(frames, inverse_taps, mode_rate, frame_factor):
    span, rows, side = frames.shape
    blocks, tiles = lax.axis_size("tm"), lax.axis_size("tile")
    own_modes = side // (blocks * tiles)
    batch = min(16, own_modes)
    streams = 2 if own_modes // batch % 2 == 0 else 1
    modes = own_modes // streams
    own_block = lax.axis_index("tm")
    own = jnp.stack([lax.axis_index("tile"), own_block]).astype(jnp.int32)
    no_own = jnp.zeros_like(own)

    matrix = cosine_matrix(side)
    by_stream = np.moveaxis(matrix.reshape(tiles, blocks, streams, modes, side), 2, 0)
    bases = [jnp.asarray(by_stream[i]) for i in range(streams)]
    basis = jnp.asarray(matrix)
    taps_b = inverse_taps.astype(BF16).astype(F32)
    factors = lax.all_gather(frame_factor, "tm", tiled=True)
    rate = lax.dynamic_slice_in_dim(mode_rate, own_block * own_modes, own_modes, 1).T
    rates = [rate[i * modes:(i + 1) * modes] for i in range(streams)]
    by_all = [[(tile, time) for tile in range(tiles) for time in range(blocks)]]
    by_tile, by_time = tile_layout(tiles, blocks), time_layout(tiles, blocks)

    start_a = forward_columns(no_own, frames, bases[0], by_all, [])
    stream_a = over_all(start_a[0], tiles, blocks)
    filter_a = filter_over(taps_b, blocks, span, batch, 0)
    stream_a = in_modes(no_own, stream_a, factors, filter_a, rates[0], basis, batch, by_all)
    stream_a = over_all(stream_a[0], tiles, blocks)
    if streams == 1:
        return back_columns([no_own], frames.shape, [stream_a], bases)
    stream_b = over_time(forward_columns(own, frames, bases[1], by_time, start_a), by_time)
    stream_b = over_tiles(arranged(stream_b, by_tile), by_tile)
    filter_b = filter_over(taps_b, blocks, span, batch, own_block)
    stream_b = over_time(in_modes(own, stream_b, factors, filter_b, rates[1], basis, batch, by_time), by_time)
    stream_b = over_tiles(arranged(stream_b, by_tile), by_tile)
    return back_columns([no_own, own], frames.shape, [stream_a, stream_b], bases)


def solution(mesh):
    return jax.shard_map(
        on_device,
        mesh=mesh,
        in_specs=(P(("grp", "tm"), "tile", None), P(), P(None, "tile"), P(("grp", "tm"))),
        out_specs=P(("grp", "tm"), "tile", None),
        check_vma=False,
    )
```

```python
import functools

import jax
import jax.numpy as jnp
import numpy as np
from jax import lax
from jax.experimental import pallas as pl
from jax.experimental.pallas import tpu as pltpu
from jax.sharding import PartitionSpec as P

F32 = jnp.float32
BF16 = jnp.bfloat16
PARAMS = pltpu.CompilerParams(vmem_limit_bytes=60 * 1024 * 1024)


def cosine_matrix(points):
    freq_idx = np.arange(points)[:, None]
    cell_idx = np.arange(points)[None, :]
    phase = (2 * cell_idx + 1) * freq_idx % (4 * points)
    values = np.cos(np.pi * phase / (2.0 * points)) * np.sqrt(2.0 / points)
    values = np.where(freq_idx == 0, values / np.sqrt(2.0), values)
    return values.astype(np.float32).astype(BF16)


def dot(a, b, a_dim, b_dim):
    return lax.dot_general(a, b, (((a_dim,), (b_dim,)), ((), ())), preferred_element_type=F32)


def cost(flops, bytes_accessed):
    return pl.CostEstimate(flops=flops, bytes_accessed=bytes_accessed, transcendentals=0)


def whole(array):
    return pl.BlockSpec(array.shape, lambda step: (0,) * array.ndim)


def columns_kernel(frames_ref, basis_ref, out_ref):
    owners, count, own_modes, rows = out_ref.shape
    frames = frames_ref[...].reshape(count * rows, frames_ref.shape[2])
    modes = dot(basis_ref[...], frames, 1, 1).astype(BF16)
    for f in range(count):
        out_ref[:, f] = modes[:, f * rows:(f + 1) * rows].reshape(owners, own_modes, rows)


def forward_columns(frames, basis, owners, step):
    span, rows, side = frames.shape
    own_modes = side // owners
    return pl.pallas_call(
        columns_kernel,
        grid=(span // step,),
        in_specs=[pl.BlockSpec((step, rows, side), lambda f: (f, 0, 0)), whole(basis)],
        out_specs=pl.BlockSpec((owners, step, own_modes, rows), lambda f: (0, f, 0, 0)),
        out_shape=jax.ShapeDtypeStruct((owners, span, own_modes, rows), BF16),
        compiler_params=PARAMS,
        cost_estimate=cost(2 * span * rows * side * side, 4 * span * rows * side + 2 * side * side),
        name="columns",
    )(frames, basis)


def modes_kernel(tiles, factor_ref, in_ref, filter_ref, rate_ref, basis_ref, out_ref, spectra_ref, running_ref):
    owners, span, batch, rows = in_ref.shape
    blocks = owners // tiles
    frames = blocks * span
    half = frames * batch // 2
    filtered = []
    for tile in range(tiles):
        piece = in_ref[tile * blocks:(tile + 1) * blocks].reshape(frames * batch, rows)
        early = dot(filter_ref[:half, :half], piece[:half], 1, 0).astype(BF16)
        late = dot(filter_ref[half:, :], piece, 1, 0).astype(BF16)
        filtered.append(jnp.concatenate([early, late], axis=0))
    column_pass = jnp.concatenate(filtered, axis=1)
    spectra_ref[...] = dot(column_pass, basis_ref[...], 1, 1)
    retain = jnp.exp(-rate_ref[...])
    state = jnp.zeros_like(retain)
    for frame in range(frames):
        at = slice(frame * batch, (frame + 1) * batch)
        state = retain * factor_ref[frame] * state + spectra_ref[at]
        running_ref[at] = state.astype(BF16)
    row_pass = dot(running_ref[...], basis_ref[...], 1, 0).astype(BF16)
    for tile in range(tiles):
        piece = row_pass[:, tile * rows:(tile + 1) * rows]
        out_ref[tile * blocks:(tile + 1) * blocks] = piece.reshape(blocks, span, batch, rows)


def in_modes(received, factors, filter_matrix, rate, basis, tiles, batch):
    owners, span, own_modes, rows = received.shape
    side = basis.shape[0]
    frames = owners // tiles * span
    block = pl.BlockSpec((owners, span, batch, rows), lambda k: (0, 0, k, 0))
    return pl.pallas_call(
        functools.partial(modes_kernel, tiles),
        grid=(own_modes // batch,),
        in_specs=[
            pl.BlockSpec(memory_space=pltpu.SMEM),
            block,
            whole(filter_matrix),
            pl.BlockSpec((batch, side), lambda k: (k, 0)),
            whole(basis),
        ],
        out_specs=block,
        out_shape=jax.ShapeDtypeStruct(received.shape, BF16),
        scratch_shapes=[pltpu.VMEM((frames * batch, side), F32), pltpu.VMEM((frames * batch, side), BF16)],
        compiler_params=PARAMS,
        cost_estimate=cost(5 * frames * own_modes * side * side, 4 * frames * own_modes * side + 2 * side * side),
        name="in_modes",
    )(factors, received, filter_matrix, rate, basis)


def lay_out_kernel(basis_ref, after_ref, out_ref):
    out_ref[...] = basis_ref[...].reshape(out_ref.shape)


def lay_out(basis, owners, after):
    side = basis.shape[0]
    return pl.pallas_call(
        lay_out_kernel,
        grid=(2,),
        in_specs=[pl.BlockSpec((side // 2, side), lambda i: (i, 0)), pl.BlockSpec(memory_space=pl.ANY)],
        out_specs=pl.BlockSpec((owners // 2, side // owners, side), lambda i: (i, 0, 0)),
        out_shape=jax.ShapeDtypeStruct((owners, side // owners, side), BF16),
        compiler_params=PARAMS,
        cost_estimate=cost(0, 4 * side * side),
        name="lay_out",
    )(basis, after)


def back_kernel(in_ref, basis_ref, out_ref):
    owners, count, own_modes, rows = in_ref.shape
    basis = basis_ref[...].reshape(owners * own_modes, basis_ref.shape[2])
    for f in range(count):
        out_ref[f] = dot(in_ref[:, f].reshape(owners * own_modes, rows), basis, 0, 0).astype(BF16)


def back_columns(received, basis, step):
    owners, span, own_modes, rows = received.shape
    side = basis.shape[2]
    return pl.pallas_call(
        back_kernel,
        grid=(span // step,),
        in_specs=[pl.BlockSpec((owners, step, own_modes, rows), lambda f: (0, f, 0, 0)), whole(basis)],
        out_specs=pl.BlockSpec((step, rows, side), lambda f: (f, 0, 0)),
        out_shape=jax.ShapeDtypeStruct((span, rows, side), BF16),
        compiler_params=PARAMS,
        cost_estimate=cost(2 * span * rows * side * side, 4 * span * rows * side + 2 * side * side),
        name="back_columns",
    )(received, basis)


def filter_over(taps_b, frames, batch):
    tap_count = taps_b.shape[0]
    lag = np.arange(frames)[:, None] - np.arange(frames)[None, :]
    onehot = lag[:, :, None] == np.arange(tap_count)
    toeplitz = jnp.sum(jnp.where(onehot, taps_b[None, None, :], 0.0), axis=2).astype(BF16)
    index = np.arange(frames * batch)
    spread = (index[:, None] // batch == np.arange(frames)[None, :]).astype(BF16)
    over_rows = dot(spread, toeplitz, 1, 0).astype(BF16)
    over_both = dot(over_rows, spread, 1, 1).astype(BF16)
    same_mode = index[:, None] % batch == index[None, :] % batch
    return jnp.where(same_mode, over_both, jnp.zeros((), BF16))


def on_device(frames, inverse_taps, mode_rate, frame_factor):
    span, rows, side = frames.shape
    blocks, tiles = lax.axis_size("tm"), lax.axis_size("tile")
    owners = blocks * tiles
    own_modes = side // owners
    batch = min(16, own_modes)
    step = 2 if span % 2 == 0 else 1

    basis = jnp.asarray(cosine_matrix(side))
    taps_b = inverse_taps.astype(BF16).astype(F32)
    filter_matrix = filter_over(taps_b, blocks * span, batch)
    factors = lax.all_gather(frame_factor, "tm", tiled=True)
    rate = lax.dynamic_slice_in_dim(mode_rate, lax.axis_index("tm") * own_modes, own_modes, 1).T

    def exchange(block):
        return lax.all_to_all(block, ("tile", "tm"), split_axis=0, concat_axis=0, tiled=True)

    received = exchange(forward_columns(frames, basis, owners, step))
    row_pass = in_modes(received, factors, filter_matrix, rate, basis, tiles, batch)
    laid_out = lay_out(basis, owners, row_pass)
    return back_columns(exchange(row_pass), laid_out, step)


def solution(mesh):
    return jax.shard_map(
        on_device,
        mesh=mesh,
        in_specs=(P(("grp", "tm"), "tile", None), P(), P(None, "tile"), P(("grp", "tm"))),
        out_specs=P(("grp", "tm"), "tile", None),
        check_vma=False,
    )
```

```python
import functools

import jax
import jax.numpy as jnp
import numpy as np
from jax import lax
from jax.experimental import pallas as pl
from jax.experimental.pallas import tpu as pltpu
from jax.sharding import PartitionSpec as P

F32 = jnp.float32
BF16 = jnp.bfloat16
PARAMS = pltpu.CompilerParams(vmem_limit_bytes=60 * 1024 * 1024)
SMEM = pl.BlockSpec(memory_space=pltpu.SMEM)


def tile_layout(tiles, blocks):
    return [[(e, d) for d in range(blocks)] for e in range(tiles)]


def time_layout(tiles, blocks):
    return [[(e, d) for e in range(tiles)] for d in range(blocks)]


def send_tile(array, e):
    tiles = lax.axis_size("tile")
    return lax.ppermute(array, "tile", [(i, (i + e) % tiles) for i in range(tiles)])


def over_tiles(arrays, layout):
    return [(send_tile(a, e) if e else a, labels) for e, (a, labels) in enumerate(zip(arrays, layout))]


def over_time(arrays, layout):
    sent = [
        lax.ppermute(a, "tm", [(i, i ^ d) for i in range(lax.axis_size("tm"))]) if d else a
        for d, a in enumerate(arrays)
    ]
    return list(zip(sent, layout))


def runs(pieces, wanted):
    where = {label: (i, j) for i, (_, labels) in enumerate(pieces) for j, label in enumerate(labels)}
    found = []
    for label in wanted:
        i, j = where[label]
        if found and found[-1][0] == i and sum(found[-1][1:]) == j:
            found[-1] = (i, found[-1][1], found[-1][2] + 1)
        else:
            found.append((i, j, 1))
    return found


def arrange_kernel(labels, layout, *refs):
    pieces = [(None, some) for some in labels]
    for out_ref, wanted in zip(refs[len(labels):], layout):
        at = 0
        for i, first, count in runs(pieces, wanted):
            out_ref[at:at + count] = refs[i][first:first + count]
            at += count


def arranged(pieces, layout):
    _, span, modes, rows = pieces[0][0].shape

    step = span // 2 if span % 2 == 0 else span

    def block(labels):
        return pl.BlockSpec((len(labels), step, modes, rows), lambda f: (0, f, 0, 0))

    total = sum(len(labels) for labels in layout) * span * modes * rows
    return pl.pallas_call(
        functools.partial(arrange_kernel, [labels for _, labels in pieces], layout),
        grid=(span // step,),
        in_specs=[block(labels) for _, labels in pieces],
        out_specs=[block(labels) for labels in layout],
        out_shape=[jax.ShapeDtypeStruct((len(labels), span, modes, rows), BF16) for labels in layout],
        compiler_params=PARAMS,
        cost_estimate=cost(0, 4 * total),
        name="arrange",
    )(*[array for array, _ in pieces])


def cosine_matrix(points):
    freq_idx = np.arange(points)[:, None]
    cell_idx = np.arange(points)[None, :]
    phase = (2 * cell_idx + 1) * freq_idx % (4 * points)
    values = np.cos(np.pi * phase / (2.0 * points)) * np.sqrt(2.0 / points)
    values = np.where(freq_idx == 0, values / np.sqrt(2.0), values)
    return values.astype(np.float32).astype(BF16)


def dot(a, b, a_dim, b_dim):
    return lax.dot_general(a, b, (((a_dim,), (b_dim,)), ((), ())), preferred_element_type=F32)


def cost(flops, bytes_accessed):
    return pl.CostEstimate(flops=flops, bytes_accessed=bytes_accessed, transcendentals=0)


def whole(array):
    return pl.BlockSpec(array.shape, lambda step: (0,) * array.ndim)


def order_rows(own_ref, basis_ref, ordered_ref, labels, sign):
    tiles, _, modes, _ = basis_ref.shape
    for i, (e, d) in enumerate(labels):
        tile = lax.rem(own_ref[0] + sign * e + tiles, tiles)
        ordered_ref[i * modes:(i + 1) * modes] = basis_ref[tile, own_ref[1] ^ d]


def gathered(refs, pieces, wanted):
    parts = [refs[i][j:j + count] for i, j, count in runs(pieces, wanted)]
    return parts[0] if len(parts) == 1 else jnp.concatenate(parts, axis=0)


def columns_kernel(layout, own_ref, frames_ref, basis_ref, *refs):
    out_refs, ordered_ref = refs[-len(layout) - 1:-1], refs[-1]

    @pl.when(pl.program_id(0) == 0)
    def _():
        order_rows(own_ref, basis_ref, ordered_ref, sum(layout, []), 1)

    step, rows, side = frames_ref.shape
    out = dot(ordered_ref[...], frames_ref[...].reshape(step * rows, side), 1, 1).astype(BF16)
    at = 0
    for out_ref in out_refs:
        count, _, modes, _ = out_ref.shape
        for f in range(step):
            piece = out[at:at + count * modes, f * rows:(f + 1) * rows]
            out_ref[:, f] = piece.reshape(count, modes, rows)
        at += count * modes


def forward_columns(own, frames, basis, layout, after):
    span, rows, side = frames.shape
    tiles, blocks, modes, _ = basis.shape
    total = tiles * blocks * modes
    step = 2 if span % 2 == 0 else 1
    return pl.pallas_call(
        functools.partial(columns_kernel, layout),
        grid=(span // step,),
        in_specs=[SMEM, pl.BlockSpec((step, rows, side), lambda f: (f, 0, 0)), whole(basis)]
        + [pl.BlockSpec(memory_space=pl.ANY)] * len(after),
        out_specs=[pl.BlockSpec((len(labels), step, modes, rows), lambda f: (0, f, 0, 0)) for labels in layout],
        out_shape=[jax.ShapeDtypeStruct((len(labels), span, modes, rows), BF16) for labels in layout],
        scratch_shapes=[pltpu.VMEM((total, side), BF16)],
        compiler_params=PARAMS,
        cost_estimate=cost(2 * span * rows * side * total, 2 * span * rows * (side + total) + 2 * side * total),
        name="columns",
    )(own, frames, basis, *after)


def modes_kernel(labels, layout, own_ref, factor_ref, *refs):
    count = len(labels)
    in_refs, (filter_ref, rate_ref, basis_ref) = refs[:count], refs[count:count + 3]
    out_refs, (ordered_ref, spectra_ref, running_ref) = refs[count + 3:-3], refs[-3:]
    _, span, batch, rows = in_refs[0].shape
    frames = spectra_ref.shape[0] // batch
    blocks = frames // span
    tiles = basis_ref.shape[1] // rows

    @pl.when(pl.program_id(0) == 0)
    def _():
        for e in range(tiles):
            start = lax.rem(own_ref[0] - e + tiles, tiles) * rows
            ordered_ref[:, e * rows:(e + 1) * rows] = basis_ref[:, pl.ds(pl.multiple_of(start, rows), rows)]

    pieces = [(None, some) for some in labels]
    filtered = []
    for e in range(tiles):
        piece = gathered(in_refs, pieces, [(e, d) for d in range(blocks)]).reshape(frames * batch, rows)
        filtered.append(dot(filter_ref[...], piece, 1, 0).astype(BF16))
    column_pass = jnp.concatenate(filtered, axis=1)
    spectra_ref[...] = dot(column_pass, ordered_ref[...], 1, 1)
    retain = jnp.exp(-rate_ref[...])
    state = jnp.zeros_like(retain)
    for block in range(blocks):
        place = block ^ own_ref[1]
        states = []
        for step in range(span):
            at = (block * span + step) * batch
            state = retain * factor_ref[place * span + step] * state + spectra_ref[at:at + batch]
            if batch % 16 == 0:
                start = pl.multiple_of((place * span + step) * batch, batch)
                running_ref[pl.ds(start, batch)] = state.astype(BF16)
            else:
                states.append(state)
        if states:
            start = pl.multiple_of(place * span * batch, span * batch)
            running_ref[pl.ds(start, span * batch)] = jnp.concatenate(states, axis=0).astype(BF16)
    row_pass = dot(running_ref[...], ordered_ref[...], 1, 0).astype(BF16)
    for e in range(tiles):
        piece = row_pass[:, e * rows:(e + 1) * rows].reshape(blocks, span, batch, rows)
        for i, j, length, d in [
            (i, labels_out.index(((tiles - e) % tiles, d)), 1, d)
            for i, labels_out in enumerate(layout)
            for d in range(blocks)
            if ((tiles - e) % tiles, d) in labels_out
        ]:
            out_refs[i][j:j + length] = piece[d:d + length]


def in_modes(own, pieces, factors, filter_matrix, rate, basis, batch, layout):
    side = basis.shape[0]
    _, span, modes, rows = pieces[0][0].shape
    frames = factors.shape[0]

    def block(count):
        return pl.BlockSpec((count, span, batch, rows), lambda k: (0, 0, k, 0))

    return pl.pallas_call(
        functools.partial(modes_kernel, [labels for _, labels in pieces], layout),
        grid=(modes // batch,),
        in_specs=[SMEM, SMEM]
        + [block(len(labels)) for _, labels in pieces]
        + [whole(filter_matrix), pl.BlockSpec((batch, side), lambda k: (k, 0)), whole(basis)],
        out_specs=[block(len(labels)) for labels in layout],
        out_shape=[jax.ShapeDtypeStruct((len(labels), span, modes, rows), BF16) for labels in layout],
        scratch_shapes=[
            pltpu.VMEM((side, side), BF16),
            pltpu.VMEM((frames * batch, side), F32),
            pltpu.VMEM((frames * batch, side), BF16),
        ],
        compiler_params=PARAMS,
        cost_estimate=cost(5 * frames * modes * side * side, 4 * frames * modes * side + 2 * side * side),
        name="in_modes",
    )(own, factors, *[array for array, _ in pieces], filter_matrix, rate, basis)


def back_kernel(labels, more, own_ref, *refs):
    in_refs, (basis_ref, *before_ref, out_ref, ordered_ref) = refs[:len(labels)], refs[len(labels):]

    @pl.when(pl.program_id(0) == 0)
    def _():
        order_rows(own_ref, basis_ref, ordered_ref, sum(labels, []), -1)

    for f in range(out_ref.shape[0]):
        parts = [ref[:, f] for ref in in_refs]
        row_pass = jnp.concatenate(parts, axis=0).reshape(ordered_ref.shape[0], parts[0].shape[-1])
        total = dot(row_pass, ordered_ref[...], 0, 0)
        if more:
            total = before_ref[0][f] + total
        out_ref[f] = total.astype(out_ref.dtype)


def back_columns(own, shape, pieces, basis, before, kind):
    span, rows, side = shape
    modes = pieces[0][0].shape[2]
    step = 2 if span % 2 == 0 else 1
    frames = pl.BlockSpec((step, rows, side), lambda f: (f, 0, 0))
    work = basis.size // side * span * rows
    return pl.pallas_call(
        functools.partial(back_kernel, [labels for _, labels in pieces], len(before)),
        grid=(span // step,),
        in_specs=[SMEM]
        + [pl.BlockSpec((len(labels), step, modes, rows), lambda f: (0, f, 0, 0)) for _, labels in pieces]
        + [whole(basis)]
        + [frames] * len(before),
        out_specs=frames,
        out_shape=jax.ShapeDtypeStruct(shape, kind),
        scratch_shapes=[pltpu.VMEM((basis.size // side, side), BF16)],
        compiler_params=PARAMS,
        cost_estimate=cost(2 * work * side, 2 * work + 6 * span * rows * side + 2 * basis.size),
        name="back_columns",
    )(own, *[array for array, _ in pieces], basis, *before)


def filter_over(taps_b, blocks, span, batch, own):
    tap_count = taps_b.shape[0]
    frames = blocks * span
    place = np.arange(frames)
    source = (place // span ^ own) * span + place % span
    lag = np.arange(frames)[:, None] - source[None, :]
    onehot = lag[:, :, None] == np.arange(tap_count)
    toeplitz = jnp.sum(jnp.where(onehot, taps_b[None, None, :], 0.0), axis=2).astype(BF16)
    index = np.arange(frames * batch)
    spread = (index[:, None] // batch == np.arange(frames)[None, :]).astype(BF16)
    over_rows = dot(spread, toeplitz, 1, 0).astype(BF16)
    over_both = dot(over_rows, spread, 1, 1).astype(BF16)
    same_mode = index[:, None] % batch == index[None, :] % batch
    return jnp.where(same_mode, over_both, jnp.zeros((), BF16))


def on_device(frames, inverse_taps, mode_rate, frame_factor):
    span, rows, side = frames.shape
    blocks, tiles = lax.axis_size("tm"), lax.axis_size("tile")
    own_modes = side // (blocks * tiles)
    batch = min(16, own_modes)
    streams = 2 if own_modes // batch % 2 == 0 else 1
    modes = own_modes // streams
    own_block = lax.axis_index("tm")
    own = jnp.stack([lax.axis_index("tile"), own_block]).astype(jnp.int32)

    matrix = cosine_matrix(side)
    by_stream = np.moveaxis(matrix.reshape(tiles, blocks, streams, modes, side), 2, 0)
    bases = [jnp.asarray(by_stream[i]) for i in range(streams)]
    basis = jnp.asarray(matrix)
    taps_b = inverse_taps.astype(BF16).astype(F32)
    filter_matrix = filter_over(taps_b, blocks, span, batch, own_block)
    rate = lax.dynamic_slice_in_dim(mode_rate, own_block * own_modes, own_modes, 1).T
    rates = [rate[i * modes:(i + 1) * modes] for i in range(streams)]
    by_tile, by_time = tile_layout(tiles, blocks), time_layout(tiles, blocks)
    factors = jnp.concatenate([piece for piece, _ in over_time([frame_factor] * blocks, by_time)])

    def middle(i, pieces, layout):
        return in_modes(own, pieces, factors, filter_matrix, rates[i], basis, batch, layout)

    start_a = forward_columns(own, frames, bases[0], by_tile, [])
    stream_a = over_tiles(start_a, by_tile)
    if streams == 2:
        stream_b = over_time(forward_columns(own, frames, bases[1], by_time, [start_a[0], factors]), by_time)
        stream_b = over_tiles(arranged(stream_b, by_tile), by_tile)
    stream_a = over_time(arranged(stream_a, by_time), by_time)
    stream_a = over_tiles(middle(0, stream_a, by_tile), by_tile)
    if streams == 2:
        stream_b = over_time(middle(1, stream_b, by_time), by_time)
        stream_b = over_tiles(arranged(stream_b, by_tile), by_tile)
    stream_a = over_time(arranged(stream_a, by_time), by_time)
    if streams == 1:
        return back_columns(own, frames.shape, stream_a, bases[0], [], BF16)
    part = back_columns(own, frames.shape, stream_a, bases[0], [], F32)
    return back_columns(own, frames.shape, stream_b, bases[1], [part], BF16)


def solution(mesh):
    return jax.shard_map(
        on_device,
        mesh=mesh,
        in_specs=(P(("grp", "tm"), "tile", None), P(), P(None, "tile"), P(("grp", "tm"))),
        out_specs=P(("grp", "tm"), "tile", None),
        check_vma=False,
    )
```

```python
import functools

import jax
import jax.numpy as jnp
import numpy as np
from jax import lax
from jax.experimental import pallas as pl
from jax.experimental.pallas import tpu as pltpu
from jax.sharding import PartitionSpec as P

F32 = jnp.float32
BF16 = jnp.bfloat16
PARAMS = pltpu.CompilerParams(vmem_limit_bytes=60 * 1024 * 1024)
SMEM = pl.BlockSpec(memory_space=pltpu.SMEM)


def tile_layout(tiles, blocks):
    return [[(e, d) for d in range(blocks)] for e in range(tiles)]


def time_layout(tiles, blocks):
    return [[(e, d) for e in range(tiles)] for d in range(blocks)]


def send_tile(array, e):
    tiles = lax.axis_size("tile")
    return lax.ppermute(array, "tile", [(i, (i + e) % tiles) for i in range(tiles)])


def over_tiles(arrays, layout):
    return [(send_tile(a, e) if e else a, labels) for e, (a, labels) in enumerate(zip(arrays, layout))]


def over_time(arrays, layout):
    sent = list(arrays)
    for d in reversed(range(1, len(arrays))):
        sent[d] = lax.ppermute(arrays[d], "tm", [(i, i ^ d) for i in range(lax.axis_size("tm"))])
    return list(zip(sent, layout))


def pass_kernel(*refs):
    pass


def held(arrays, after):
    anywhere = pl.BlockSpec(memory_space=pl.ANY)
    return pl.pallas_call(
        pass_kernel,
        in_specs=[anywhere] * (len(arrays) + len(after)),
        out_specs=[anywhere] * len(arrays),
        out_shape=[jax.ShapeDtypeStruct(a.shape, a.dtype) for a in arrays],
        input_output_aliases={i: i for i in range(len(arrays))},
        name="held",
    )(*arrays, *after)


def runs(pieces, wanted):
    where = {label: (i, j) for i, (_, labels) in enumerate(pieces) for j, label in enumerate(labels)}
    found = []
    for label in wanted:
        i, j = where[label]
        if found and found[-1][0] == i and sum(found[-1][1:]) == j:
            found[-1] = (i, found[-1][1], found[-1][2] + 1)
        else:
            found.append((i, j, 1))
    return found


def arrange_kernel(labels, layout, *refs):
    pieces = [(None, some) for some in labels]
    for out_ref, wanted in zip(refs[-len(layout):], layout):
        at = 0
        for i, first, count in runs(pieces, wanted):
            out_ref[at:at + count] = refs[i][first:first + count]
            at += count


def arranged(pieces, layout, after=()):
    _, span, modes, rows = pieces[0][0].shape

    step = span // 2 if span % 2 == 0 else span

    def block(labels):
        return pl.BlockSpec((len(labels), step, modes, rows), lambda f: (0, f, 0, 0))

    total = sum(len(labels) for labels in layout) * span * modes * rows
    return pl.pallas_call(
        functools.partial(arrange_kernel, [labels for _, labels in pieces], layout),
        grid=(span // step,),
        in_specs=[block(labels) for _, labels in pieces] + [pl.BlockSpec(memory_space=pl.ANY)] * len(after),
        out_specs=[block(labels) for labels in layout],
        out_shape=[jax.ShapeDtypeStruct((len(labels), span, modes, rows), BF16) for labels in layout],
        compiler_params=PARAMS,
        cost_estimate=cost(0, 4 * total),
        name="arrange",
    )(*[array for array, _ in pieces], *after)


def cosine_matrix(points):
    freq_idx = np.arange(points)[:, None]
    cell_idx = np.arange(points)[None, :]
    phase = (2 * cell_idx + 1) * freq_idx % (4 * points)
    values = np.cos(np.pi * phase / (2.0 * points)) * np.sqrt(2.0 / points)
    values = np.where(freq_idx == 0, values / np.sqrt(2.0), values)
    return values.astype(np.float32).astype(BF16)


def dot(a, b, a_dim, b_dim):
    return lax.dot_general(a, b, (((a_dim,), (b_dim,)), ((), ())), preferred_element_type=F32)


def cost(flops, bytes_accessed):
    return pl.CostEstimate(flops=flops >> 10, bytes_accessed=bytes_accessed >> 10, transcendentals=0)


def whole(array):
    return pl.BlockSpec(array.shape, lambda step: (0,) * array.ndim)


def order_rows(own_ref, basis_ref, ordered_ref, labels, sign):
    tiles, _, modes, _ = basis_ref.shape
    for i, (e, d) in enumerate(labels):
        tile = lax.rem(own_ref[0] + sign * e + tiles, tiles)
        ordered_ref[i * modes:(i + 1) * modes] = basis_ref[tile, own_ref[1] ^ d]


def gathered(refs, pieces, wanted):
    parts = [refs[i][j:j + count] for i, j, count in runs(pieces, wanted)]
    return parts[0] if len(parts) == 1 else jnp.concatenate(parts, axis=0)


def columns_kernel(layouts, own_ref, frames_ref, *refs):
    basis_refs, (*out_refs, ordered_ref) = refs[:len(layouts)], refs[len(layouts):]

    @pl.when(pl.program_id(0) == 0)
    def _():
        size = ordered_ref.shape[0] // len(layouts)
        for i, (layout, basis_ref) in enumerate(zip(layouts, basis_refs)):
            order_rows(own_ref, basis_ref, ordered_ref.at[i * size:(i + 1) * size], sum(layout, []), 1)

    step, rows, side = frames_ref.shape
    out = dot(ordered_ref[...], frames_ref[...].reshape(step * rows, side), 1, 1).astype(BF16)
    at = 0
    for out_ref in out_refs:
        count, _, modes, _ = out_ref.shape
        for f in range(step):
            piece = out[at:at + count * modes, f * rows:(f + 1) * rows]
            out_ref[:, f] = piece.reshape(count, modes, rows)
        at += count * modes


def forward_columns(own, frames, bases, layouts):
    span, rows, side = frames.shape
    modes = bases[0].shape[2]
    total = sum(basis.size for basis in bases) // side
    step = 2 if span % 2 == 0 else 1
    counts = [len(labels) for layout in layouts for labels in layout]
    out = pl.pallas_call(
        functools.partial(columns_kernel, layouts),
        grid=(span // step,),
        in_specs=[SMEM, pl.BlockSpec((step, rows, side), lambda f: (f, 0, 0))] + [whole(basis) for basis in bases],
        out_specs=[pl.BlockSpec((count, step, modes, rows), lambda f: (0, f, 0, 0)) for count in counts],
        out_shape=[jax.ShapeDtypeStruct((count, span, modes, rows), BF16) for count in counts],
        scratch_shapes=[pltpu.VMEM((total, side), BF16)],
        compiler_params=PARAMS,
        cost_estimate=cost(2 * span * rows * side * total, 2 * span * rows * (side + total) + 2 * side * total),
        name="columns",
    )(own, frames, *bases)
    arrays = iter(out)
    return [[next(arrays) for _ in layout] for layout in layouts]


def modes_kernel(labels, layout, own_ref, factor_ref, *refs):
    count = len(labels)
    in_refs, (filter_ref, rate_ref, basis_ref) = refs[:count], refs[count:count + 3]
    out_refs, (ordered_ref, spectra_ref, running_ref) = refs[-3 - len(layout):-3], refs[-3:]
    _, span, batch, rows = in_refs[0].shape
    frames = spectra_ref.shape[0] // batch
    blocks = frames // span
    tiles = basis_ref.shape[1] // rows

    @pl.when(pl.program_id(0) == 0)
    def _():
        for e in range(tiles):
            start = lax.rem(own_ref[0] - e + tiles, tiles) * rows
            ordered_ref[:, e * rows:(e + 1) * rows] = basis_ref[:, pl.ds(pl.multiple_of(start, rows), rows)]

    pieces = [(None, some) for some in labels]
    filtered = []
    for e in range(tiles):
        piece = gathered(in_refs, pieces, [(e, d) for d in range(blocks)]).reshape(frames * batch, rows)
        filtered.append(dot(filter_ref[...], piece, 1, 0).astype(BF16))
    column_pass = jnp.concatenate(filtered, axis=1)
    spectra_ref[...] = dot(column_pass, ordered_ref[...], 1, 1)
    retain = jnp.exp(-rate_ref[...])
    state = jnp.zeros_like(retain)
    for block in range(blocks):
        place = block ^ own_ref[1]
        states = []
        for step in range(span):
            at = (block * span + step) * batch
            state = retain * factor_ref[block * span + step] * state + spectra_ref[at:at + batch]
            if batch % 16 == 0:
                start = pl.multiple_of((place * span + step) * batch, batch)
                running_ref[pl.ds(start, batch)] = state.astype(BF16)
            else:
                states.append(state)
        if states:
            start = pl.multiple_of(place * span * batch, span * batch)
            running_ref[pl.ds(start, span * batch)] = jnp.concatenate(states, axis=0).astype(BF16)
    row_pass = dot(running_ref[...], ordered_ref[...], 1, 0).astype(BF16)
    for e in range(tiles):
        piece = row_pass[:, e * rows:(e + 1) * rows].reshape(blocks, span, batch, rows)
        for i, j, length, d in [
            (i, labels_out.index(((tiles - e) % tiles, d)), 1, d)
            for i, labels_out in enumerate(layout)
            for d in range(blocks)
            if ((tiles - e) % tiles, d) in labels_out
        ]:
            out_refs[i][j:j + length] = piece[d:d + length]


def in_modes(own, pieces, factors, filter_matrix, rate, basis, batch, layout, after):
    side = basis.shape[0]
    _, span, modes, rows = pieces[0][0].shape
    frames = factors.shape[0]

    def block(count):
        return pl.BlockSpec((count, span, batch, rows), lambda k: (0, 0, k, 0))

    return pl.pallas_call(
        functools.partial(modes_kernel, [labels for _, labels in pieces], layout),
        grid=(modes // batch,),
        in_specs=[SMEM, SMEM]
        + [block(len(labels)) for _, labels in pieces]
        + [whole(filter_matrix), pl.BlockSpec((batch, side), lambda k: (k, 0)), whole(basis)]
        + [pl.BlockSpec(memory_space=pl.ANY)] * len(after),
        out_specs=[block(len(labels)) for labels in layout],
        out_shape=[jax.ShapeDtypeStruct((len(labels), span, modes, rows), BF16) for labels in layout],
        scratch_shapes=[
            pltpu.VMEM((side, side), BF16),
            pltpu.VMEM((frames * batch, side), F32),
            pltpu.VMEM((frames * batch, side), BF16),
        ],
        compiler_params=PARAMS,
        cost_estimate=cost(5 * frames * modes * side * side, 4 * frames * modes * side + 2 * side * side),
        name="in_modes",
    )(own, factors, *[array for array, _ in pieces], filter_matrix, rate, basis, *after)


def back_kernel(labels, more, own_ref, *refs):
    in_refs, (basis_ref, *before_ref, out_ref, ordered_ref) = refs[:len(labels)], refs[len(labels):]

    @pl.when(pl.program_id(0) == 0)
    def _():
        order_rows(own_ref, basis_ref, ordered_ref, sum(labels, []), -1)

    for f in range(out_ref.shape[0]):
        parts = [ref[:, f] for ref in in_refs]
        row_pass = jnp.concatenate(parts, axis=0).reshape(ordered_ref.shape[0], parts[0].shape[-1])
        total = dot(row_pass, ordered_ref[...], 0, 0)
        if more:
            total = before_ref[0][f] + total
        out_ref[f] = total.astype(out_ref.dtype)


def back_columns(own, shape, pieces, basis, before, kind):
    span, rows, side = shape
    modes = pieces[0][0].shape[2]
    step = 2 if span % 2 == 0 else 1
    frames = pl.BlockSpec((step, rows, side), lambda f: (f, 0, 0))
    work = basis.size // side * span * rows
    return pl.pallas_call(
        functools.partial(back_kernel, [labels for _, labels in pieces], len(before)),
        grid=(span // step,),
        in_specs=[SMEM]
        + [pl.BlockSpec((len(labels), step, modes, rows), lambda f: (0, f, 0, 0)) for _, labels in pieces]
        + [whole(basis)]
        + [frames] * len(before),
        out_specs=frames,
        out_shape=jax.ShapeDtypeStruct(shape, kind),
        scratch_shapes=[pltpu.VMEM((basis.size // side, side), BF16)],
        compiler_params=PARAMS,
        cost_estimate=cost(2 * work * side, 2 * work + 6 * span * rows * side + 2 * basis.size),
        name="back_columns",
    )(own, *[array for array, _ in pieces], basis, *before)


def filter_over(taps_b, blocks, span, batch, own):
    tap_count = taps_b.shape[0]
    frames = blocks * span
    place = np.arange(frames)
    source = (place // span ^ own) * span + place % span
    lag = np.arange(frames)[:, None] - source[None, :]
    onehot = lag[:, :, None] == np.arange(tap_count)
    toeplitz = jnp.sum(jnp.where(onehot, taps_b[None, None, :], 0.0), axis=2).astype(BF16)
    index = np.arange(frames * batch)
    spread = (index[:, None] // batch == np.arange(frames)[None, :]).astype(BF16)
    over_rows = dot(spread, toeplitz, 1, 0).astype(BF16)
    over_both = dot(over_rows, spread, 1, 1).astype(BF16)
    same_mode = index[:, None] % batch == index[None, :] % batch
    return jnp.where(same_mode, over_both, jnp.zeros((), BF16))


def on_device(frames, inverse_taps, mode_rate, frame_factor):
    span, rows, side = frames.shape
    blocks, tiles = lax.axis_size("tm"), lax.axis_size("tile")
    own_modes = side // (blocks * tiles)
    batch = min(16, own_modes)
    streams = 2 if own_modes // batch % 2 == 0 else 1
    modes = own_modes // streams
    own_block = lax.axis_index("tm")
    own = jnp.stack([lax.axis_index("tile"), own_block]).astype(jnp.int32)

    matrix = cosine_matrix(side)
    by_stream = np.moveaxis(matrix.reshape(tiles, blocks, streams, modes, side), 2, 0)
    bases = [jnp.asarray(by_stream[i]) for i in range(streams)]
    basis = jnp.asarray(matrix)
    taps_b = inverse_taps.astype(BF16).astype(F32)
    filter_matrix = filter_over(taps_b, blocks, span, batch, own_block)
    rate = lax.dynamic_slice_in_dim(mode_rate, own_block * own_modes, own_modes, 1).T
    rates = [rate[i * modes:(i + 1) * modes] for i in range(streams)]
    by_tile, by_time = tile_layout(tiles, blocks), time_layout(tiles, blocks)

    def middle(i, pieces, layout, after=()):
        return in_modes(own, pieces, factors, filter_matrix, rates[i], basis, batch, layout, after)

    stream_a, *stream_b = forward_columns(own, frames, bases, [by_tile, by_time][:streams])
    factors = lax.all_gather(held([frame_factor], stream_a[:1])[0], "tm", tiled=True)
    if streams == 1:
        stream_a = over_tiles(stream_a, by_tile)
        stream_a = over_time(arranged(stream_a, by_time), by_time)
        stream_a = over_tiles(middle(0, stream_a, by_tile), by_tile)
        stream_a = over_time(arranged(stream_a, by_time), by_time)
        return back_columns(own, frames.shape, stream_a, bases[0], [], BF16)
    stream_a = over_tiles(stream_a, by_tile)
    stream_b = arranged(over_time(stream_b[0], by_time), by_tile, [factors, filter_matrix, *rates])
    stream_a = over_time(arranged(stream_a, by_time, stream_b[:1]), by_time)
    stream_b = over_tiles(stream_b, by_tile)
    stream_a = middle(0, stream_a, by_tile, [array for array, _ in stream_b[1:-1]])
    middle_b = middle(1, stream_b, by_time, stream_a[:1])
    stream_a = over_tiles(stream_a, by_tile)
    stream_b = arranged(over_time(middle_b, by_time), by_tile)
    stream_a = over_time(arranged(stream_a, by_time), by_time)
    stream_b = over_tiles(stream_b, by_tile)
    part = back_columns(own, frames.shape, stream_a, bases[0], [], F32)
    return back_columns(own, frames.shape, stream_b, bases[1], [part], BF16)


def solution(mesh):
    return jax.shard_map(
        on_device,
        mesh=mesh,
        in_specs=(P(("grp", "tm"), "tile", None), P(), P(None, "tile"), P(("grp", "tm"))),
        out_specs=P(("grp", "tm"), "tile", None),
        check_vma=False,
    )
```

```python
import functools

import jax
import jax.numpy as jnp
import numpy as np
from jax import lax
from jax.experimental import pallas as pl
from jax.experimental.pallas import tpu as pltpu
from jax.sharding import PartitionSpec as P

F32 = jnp.float32
BF16 = jnp.bfloat16
PARAMS = pltpu.CompilerParams(vmem_limit_bytes=60 * 1024 * 1024)
SMEM = pl.BlockSpec(memory_space=pltpu.SMEM)


def tile_layout(tiles, blocks):
    return [[(e, d) for d in range(blocks)] for e in range(tiles)]


def time_layout(tiles, blocks):
    return [[(e, d) for e in range(tiles)] for d in range(blocks)]


def send_tile(array, e):
    tiles = lax.axis_size("tile")
    return lax.ppermute(array, "tile", [(i, (i + e) % tiles) for i in range(tiles)])


def over_tiles(arrays, layout):
    return [(send_tile(a, e) if e else a, labels) for e, (a, labels) in enumerate(zip(arrays, layout))]


def over_time(arrays, layout):
    sent = list(arrays)
    for d in reversed(range(1, len(arrays))):
        sent[d] = lax.ppermute(arrays[d], "tm", [(i, i ^ d) for i in range(lax.axis_size("tm"))])
    return list(zip(sent, layout))


def pass_kernel(*refs):
    pass


def held(arrays, after):
    anywhere = pl.BlockSpec(memory_space=pl.ANY)
    return pl.pallas_call(
        pass_kernel,
        in_specs=[anywhere] * (len(arrays) + len(after)),
        out_specs=[anywhere] * len(arrays),
        out_shape=[jax.ShapeDtypeStruct(a.shape, a.dtype) for a in arrays],
        input_output_aliases={i: i for i in range(len(arrays))},
        name="held",
    )(*arrays, *after)


def runs(pieces, wanted):
    where = {label: (i, j) for i, (_, labels) in enumerate(pieces) for j, label in enumerate(labels)}
    found = []
    for label in wanted:
        i, j = where[label]
        if found and found[-1][0] == i and sum(found[-1][1:]) == j:
            found[-1] = (i, found[-1][1], found[-1][2] + 1)
        else:
            found.append((i, j, 1))
    return found


def arrange_kernel(labels, layout, *refs):
    pieces = [(None, some) for some in labels]
    for out_ref, wanted in zip(refs[-len(layout):], layout):
        at = 0
        for i, first, count in runs(pieces, wanted):
            out_ref[at:at + count] = refs[i][first:first + count]
            at += count


def arranged(pieces, layout, after=()):
    _, span, modes, rows = pieces[0][0].shape

    step = span // 2 if span % 2 == 0 else span

    def block(labels):
        return pl.BlockSpec((len(labels), step, modes, rows), lambda f: (0, f, 0, 0))

    total = sum(len(labels) for labels in layout) * span * modes * rows
    return pl.pallas_call(
        functools.partial(arrange_kernel, [labels for _, labels in pieces], layout),
        grid=(span // step,),
        in_specs=[block(labels) for _, labels in pieces] + [pl.BlockSpec(memory_space=pl.ANY)] * len(after),
        out_specs=[block(labels) for labels in layout],
        out_shape=[jax.ShapeDtypeStruct((len(labels), span, modes, rows), BF16) for labels in layout],
        compiler_params=PARAMS,
        cost_estimate=cost(0, 4 * total),
        name="arrange",
    )(*[array for array, _ in pieces], *after)


def cosine_matrix(points):
    freq_idx = np.arange(points)[:, None]
    cell_idx = np.arange(points)[None, :]
    phase = (2 * cell_idx + 1) * freq_idx % (4 * points)
    values = np.cos(np.pi * phase / (2.0 * points)) * np.sqrt(2.0 / points)
    values = np.where(freq_idx == 0, values / np.sqrt(2.0), values)
    return values.astype(np.float32).astype(BF16)


def dot(a, b, a_dim, b_dim):
    return lax.dot_general(a, b, (((a_dim,), (b_dim,)), ((), ())), preferred_element_type=F32)


def cost(flops, bytes_accessed):
    return pl.CostEstimate(flops=flops >> 10, bytes_accessed=bytes_accessed >> 10, transcendentals=0)


def whole(array):
    return pl.BlockSpec(array.shape, lambda step: (0,) * array.ndim)


def order_rows(own_ref, basis_ref, ordered_ref, labels, sign):
    tiles, _, modes, _ = basis_ref.shape
    for i, (e, d) in enumerate(labels):
        tile = lax.rem(own_ref[0] + sign * e + tiles, tiles)
        ordered_ref[i * modes:(i + 1) * modes] = basis_ref[tile, own_ref[1] ^ d]


def gathered(refs, pieces, wanted):
    parts = [refs[i][j:j + count] for i, j, count in runs(pieces, wanted)]
    return parts[0] if len(parts) == 1 else jnp.concatenate(parts, axis=0)


def columns_kernel(layouts, own_ref, frames_ref, *refs):
    basis_refs, (*out_refs, ordered_ref) = refs[:len(layouts)], refs[len(layouts):]

    @pl.when(pl.program_id(0) == 0)
    def _():
        size = ordered_ref.shape[0] // len(layouts)
        for i, (layout, basis_ref) in enumerate(zip(layouts, basis_refs)):
            order_rows(own_ref, basis_ref, ordered_ref.at[i * size:(i + 1) * size], sum(layout, []), 1)

    step, rows, side = frames_ref.shape
    out = dot(ordered_ref[...], frames_ref[...].reshape(step * rows, side), 1, 1).astype(BF16)
    at = 0
    for out_ref in out_refs:
        count, _, modes, _ = out_ref.shape
        for f in range(step):
            piece = out[at:at + count * modes, f * rows:(f + 1) * rows]
            out_ref[:, f] = piece.reshape(count, modes, rows)
        at += count * modes


def forward_columns(own, frames, bases, layouts):
    span, rows, side = frames.shape
    modes = bases[0].shape[2]
    total = sum(basis.size for basis in bases) // side
    step = 2 if span % 2 == 0 else 1
    counts = [len(labels) for layout in layouts for labels in layout]
    out = pl.pallas_call(
        functools.partial(columns_kernel, layouts),
        grid=(span // step,),
        in_specs=[SMEM, pl.BlockSpec((step, rows, side), lambda f: (f, 0, 0))] + [whole(basis) for basis in bases],
        out_specs=[pl.BlockSpec((count, step, modes, rows), lambda f: (0, f, 0, 0)) for count in counts],
        out_shape=[jax.ShapeDtypeStruct((count, span, modes, rows), BF16) for count in counts],
        scratch_shapes=[pltpu.VMEM((total, side), BF16)],
        compiler_params=PARAMS,
        cost_estimate=cost(2 * span * rows * side * total, 2 * span * rows * (side + total) + 2 * side * total),
        name="columns",
    )(own, frames, *bases)
    arrays = iter(out)
    return [[next(arrays) for _ in layout] for layout in layouts]


def modes_kernel(labels, layout, own_ref, factor_ref, *refs):
    count = len(labels)
    in_refs, (filter_ref, rate_ref, basis_ref) = refs[:count], refs[count:count + 3]
    out_refs, (ordered_ref, spectra_ref, running_ref) = refs[-3 - len(layout):-3], refs[-3:]
    _, span, batch, rows = in_refs[0].shape
    frames = spectra_ref.shape[0] // batch
    blocks = frames // span
    tiles = basis_ref.shape[1] // rows

    @pl.when(pl.program_id(0) == 0)
    def _():
        for e in range(tiles):
            start = lax.rem(own_ref[0] - e + tiles, tiles) * rows
            ordered_ref[:, e * rows:(e + 1) * rows] = basis_ref[:, pl.ds(pl.multiple_of(start, rows), rows)]

    pieces = [(None, some) for some in labels]
    filtered = []
    for e in range(tiles):
        piece = gathered(in_refs, pieces, [(e, d) for d in range(blocks)]).reshape(frames * batch, rows)
        filtered.append(dot(filter_ref[...], piece, 1, 0).astype(BF16))
    column_pass = jnp.concatenate(filtered, axis=1)
    spectra_ref[...] = dot(column_pass, ordered_ref[...], 1, 1)
    retain = jnp.exp(-rate_ref[...])
    state = jnp.zeros_like(retain)
    for block in range(blocks):
        place = block ^ own_ref[1]
        states = []
        for step in range(span):
            at = (block * span + step) * batch
            state = retain * factor_ref[block * span + step] * state + spectra_ref[at:at + batch]
            if batch % 16 == 0:
                start = pl.multiple_of((place * span + step) * batch, batch)
                running_ref[pl.ds(start, batch)] = state.astype(BF16)
            else:
                states.append(state)
        if states:
            start = pl.multiple_of(place * span * batch, span * batch)
            running_ref[pl.ds(start, span * batch)] = jnp.concatenate(states, axis=0).astype(BF16)
    row_pass = dot(running_ref[...], ordered_ref[...], 1, 0).astype(BF16)
    for e in range(tiles):
        piece = row_pass[:, e * rows:(e + 1) * rows].reshape(blocks, span, batch, rows)
        for i, j, length, d in [
            (i, labels_out.index(((tiles - e) % tiles, d)), 1, d)
            for i, labels_out in enumerate(layout)
            for d in range(blocks)
            if ((tiles - e) % tiles, d) in labels_out
        ]:
            out_refs[i][j:j + length] = piece[d:d + length]


def in_modes(own, pieces, factors, filter_matrix, rate, basis, batch, layout, after):
    side = basis.shape[0]
    _, span, modes, rows = pieces[0][0].shape
    frames = factors.shape[0]

    def block(count):
        return pl.BlockSpec((count, span, batch, rows), lambda k: (0, 0, k, 0))

    return pl.pallas_call(
        functools.partial(modes_kernel, [labels for _, labels in pieces], layout),
        grid=(modes // batch,),
        in_specs=[SMEM, SMEM]
        + [block(len(labels)) for _, labels in pieces]
        + [whole(filter_matrix), pl.BlockSpec((batch, side), lambda k: (k, 0)), whole(basis)]
        + [pl.BlockSpec(memory_space=pl.ANY)] * len(after),
        out_specs=[block(len(labels)) for labels in layout],
        out_shape=[jax.ShapeDtypeStruct((len(labels), span, modes, rows), BF16) for labels in layout],
        scratch_shapes=[
            pltpu.VMEM((side, side), BF16),
            pltpu.VMEM((frames * batch, side), F32),
            pltpu.VMEM((frames * batch, side), BF16),
        ],
        compiler_params=PARAMS,
        cost_estimate=cost(5 * frames * modes * side * side, 4 * frames * modes * side + 2 * side * side),
        name="in_modes",
    )(own, factors, *[array for array, _ in pieces], filter_matrix, rate, basis, *after)


def back_kernel(labels, more, own_ref, *refs):
    in_refs, (basis_ref, *before_ref, out_ref, ordered_ref) = refs[:len(labels)], refs[len(labels):]

    @pl.when(pl.program_id(0) == 0)
    def _():
        order_rows(own_ref, basis_ref, ordered_ref, sum(labels, []), -1)

    for f in range(out_ref.shape[0]):
        parts = [ref[:, f] for ref in in_refs]
        row_pass = jnp.concatenate(parts, axis=0).reshape(ordered_ref.shape[0], parts[0].shape[-1])
        total = dot(row_pass, ordered_ref[...], 0, 0)
        if more:
            total = before_ref[0][f] + total
        out_ref[f] = total.astype(out_ref.dtype)


def back_columns(own, shape, pieces, basis, before, kind):
    span, rows, side = shape
    modes = pieces[0][0].shape[2]
    step = 2 if span % 2 == 0 else 1
    frames = pl.BlockSpec((step, rows, side), lambda f: (f, 0, 0))
    work = basis.size // side * span * rows
    return pl.pallas_call(
        functools.partial(back_kernel, [labels for _, labels in pieces], len(before)),
        grid=(span // step,),
        in_specs=[SMEM]
        + [pl.BlockSpec((len(labels), step, modes, rows), lambda f: (0, f, 0, 0)) for _, labels in pieces]
        + [whole(basis)]
        + [frames] * len(before),
        out_specs=frames,
        out_shape=jax.ShapeDtypeStruct(shape, kind),
        scratch_shapes=[pltpu.VMEM((basis.size // side, side), BF16)],
        compiler_params=PARAMS,
        cost_estimate=cost(2 * work * side, 2 * work + 6 * span * rows * side + 2 * basis.size),
        name="back_columns",
    )(own, *[array for array, _ in pieces], basis, *before)


def filter_over(taps_b, blocks, span, batch, own):
    tap_count = taps_b.shape[0]
    frames = blocks * span
    place = np.arange(frames)
    source = (place // span ^ own) * span + place % span
    lag = np.arange(frames)[:, None] - source[None, :]
    onehot = lag[:, :, None] == np.arange(tap_count)
    toeplitz = jnp.sum(jnp.where(onehot, taps_b[None, None, :], 0.0), axis=2).astype(BF16)
    index = np.arange(frames * batch)
    spread = (index[:, None] // batch == np.arange(frames)[None, :]).astype(BF16)
    over_rows = dot(spread, toeplitz, 1, 0).astype(BF16)
    over_both = dot(over_rows, spread, 1, 1).astype(BF16)
    same_mode = index[:, None] % batch == index[None, :] % batch
    return jnp.where(same_mode, over_both, jnp.zeros((), BF16))


def on_device(frames, inverse_taps, mode_rate, frame_factor):
    span, rows, side = frames.shape
    blocks, tiles = lax.axis_size("tm"), lax.axis_size("tile")
    own_modes = side // (blocks * tiles)
    batch = min(16, own_modes)
    streams = 2 if own_modes // batch % 2 == 0 else 1
    modes = own_modes // streams
    own_block = lax.axis_index("tm")
    own = jnp.stack([lax.axis_index("tile"), own_block]).astype(jnp.int32)

    matrix = cosine_matrix(side)
    by_stream = np.moveaxis(matrix.reshape(tiles, blocks, streams, modes, side), 2, 0)
    bases = [jnp.asarray(by_stream[i]) for i in range(streams)]
    basis = jnp.asarray(matrix)
    taps_b = inverse_taps.astype(BF16).astype(F32)
    filter_matrix = filter_over(taps_b, blocks, span, batch, own_block)
    rate = lax.dynamic_slice_in_dim(mode_rate, own_block * own_modes, own_modes, 1).T
    rates = [rate[i * modes:(i + 1) * modes] for i in range(streams)]
    by_tile, by_time = tile_layout(tiles, blocks), time_layout(tiles, blocks)

    def middle(i, pieces, layout, after=()):
        return in_modes(own, pieces, factors, filter_matrix, rates[i], basis, batch, layout, after)

    def short(pieces):
        return [array for e, (array, _) in enumerate(pieces) if e not in (0, tiles // 2)]

    stream_a, *stream_b = forward_columns(own, frames, bases, [by_tile, by_time][:streams])
    factors = lax.all_gather(held([frame_factor], stream_a[:1])[0], "tm", tiled=True)
    if streams == 1:
        stream_a = over_tiles(stream_a, by_tile)
        stream_a = over_time(arranged(stream_a, by_time), by_time)
        stream_a = over_tiles(middle(0, stream_a, by_tile), by_tile)
        stream_a = over_time(arranged(stream_a, by_time), by_time)
        return back_columns(own, frames.shape, stream_a, bases[0], [], BF16)
    stream_a = over_tiles(stream_a, by_tile)
    stream_b = arranged(over_time(stream_b[0], by_time), by_tile, [factors, filter_matrix, *rates, *short(stream_a)])
    stream_a = over_time(arranged(stream_a, by_time, stream_b[:1]), by_time)
    stream_b = over_tiles(stream_b, by_tile)
    stream_a = middle(0, stream_a, by_tile, short(stream_b))
    middle_b = middle(1, stream_b, by_time, stream_a[:1])
    stream_a = over_tiles(stream_a, by_tile)
    stream_b = arranged(over_time(middle_b, by_time), by_tile)
    stream_a = over_time(arranged(stream_a, by_time), by_time)
    stream_b = over_tiles(stream_b, by_tile)
    part = back_columns(own, frames.shape, stream_a, bases[0], [], F32)
    return back_columns(own, frames.shape, stream_b, bases[1], [part], BF16)


def solution(mesh):
    return jax.shard_map(
        on_device,
        mesh=mesh,
        in_specs=(P(("grp", "tm"), "tile", None), P(), P(None, "tile"), P(("grp", "tm"))),
        out_specs=P(("grp", "tm"), "tile", None),
        check_vma=False,
    )
```

```python
import functools

import jax
import jax.numpy as jnp
import numpy as np
from jax import lax
from jax.experimental import pallas as pl
from jax.experimental.pallas import tpu as pltpu
from jax.sharding import PartitionSpec as P

F32 = jnp.float32
BF16 = jnp.bfloat16
MIB = 1024 * 1024
PARAMS = pltpu.CompilerParams(vmem_limit_bytes=60 * MIB)
SMEM = pl.BlockSpec(memory_space=pltpu.SMEM)


def tile_layout(tiles, blocks):
    return [[(e, d) for d in range(blocks)] for e in range(tiles)]


def time_layout(tiles, blocks):
    return [[(e, d) for e in range(tiles)] for d in range(blocks)]


def send_tile(array, e):
    tiles = lax.axis_size("tile")
    return lax.ppermute(array, "tile", [(i, (i + e) % tiles) for i in range(tiles)])


def over_tiles(arrays, layout):
    return [(send_tile(a, e) if e else a, labels) for e, (a, labels) in enumerate(zip(arrays, layout))]


def over_time(arrays, layout):
    sent = list(arrays)
    for d in reversed(range(1, len(arrays))):
        sent[d] = lax.ppermute(arrays[d], "tm", [(i, i ^ d) for i in range(lax.axis_size("tm"))])
    return list(zip(sent, layout))


def pass_kernel(*refs):
    pass


def held(arrays, after):
    anywhere = pl.BlockSpec(memory_space=pl.ANY)
    return pl.pallas_call(
        pass_kernel,
        in_specs=[anywhere] * (len(arrays) + len(after)),
        out_specs=[anywhere] * len(arrays),
        out_shape=[jax.ShapeDtypeStruct(a.shape, a.dtype) for a in arrays],
        input_output_aliases={i: i for i in range(len(arrays))},
        name="held",
    )(*arrays, *after)


def runs(pieces, wanted):
    where = {label: (i, j) for i, (_, labels) in enumerate(pieces) for j, label in enumerate(labels)}
    found = []
    for label in wanted:
        i, j = where[label]
        if found and found[-1][0] == i and sum(found[-1][1:]) == j:
            found[-1] = (i, found[-1][1], found[-1][2] + 1)
        else:
            found.append((i, j, 1))
    return found


def arrange_kernel(labels, layout, *refs):
    pieces = [(None, some) for some in labels]
    for out_ref, wanted in zip(refs[-len(layout):], layout):
        at = 0
        for i, first, count in runs(pieces, wanted):
            out_ref[at:at + count] = refs[i][first:first + count]
            at += count


def arranged(pieces, layout, after=()):
    _, span, modes, rows = pieces[0][0].shape

    step = span // 2 if span % 2 == 0 else span

    def block(labels):
        return pl.BlockSpec((len(labels), step, modes, rows), lambda f: (0, f, 0, 0))

    total = sum(len(labels) for labels in layout) * span * modes * rows
    return pl.pallas_call(
        functools.partial(arrange_kernel, [labels for _, labels in pieces], layout),
        grid=(span // step,),
        in_specs=[block(labels) for _, labels in pieces] + [pl.BlockSpec(memory_space=pl.ANY)] * len(after),
        out_specs=[block(labels) for labels in layout],
        out_shape=[jax.ShapeDtypeStruct((len(labels), span, modes, rows), BF16) for labels in layout],
        compiler_params=pltpu.CompilerParams(vmem_limit_bytes=16 * MIB),
        cost_estimate=cost(0, 4 * total),
        name="arrange",
    )(*[array for array, _ in pieces], *after)


def cosine_matrix(points):
    freq_idx = np.arange(points)[:, None]
    cell_idx = np.arange(points)[None, :]
    phase = (2 * cell_idx + 1) * freq_idx % (4 * points)
    values = np.cos(np.pi * phase / (2.0 * points)) * np.sqrt(2.0 / points)
    values = np.where(freq_idx == 0, values / np.sqrt(2.0), values)
    return values.astype(np.float32).astype(BF16)


def dot(a, b, a_dim, b_dim):
    return lax.dot_general(a, b, (((a_dim,), (b_dim,)), ((), ())), preferred_element_type=F32)


def cost(flops, bytes_accessed):
    return pl.CostEstimate(flops=flops >> 10, bytes_accessed=bytes_accessed >> 10, transcendentals=0)


def whole(array):
    return pl.BlockSpec(array.shape, lambda step: (0,) * array.ndim)


def order_rows(own_ref, basis_ref, ordered_ref, labels, sign):
    tiles, _, modes, _ = basis_ref.shape
    for i, (e, d) in enumerate(labels):
        tile = lax.rem(own_ref[0] + sign * e + tiles, tiles)
        ordered_ref[i * modes:(i + 1) * modes] = basis_ref[tile, own_ref[1] ^ d]


def gathered(refs, pieces, wanted):
    parts = [refs[i][j:j + count] for i, j, count in runs(pieces, wanted)]
    return parts[0] if len(parts) == 1 else jnp.concatenate(parts, axis=0)


def columns_kernel(layouts, own_ref, frames_ref, *refs):
    basis_refs, (*out_refs, ordered_ref) = refs[:len(layouts)], refs[len(layouts):]

    @pl.when(pl.program_id(0) == 0)
    def _():
        size = ordered_ref.shape[0] // len(layouts)
        for i, (layout, basis_ref) in enumerate(zip(layouts, basis_refs)):
            order_rows(own_ref, basis_ref, ordered_ref.at[i * size:(i + 1) * size], sum(layout, []), 1)

    step, rows, side = frames_ref.shape
    out = dot(ordered_ref[...], frames_ref[...].reshape(step * rows, side), 1, 1).astype(BF16)
    at = 0
    for out_ref in out_refs:
        count, _, modes, _ = out_ref.shape
        for f in range(step):
            piece = out[at:at + count * modes, f * rows:(f + 1) * rows]
            out_ref[:, f] = piece.reshape(count, modes, rows)
        at += count * modes


def forward_columns(own, frames, bases, layouts):
    span, rows, side = frames.shape
    modes = bases[0].shape[2]
    total = sum(basis.size for basis in bases) // side
    step = 2 if span % 2 == 0 else 1
    counts = [len(labels) for layout in layouts for labels in layout]
    out = pl.pallas_call(
        functools.partial(columns_kernel, layouts),
        grid=(span // step,),
        in_specs=[SMEM, pl.BlockSpec((step, rows, side), lambda f: (f, 0, 0))] + [whole(basis) for basis in bases],
        out_specs=[pl.BlockSpec((count, step, modes, rows), lambda f: (0, f, 0, 0)) for count in counts],
        out_shape=[jax.ShapeDtypeStruct((count, span, modes, rows), BF16) for count in counts],
        scratch_shapes=[pltpu.VMEM((total, side), BF16)],
        compiler_params=PARAMS,
        cost_estimate=cost(2 * span * rows * side * total, 2 * span * rows * (side + total) + 2 * side * total),
        name="columns",
    )(own, frames, *bases)
    arrays = iter(out)
    return [[next(arrays) for _ in layout] for layout in layouts]


def modes_kernel(labels, layout, own_ref, factor_ref, *refs):
    count = len(labels)
    in_refs, (filter_ref, rate_ref, basis_ref) = refs[:count], refs[count:count + 3]
    out_refs, (ordered_ref, spectra_ref, running_ref) = refs[-3 - len(layout):-3], refs[-3:]
    _, span, batch, rows = in_refs[0].shape
    frames = spectra_ref.shape[0] // batch
    blocks = frames // span
    tiles = basis_ref.shape[1] // rows

    @pl.when(pl.program_id(0) == 0)
    def _():
        for e in range(tiles):
            start = lax.rem(own_ref[0] - e + tiles, tiles) * rows
            ordered_ref[:, e * rows:(e + 1) * rows] = basis_ref[:, pl.ds(pl.multiple_of(start, rows), rows)]

    pieces = [(None, some) for some in labels]
    filtered = []
    for e in range(tiles):
        piece = gathered(in_refs, pieces, [(e, d) for d in range(blocks)]).reshape(frames * batch, rows)
        filtered.append(dot(filter_ref[...], piece, 1, 0).astype(BF16))
    column_pass = jnp.concatenate(filtered, axis=1)
    spectra_ref[...] = dot(column_pass, ordered_ref[...], 1, 1)
    retain = jnp.exp(-rate_ref[...])
    state = jnp.zeros_like(retain)
    for block in range(blocks):
        place = block ^ own_ref[1]
        states = []
        for step in range(span):
            at = (block * span + step) * batch
            state = retain * factor_ref[block * span + step] * state + spectra_ref[at:at + batch]
            if batch % 16 == 0:
                start = pl.multiple_of((place * span + step) * batch, batch)
                running_ref[pl.ds(start, batch)] = state.astype(BF16)
            else:
                states.append(state)
        if states:
            start = pl.multiple_of(place * span * batch, span * batch)
            running_ref[pl.ds(start, span * batch)] = jnp.concatenate(states, axis=0).astype(BF16)
    row_pass = dot(running_ref[...], ordered_ref[...], 1, 0).astype(BF16)
    for e in range(tiles):
        piece = row_pass[:, e * rows:(e + 1) * rows].reshape(blocks, span, batch, rows)
        for i, j, length, d in [
            (i, labels_out.index(((tiles - e) % tiles, d)), 1, d)
            for i, labels_out in enumerate(layout)
            for d in range(blocks)
            if ((tiles - e) % tiles, d) in labels_out
        ]:
            out_refs[i][j:j + length] = piece[d:d + length]


def in_modes(own, pieces, factors, filter_matrix, rate, basis, batch, layout, after):
    side = basis.shape[0]
    _, span, modes, rows = pieces[0][0].shape
    frames = factors.shape[0]

    def block(count):
        return pl.BlockSpec((count, span, batch, rows), lambda k: (0, 0, k, 0))

    return pl.pallas_call(
        functools.partial(modes_kernel, [labels for _, labels in pieces], layout),
        grid=(modes // batch,),
        in_specs=[SMEM, SMEM]
        + [block(len(labels)) for _, labels in pieces]
        + [whole(filter_matrix), pl.BlockSpec((batch, side), lambda k: (k, 0)), whole(basis)]
        + [pl.BlockSpec(memory_space=pl.ANY)] * len(after),
        out_specs=[block(len(labels)) for labels in layout],
        out_shape=[jax.ShapeDtypeStruct((len(labels), span, modes, rows), BF16) for labels in layout],
        scratch_shapes=[
            pltpu.VMEM((side, side), BF16),
            pltpu.VMEM((frames * batch, side), F32),
            pltpu.VMEM((frames * batch, side), BF16),
        ],
        compiler_params=PARAMS,
        cost_estimate=cost(5 * frames * modes * side * side, 4 * frames * modes * side + 2 * side * side),
        name="in_modes",
    )(own, factors, *[array for array, _ in pieces], filter_matrix, rate, basis, *after)


def back_kernel(labels, more, own_ref, *refs):
    in_refs, (basis_ref, *before_ref, out_ref, ordered_ref) = refs[:len(labels)], refs[len(labels):]

    @pl.when(pl.program_id(0) == 0)
    def _():
        order_rows(own_ref, basis_ref, ordered_ref, sum(labels, []), -1)

    for f in range(out_ref.shape[0]):
        parts = [ref[:, f] for ref in in_refs]
        row_pass = jnp.concatenate(parts, axis=0).reshape(ordered_ref.shape[0], parts[0].shape[-1])
        total = dot(row_pass, ordered_ref[...], 0, 0)
        if more:
            total = before_ref[0][f] + total
        out_ref[f] = total.astype(out_ref.dtype)


def back_columns(own, shape, pieces, basis, before, kind):
    span, rows, side = shape
    modes = pieces[0][0].shape[2]
    step = 2 if span % 2 == 0 else 1
    frames = pl.BlockSpec((step, rows, side), lambda f: (f, 0, 0))
    work = basis.size // side * span * rows
    return pl.pallas_call(
        functools.partial(back_kernel, [labels for _, labels in pieces], len(before)),
        grid=(span // step,),
        in_specs=[SMEM]
        + [pl.BlockSpec((len(labels), step, modes, rows), lambda f: (0, f, 0, 0)) for _, labels in pieces]
        + [whole(basis)]
        + [frames] * len(before),
        out_specs=frames,
        out_shape=jax.ShapeDtypeStruct(shape, kind),
        scratch_shapes=[pltpu.VMEM((basis.size // side, side), BF16)],
        compiler_params=pltpu.CompilerParams(vmem_limit_bytes=24 * MIB),
        cost_estimate=cost(2 * work * side, 2 * work + 6 * span * rows * side + 2 * basis.size),
        name="back_columns",
    )(own, *[array for array, _ in pieces], basis, *before)


def filter_over(taps_b, blocks, span, batch, own):
    tap_count = taps_b.shape[0]
    frames = blocks * span
    place = np.arange(frames)
    source = (place // span ^ own) * span + place % span
    lag = np.arange(frames)[:, None] - source[None, :]
    onehot = lag[:, :, None] == np.arange(tap_count)
    toeplitz = jnp.sum(jnp.where(onehot, taps_b[None, None, :], 0.0), axis=2).astype(BF16)
    index = np.arange(frames * batch)
    spread = (index[:, None] // batch == np.arange(frames)[None, :]).astype(BF16)
    over_rows = dot(spread, toeplitz, 1, 0).astype(BF16)
    over_both = dot(over_rows, spread, 1, 1).astype(BF16)
    same_mode = index[:, None] % batch == index[None, :] % batch
    return jnp.where(same_mode, over_both, jnp.zeros((), BF16))


def on_device(frames, inverse_taps, mode_rate, frame_factor):
    span, rows, side = frames.shape
    blocks, tiles = lax.axis_size("tm"), lax.axis_size("tile")
    own_modes = side // (blocks * tiles)
    batch = min(16, own_modes)
    streams = 2 if own_modes // batch % 2 == 0 else 1
    modes = own_modes // streams
    own_block = lax.axis_index("tm")
    own = jnp.stack([lax.axis_index("tile"), own_block]).astype(jnp.int32)

    matrix = cosine_matrix(side)
    by_stream = np.moveaxis(matrix.reshape(tiles, blocks, streams, modes, side), 2, 0)
    bases = [jnp.asarray(by_stream[i]) for i in range(streams)]
    basis = jnp.asarray(matrix)
    taps_b = inverse_taps.astype(BF16).astype(F32)
    filter_matrix = filter_over(taps_b, blocks, span, batch, own_block)
    rate = lax.dynamic_slice_in_dim(mode_rate, own_block * own_modes, own_modes, 1).T
    rates = [rate[i * modes:(i + 1) * modes] for i in range(streams)]
    by_tile, by_time = tile_layout(tiles, blocks), time_layout(tiles, blocks)

    def middle(i, pieces, layout, after=()):
        return in_modes(own, pieces, factors, filter_matrix, rates[i], basis, batch, layout, after)

    def short(pieces):
        return [array for e, (array, _) in enumerate(pieces) if e not in (0, tiles // 2)]

    stream_a, *stream_b = forward_columns(own, frames, bases, [by_tile, by_time][:streams])
    factors = lax.all_gather(held([frame_factor], stream_a[:1])[0], "tm", tiled=True)
    if streams == 1:
        stream_a = over_tiles(stream_a, by_tile)
        stream_a = over_time(arranged(stream_a, by_time), by_time)
        stream_a = over_tiles(middle(0, stream_a, by_tile), by_tile)
        stream_a = over_time(arranged(stream_a, by_time), by_time)
        return back_columns(own, frames.shape, stream_a, bases[0], [], BF16)
    stream_a = over_tiles(stream_a, by_tile)
    stream_b = arranged(over_time(stream_b[0], by_time), by_tile, [factors, filter_matrix, *rates, *short(stream_a)])
    stream_a = over_time(arranged(stream_a, by_time, stream_b[:1]), by_time)
    stream_b = over_tiles(stream_b, by_tile)
    stream_a = middle(0, stream_a, by_tile, short(stream_b))
    middle_b = middle(1, stream_b, by_time, stream_a[:1])
    stream_a = over_tiles(stream_a, by_tile)
    stream_b = arranged(over_time(middle_b, by_time), by_tile)
    stream_a = over_time(arranged(stream_a, by_time), by_time)
    stream_b = over_tiles(stream_b, by_tile)
    part = back_columns(own, frames.shape, stream_a, bases[0], [], F32)
    return back_columns(own, frames.shape, stream_b, bases[1], [part], BF16)


def solution(mesh):
    return jax.shard_map(
        on_device,
        mesh=mesh,
        in_specs=(P(("grp", "tm"), "tile", None), P(), P(None, "tile"), P(("grp", "tm"))),
        out_specs=P(("grp", "tm"), "tile", None),
        check_vma=False,
    )
```

```python
import functools

import jax
import jax.numpy as jnp
import numpy as np
from jax import lax
from jax.experimental import pallas as pl
from jax.experimental.pallas import tpu as pltpu
from jax.sharding import PartitionSpec as P

F32 = jnp.float32
BF16 = jnp.bfloat16
MIB = 1024 * 1024
PARAMS = pltpu.CompilerParams(vmem_limit_bytes=60 * MIB)
SMEM = pl.BlockSpec(memory_space=pltpu.SMEM)


def tile_layout(tiles, blocks):
    return [[(e, d) for d in range(blocks)] for e in range(tiles)]


def time_layout(tiles, blocks):
    return [[(e, d) for e in range(tiles)] for d in range(blocks)]


def send_tile(array, e):
    tiles = lax.axis_size("tile")
    return lax.ppermute(array, "tile", [(i, (i + e) % tiles) for i in range(tiles)])


def over_tiles(arrays, layout):
    return [(send_tile(a, e) if e else a, labels) for e, (a, labels) in enumerate(zip(arrays, layout))]


def over_time(arrays, layout):
    sent = list(arrays)
    for d in reversed(range(1, len(arrays))):
        sent[d] = lax.ppermute(arrays[d], "tm", [(i, i ^ d) for i in range(lax.axis_size("tm"))])
    return list(zip(sent, layout))


def pass_kernel(*refs):
    pass


def held(arrays, after):
    anywhere = pl.BlockSpec(memory_space=pl.ANY)
    return pl.pallas_call(
        pass_kernel,
        in_specs=[anywhere] * (len(arrays) + len(after)),
        out_specs=[anywhere] * len(arrays),
        out_shape=[jax.ShapeDtypeStruct(a.shape, a.dtype) for a in arrays],
        input_output_aliases={i: i for i in range(len(arrays))},
        name="held",
    )(*arrays, *after)


def runs(pieces, wanted):
    where = {label: (i, j) for i, (_, labels) in enumerate(pieces) for j, label in enumerate(labels)}
    found = []
    for label in wanted:
        i, j = where[label]
        if found and found[-1][0] == i and sum(found[-1][1:]) == j:
            found[-1] = (i, found[-1][1], found[-1][2] + 1)
        else:
            found.append((i, j, 1))
    return found


def arrange_kernel(labels, layout, *refs):
    pieces = [(None, some) for some in labels]
    for out_ref, wanted in zip(refs[-len(layout):], layout):
        at = 0
        for i, first, count in runs(pieces, wanted):
            out_ref[at:at + count] = refs[i][first:first + count]
            at += count


def arranged(pieces, layout, after=()):
    _, span, modes, rows = pieces[0][0].shape

    step = span // 2 if span % 2 == 0 else span

    def block(labels):
        return pl.BlockSpec((len(labels), step, modes, rows), lambda f: (0, f, 0, 0))

    total = sum(len(labels) for labels in layout) * span * modes * rows
    return pl.pallas_call(
        functools.partial(arrange_kernel, [labels for _, labels in pieces], layout),
        grid=(span // step,),
        in_specs=[block(labels) for _, labels in pieces] + [pl.BlockSpec(memory_space=pl.ANY)] * len(after),
        out_specs=[block(labels) for labels in layout],
        out_shape=[jax.ShapeDtypeStruct((len(labels), span, modes, rows), BF16) for labels in layout],
        compiler_params=pltpu.CompilerParams(vmem_limit_bytes=16 * MIB),
        cost_estimate=cost(0, 4 * total),
        name="arrange",
    )(*[array for array, _ in pieces], *after)


def cosine_matrix(points):
    freq_idx = np.arange(points)[:, None]
    cell_idx = np.arange(points)[None, :]
    phase = (2 * cell_idx + 1) * freq_idx % (4 * points)
    values = np.cos(np.pi * phase / (2.0 * points)) * np.sqrt(2.0 / points)
    values = np.where(freq_idx == 0, values / np.sqrt(2.0), values)
    return values.astype(np.float32).astype(BF16)


def dot(a, b, a_dim, b_dim):
    return lax.dot_general(a, b, (((a_dim,), (b_dim,)), ((), ())), preferred_element_type=F32)


def cost(flops, bytes_accessed):
    return pl.CostEstimate(flops=flops >> 10, bytes_accessed=bytes_accessed >> 10, transcendentals=0)


def whole(array):
    return pl.BlockSpec(array.shape, lambda step: (0,) * array.ndim)


def order_rows(own_ref, basis_ref, ordered_ref, labels, sign):
    tiles, _, modes, _ = basis_ref.shape
    for i, (e, d) in enumerate(labels):
        tile = lax.rem(own_ref[0] + sign * e + tiles, tiles)
        ordered_ref[i * modes:(i + 1) * modes] = basis_ref[tile, own_ref[1] ^ d]


def gathered(refs, pieces, wanted):
    parts = [refs[i][j:j + count] for i, j, count in runs(pieces, wanted)]
    return parts[0] if len(parts) == 1 else jnp.concatenate(parts, axis=0)


def columns_kernel(layouts, own_ref, frames_ref, *refs):
    basis_refs, (*out_refs, ordered_ref) = refs[:len(layouts)], refs[len(layouts):]

    @pl.when(pl.program_id(0) == 0)
    def _():
        size = ordered_ref.shape[0] // len(layouts)
        for i, (layout, basis_ref) in enumerate(zip(layouts, basis_refs)):
            order_rows(own_ref, basis_ref, ordered_ref.at[i * size:(i + 1) * size], sum(layout, []), 1)

    step, rows, side = frames_ref.shape
    out = dot(ordered_ref[...], frames_ref[...].reshape(step * rows, side), 1, 1).astype(BF16)
    at = 0
    for out_ref in out_refs:
        count, _, modes, _ = out_ref.shape
        for f in range(step):
            piece = out[at:at + count * modes, f * rows:(f + 1) * rows]
            out_ref[:, f] = piece.reshape(count, modes, rows)
        at += count * modes


def forward_columns(own, frames, bases, layouts):
    span, rows, side = frames.shape
    modes = bases[0].shape[2]
    total = sum(basis.size for basis in bases) // side
    step = 2 if span % 2 == 0 else 1
    counts = [len(labels) for layout in layouts for labels in layout]
    out = pl.pallas_call(
        functools.partial(columns_kernel, layouts),
        grid=(span // step,),
        in_specs=[SMEM, pl.BlockSpec((step, rows, side), lambda f: (f, 0, 0))] + [whole(basis) for basis in bases],
        out_specs=[pl.BlockSpec((count, step, modes, rows), lambda f: (0, f, 0, 0)) for count in counts],
        out_shape=[jax.ShapeDtypeStruct((count, span, modes, rows), BF16) for count in counts],
        scratch_shapes=[pltpu.VMEM((total, side), BF16)],
        compiler_params=PARAMS,
        cost_estimate=cost(2 * span * rows * side * total, 2 * span * rows * (side + total) + 2 * side * total),
        name="columns",
    )(own, frames, *bases)
    arrays = iter(out)
    return [[next(arrays) for _ in layout] for layout in layouts]


def modes_kernel(labels, layout, own_ref, factor_ref, *refs):
    count = len(labels)
    in_refs, (filter_ref, rate_ref, basis_ref) = refs[:count], refs[count:count + 3]
    out_refs, (ordered_ref, spectra_ref, running_ref) = refs[-3 - len(layout):-3], refs[-3:]
    _, span, batch, rows = in_refs[0].shape
    frames = spectra_ref.shape[0] // batch
    blocks = frames // span
    tiles = basis_ref.shape[1] // rows

    @pl.when(pl.program_id(0) == 0)
    def _():
        for e in range(tiles):
            start = lax.rem(own_ref[0] - e + tiles, tiles) * rows
            ordered_ref[:, e * rows:(e + 1) * rows] = basis_ref[:, pl.ds(pl.multiple_of(start, rows), rows)]

    pieces = [(None, some) for some in labels]
    filtered = []
    for e in range(tiles):
        piece = gathered(in_refs, pieces, [(e, d) for d in range(blocks)]).reshape(frames * batch, rows)
        filtered.append(dot(filter_ref[...], piece, 1, 0).astype(BF16))
    column_pass = jnp.concatenate(filtered, axis=1)
    spectra_ref[...] = dot(column_pass, ordered_ref[...], 1, 1)
    retain = jnp.exp(-rate_ref[...])
    state = jnp.zeros_like(retain)
    for block in range(blocks):
        place = block ^ own_ref[1]
        states = []
        for step in range(span):
            at = (block * span + step) * batch
            state = retain * factor_ref[block * span + step] * state + spectra_ref[at:at + batch]
            if batch % 16 == 0:
                start = pl.multiple_of((place * span + step) * batch, batch)
                running_ref[pl.ds(start, batch)] = state.astype(BF16)
            else:
                states.append(state)
        if states:
            start = pl.multiple_of(place * span * batch, span * batch)
            running_ref[pl.ds(start, span * batch)] = jnp.concatenate(states, axis=0).astype(BF16)
    row_pass = dot(running_ref[...], ordered_ref[...], 1, 0).astype(BF16)
    for e in range(tiles):
        piece = row_pass[:, e * rows:(e + 1) * rows].reshape(blocks, span, batch, rows)
        for i, j, length, d in [
            (i, labels_out.index(((tiles - e) % tiles, d)), 1, d)
            for i, labels_out in enumerate(layout)
            for d in range(blocks)
            if ((tiles - e) % tiles, d) in labels_out
        ]:
            out_refs[i][j:j + length] = piece[d:d + length]


def in_modes(own, pieces, factors, filter_matrix, rate, basis, batch, layout, after):
    side = basis.shape[0]
    _, span, modes, rows = pieces[0][0].shape
    frames = factors.shape[0]

    def block(count):
        return pl.BlockSpec((count, span, batch, rows), lambda k: (0, 0, k, 0))

    return pl.pallas_call(
        functools.partial(modes_kernel, [labels for _, labels in pieces], layout),
        grid=(modes // batch,),
        in_specs=[SMEM, SMEM]
        + [block(len(labels)) for _, labels in pieces]
        + [whole(filter_matrix), pl.BlockSpec((batch, side), lambda k: (k, 0)), whole(basis)]
        + [pl.BlockSpec(memory_space=pl.ANY)] * len(after),
        out_specs=[block(len(labels)) for labels in layout],
        out_shape=[jax.ShapeDtypeStruct((len(labels), span, modes, rows), BF16) for labels in layout],
        scratch_shapes=[
            pltpu.VMEM((side, side), BF16),
            pltpu.VMEM((frames * batch, side), F32),
            pltpu.VMEM((frames * batch, side), BF16),
        ],
        compiler_params=pltpu.CompilerParams(vmem_limit_bytes=40 * MIB),
        cost_estimate=cost(5 * frames * modes * side * side, 4 * frames * modes * side + 2 * side * side),
        name="in_modes",
    )(own, factors, *[array for array, _ in pieces], filter_matrix, rate, basis, *after)


def back_kernel(labels, more, own_ref, *refs):
    in_refs, (basis_ref, *before_ref, out_ref, ordered_ref) = refs[:len(labels)], refs[len(labels):]

    @pl.when(pl.program_id(0) == 0)
    def _():
        order_rows(own_ref, basis_ref, ordered_ref, sum(labels, []), -1)

    for f in range(out_ref.shape[0]):
        parts = [ref[:, f] for ref in in_refs]
        row_pass = jnp.concatenate(parts, axis=0).reshape(ordered_ref.shape[0], parts[0].shape[-1])
        total = dot(row_pass, ordered_ref[...], 0, 0)
        if more:
            total = before_ref[0][f] + total
        out_ref[f] = total.astype(out_ref.dtype)


def back_columns(own, shape, pieces, basis, before, kind):
    span, rows, side = shape
    modes = pieces[0][0].shape[2]
    step = 2 if span % 2 == 0 else 1
    frames = pl.BlockSpec((step, rows, side), lambda f: (f, 0, 0))
    work = basis.size // side * span * rows
    return pl.pallas_call(
        functools.partial(back_kernel, [labels for _, labels in pieces], len(before)),
        grid=(span // step,),
        in_specs=[SMEM]
        + [pl.BlockSpec((len(labels), step, modes, rows), lambda f: (0, f, 0, 0)) for _, labels in pieces]
        + [whole(basis)]
        + [frames] * len(before),
        out_specs=frames,
        out_shape=jax.ShapeDtypeStruct(shape, kind),
        scratch_shapes=[pltpu.VMEM((basis.size // side, side), BF16)],
        compiler_params=pltpu.CompilerParams(vmem_limit_bytes=24 * MIB),
        cost_estimate=cost(2 * work * side, 2 * work + 6 * span * rows * side + 2 * basis.size),
        name="back_columns",
    )(own, *[array for array, _ in pieces], basis, *before)


def filter_over(taps_b, blocks, span, batch, own):
    tap_count = taps_b.shape[0]
    frames = blocks * span
    place = np.arange(frames)
    source = (place // span ^ own) * span + place % span
    lag = np.arange(frames)[:, None] - source[None, :]
    onehot = lag[:, :, None] == np.arange(tap_count)
    toeplitz = jnp.sum(jnp.where(onehot, taps_b[None, None, :], 0.0), axis=2).astype(BF16)
    index = np.arange(frames * batch)
    spread = (index[:, None] // batch == np.arange(frames)[None, :]).astype(BF16)
    over_rows = dot(spread, toeplitz, 1, 0).astype(BF16)
    over_both = dot(over_rows, spread, 1, 1).astype(BF16)
    same_mode = index[:, None] % batch == index[None, :] % batch
    return jnp.where(same_mode, over_both, jnp.zeros((), BF16))


def on_device(frames, inverse_taps, mode_rate, frame_factor):
    span, rows, side = frames.shape
    blocks, tiles = lax.axis_size("tm"), lax.axis_size("tile")
    own_modes = side // (blocks * tiles)
    batch = min(16, own_modes)
    streams = 2 if own_modes // batch % 2 == 0 else 1
    modes = own_modes // streams
    own_block = lax.axis_index("tm")
    own = jnp.stack([lax.axis_index("tile"), own_block]).astype(jnp.int32)

    matrix = cosine_matrix(side)
    by_stream = np.moveaxis(matrix.reshape(tiles, blocks, streams, modes, side), 2, 0)
    bases = [jnp.asarray(by_stream[i]) for i in range(streams)]
    basis = jnp.asarray(matrix)
    taps_b = inverse_taps.astype(BF16).astype(F32)
    filter_matrix = filter_over(taps_b, blocks, span, batch, own_block)
    rate = lax.dynamic_slice_in_dim(mode_rate, own_block * own_modes, own_modes, 1).T
    rates = [rate[i * modes:(i + 1) * modes] for i in range(streams)]
    by_tile, by_time = tile_layout(tiles, blocks), time_layout(tiles, blocks)

    def middle(i, pieces, layout, after=()):
        return in_modes(own, pieces, factors, filter_matrix, rates[i], basis, batch, layout, after)

    def short(pieces):
        return [array for e, (array, _) in enumerate(pieces) if e not in (0, tiles // 2)]

    stream_a, *stream_b = forward_columns(own, frames, bases, [by_tile, by_time][:streams])
    factors = lax.all_gather(held([frame_factor], stream_a[:1])[0], "tm", tiled=True)
    if streams == 1:
        stream_a = over_tiles(stream_a, by_tile)
        stream_a = over_time(arranged(stream_a, by_time), by_time)
        stream_a = over_tiles(middle(0, stream_a, by_tile), by_tile)
        stream_a = over_time(arranged(stream_a, by_time), by_time)
        return back_columns(own, frames.shape, stream_a, bases[0], [], BF16)
    stream_a = over_tiles(stream_a, by_tile)
    stream_b = arranged(over_time(stream_b[0], by_time), by_tile, [factors, filter_matrix, *rates, *short(stream_a)])
    stream_a = over_time(arranged(stream_a, by_time, stream_b[:1]), by_time)
    stream_b = over_tiles(stream_b, by_tile)
    stream_a = middle(0, stream_a, by_tile, short(stream_b))
    middle_b = middle(1, stream_b, by_time, stream_a[:1])
    stream_a = over_tiles(stream_a, by_tile)
    stream_b = arranged(over_time(middle_b, by_time), by_tile)
    stream_a = over_time(arranged(stream_a, by_time), by_time)
    stream_b = over_tiles(stream_b, by_tile)
    part = back_columns(own, frames.shape, stream_a, bases[0], [], F32)
    return back_columns(own, frames.shape, stream_b, bases[1], [part], BF16)


def solution(mesh):
    return jax.shard_map(
        on_device,
        mesh=mesh,
        in_specs=(P(("grp", "tm"), "tile", None), P(), P(None, "tile"), P(("grp", "tm"))),
        out_specs=P(("grp", "tm"), "tile", None),
        check_vma=False,
    )
```

```python
import functools

import jax
import jax.numpy as jnp
import numpy as np
from jax import lax
from jax.experimental import pallas as pl
from jax.experimental.pallas import tpu as pltpu
from jax.sharding import PartitionSpec as P

F32 = jnp.float32
BF16 = jnp.bfloat16
MIB = 1024 * 1024
PARAMS = pltpu.CompilerParams(vmem_limit_bytes=60 * MIB)
SMEM = pl.BlockSpec(memory_space=pltpu.SMEM)


def tile_layout(tiles, blocks):
    return [[(e, d) for d in range(blocks)] for e in range(tiles)]


def time_layout(tiles, blocks):
    return [[(e, d) for e in range(tiles)] for d in range(blocks)]


def send_tile(array, e):
    tiles = lax.axis_size("tile")
    return lax.ppermute(array, "tile", [(i, (i + e) % tiles) for i in range(tiles)])


def over_tiles(arrays, layout):
    return [(send_tile(a, e) if e else a, labels) for e, (a, labels) in enumerate(zip(arrays, layout))]


def over_time(arrays, layout):
    sent = list(arrays)
    for d in reversed(range(1, len(arrays))):
        sent[d] = lax.ppermute(arrays[d], "tm", [(i, i ^ d) for i in range(lax.axis_size("tm"))])
    return list(zip(sent, layout))


def pass_kernel(*refs):
    pass


def held(arrays, after):
    anywhere = pl.BlockSpec(memory_space=pl.ANY)
    return pl.pallas_call(
        pass_kernel,
        in_specs=[anywhere] * (len(arrays) + len(after)),
        out_specs=[anywhere] * len(arrays),
        out_shape=[jax.ShapeDtypeStruct(a.shape, a.dtype) for a in arrays],
        input_output_aliases={i: i for i in range(len(arrays))},
        name="held",
    )(*arrays, *after)


def runs(pieces, wanted):
    where = {label: (i, j) for i, (_, labels) in enumerate(pieces) for j, label in enumerate(labels)}
    found = []
    for label in wanted:
        i, j = where[label]
        if found and found[-1][0] == i and sum(found[-1][1:]) == j:
            found[-1] = (i, found[-1][1], found[-1][2] + 1)
        else:
            found.append((i, j, 1))
    return found


def arrange_kernel(labels, layout, *refs):
    pieces = [(None, some) for some in labels]
    for out_ref, wanted in zip(refs[-len(layout):], layout):
        at = 0
        for i, first, count in runs(pieces, wanted):
            out_ref[at:at + count] = refs[i][first:first + count]
            at += count


def arranged(pieces, layout, after=()):
    _, span, modes, rows = pieces[0][0].shape

    step = span // 2 if span % 2 == 0 else span

    def block(labels):
        return pl.BlockSpec((len(labels), step, modes, rows), lambda f: (0, f, 0, 0))

    total = sum(len(labels) for labels in layout) * span * modes * rows
    return pl.pallas_call(
        functools.partial(arrange_kernel, [labels for _, labels in pieces], layout),
        grid=(span // step,),
        in_specs=[block(labels) for _, labels in pieces] + [pl.BlockSpec(memory_space=pl.ANY)] * len(after),
        out_specs=[block(labels) for labels in layout],
        out_shape=[jax.ShapeDtypeStruct((len(labels), span, modes, rows), BF16) for labels in layout],
        compiler_params=pltpu.CompilerParams(vmem_limit_bytes=16 * MIB),
        cost_estimate=cost(0, 4 * total),
        name="arrange",
    )(*[array for array, _ in pieces], *after)


def cosine_matrix(points):
    freq_idx = np.arange(points)[:, None]
    cell_idx = np.arange(points)[None, :]
    phase = (2 * cell_idx + 1) * freq_idx % (4 * points)
    values = np.cos(np.pi * phase / (2.0 * points)) * np.sqrt(2.0 / points)
    values = np.where(freq_idx == 0, values / np.sqrt(2.0), values)
    return values.astype(np.float32).astype(BF16)


def dot(a, b, a_dim, b_dim):
    return lax.dot_general(a, b, (((a_dim,), (b_dim,)), ((), ())), preferred_element_type=F32)


def cost(flops, bytes_accessed):
    return pl.CostEstimate(flops=flops >> 10, bytes_accessed=bytes_accessed >> 10, transcendentals=0)


def whole(array):
    return pl.BlockSpec(array.shape, lambda step: (0,) * array.ndim)


def order_rows(own_ref, basis_ref, ordered_ref, labels, sign, share, sizes):
    tiles, blocks, shares = sizes
    modes = ordered_ref.shape[0] // len(labels)
    for i, (e, d) in enumerate(labels):
        tile = lax.rem(own_ref[0] + sign * e + tiles, tiles)
        start = ((tile * blocks + (own_ref[1] ^ d)) * shares + share) * modes
        ordered_ref[i * modes:(i + 1) * modes] = basis_ref[pl.ds(pl.multiple_of(start, modes), modes)]


def gathered(refs, pieces, wanted):
    parts = [refs[i][j:j + count] for i, j, count in runs(pieces, wanted)]
    return parts[0] if len(parts) == 1 else jnp.concatenate(parts, axis=0)


def columns_kernel(layouts, sizes, own_ref, frames_ref, basis_ref, *refs):
    *out_refs, ordered_ref = refs

    @pl.when(pl.program_id(0) == 0)
    def _():
        size = ordered_ref.shape[0] // len(layouts)
        for i, layout in enumerate(layouts):
            order_rows(own_ref, basis_ref, ordered_ref.at[i * size:(i + 1) * size], sum(layout, []), 1, i, sizes)

    step, rows, side = frames_ref.shape
    out = dot(ordered_ref[...], frames_ref[...].reshape(step * rows, side), 1, 1).astype(BF16)
    at = 0
    for out_ref in out_refs:
        count, _, modes, _ = out_ref.shape
        for f in range(step):
            piece = out[at:at + count * modes, f * rows:(f + 1) * rows]
            out_ref[:, f] = piece.reshape(count, modes, rows)
        at += count * modes


def forward_columns(own, frames, basis, layouts, sizes):
    span, rows, side = frames.shape
    modes = side // (sizes[0] * sizes[1] * sizes[2])
    total = side
    step = 2 if span % 2 == 0 else 1
    counts = [len(labels) for layout in layouts for labels in layout]
    out = pl.pallas_call(
        functools.partial(columns_kernel, layouts, sizes),
        grid=(span // step,),
        in_specs=[SMEM, pl.BlockSpec((step, rows, side), lambda f: (f, 0, 0)), whole(basis)],
        out_specs=[pl.BlockSpec((count, step, modes, rows), lambda f: (0, f, 0, 0)) for count in counts],
        out_shape=[jax.ShapeDtypeStruct((count, span, modes, rows), BF16) for count in counts],
        scratch_shapes=[pltpu.VMEM((total, side), BF16)],
        compiler_params=PARAMS,
        cost_estimate=cost(2 * span * rows * side * total, 2 * span * rows * (side + total) + 2 * side * total),
        name="columns",
    )(own, frames, basis)
    arrays = iter(out)
    return [[next(arrays) for _ in layout] for layout in layouts]


def modes_kernel(labels, layout, own_ref, factor_ref, *refs):
    count = len(labels)
    in_refs, (filter_ref, rate_ref, basis_ref) = refs[:count], refs[count:count + 3]
    out_refs, (ordered_ref, spectra_ref, running_ref) = refs[-3 - len(layout):-3], refs[-3:]
    _, span, batch, rows = in_refs[0].shape
    frames = spectra_ref.shape[0] // batch
    blocks = frames // span
    tiles = basis_ref.shape[1] // rows

    @pl.when(pl.program_id(0) == 0)
    def _():
        for e in range(tiles):
            start = lax.rem(own_ref[0] - e + tiles, tiles) * rows
            ordered_ref[:, e * rows:(e + 1) * rows] = basis_ref[:, pl.ds(pl.multiple_of(start, rows), rows)]

    pieces = [(None, some) for some in labels]
    filtered = []
    for e in range(tiles):
        piece = gathered(in_refs, pieces, [(e, d) for d in range(blocks)]).reshape(frames * batch, rows)
        filtered.append(dot(filter_ref[...], piece, 1, 0).astype(BF16))
    column_pass = jnp.concatenate(filtered, axis=1)
    spectra_ref[...] = dot(column_pass, ordered_ref[...], 1, 1)
    retain = jnp.exp(-rate_ref[...])
    state = jnp.zeros_like(retain)
    for block in range(blocks):
        place = block ^ own_ref[1]
        states = []
        for step in range(span):
            at = (block * span + step) * batch
            state = retain * factor_ref[block * span + step] * state + spectra_ref[at:at + batch]
            if batch % 16 == 0:
                start = pl.multiple_of((place * span + step) * batch, batch)
                running_ref[pl.ds(start, batch)] = state.astype(BF16)
            else:
                states.append(state)
        if states:
            start = pl.multiple_of(place * span * batch, span * batch)
            running_ref[pl.ds(start, span * batch)] = jnp.concatenate(states, axis=0).astype(BF16)
    row_pass = dot(running_ref[...], ordered_ref[...], 1, 0).astype(BF16)
    for e in range(tiles):
        piece = row_pass[:, e * rows:(e + 1) * rows].reshape(blocks, span, batch, rows)
        for i, j, length, d in [
            (i, labels_out.index(((tiles - e) % tiles, d)), 1, d)
            for i, labels_out in enumerate(layout)
            for d in range(blocks)
            if ((tiles - e) % tiles, d) in labels_out
        ]:
            out_refs[i][j:j + length] = piece[d:d + length]


def in_modes(own, pieces, factors, filter_matrix, rate, basis, batch, layout, after):
    side = basis.shape[0]
    _, span, modes, rows = pieces[0][0].shape
    frames = factors.shape[0]

    def block(count):
        return pl.BlockSpec((count, span, batch, rows), lambda k: (0, 0, k, 0))

    return pl.pallas_call(
        functools.partial(modes_kernel, [labels for _, labels in pieces], layout),
        grid=(modes // batch,),
        in_specs=[SMEM, SMEM]
        + [block(len(labels)) for _, labels in pieces]
        + [whole(filter_matrix), pl.BlockSpec((batch, side), lambda k: (k, 0)), whole(basis)]
        + [pl.BlockSpec(memory_space=pl.ANY)] * len(after),
        out_specs=[block(len(labels)) for labels in layout],
        out_shape=[jax.ShapeDtypeStruct((len(labels), span, modes, rows), BF16) for labels in layout],
        scratch_shapes=[
            pltpu.VMEM((side, side), BF16),
            pltpu.VMEM((frames * batch, side), F32),
            pltpu.VMEM((frames * batch, side), BF16),
        ],
        compiler_params=pltpu.CompilerParams(vmem_limit_bytes=40 * MIB),
        cost_estimate=cost(5 * frames * modes * side * side, 4 * frames * modes * side + 2 * side * side),
        name="in_modes",
    )(own, factors, *[array for array, _ in pieces], filter_matrix, rate, basis, *after)


def back_kernel(labels, more, share, sizes, own_ref, *refs):
    in_refs, (basis_ref, *before_ref, out_ref, ordered_ref) = refs[:len(labels)], refs[len(labels):]

    @pl.when(pl.program_id(0) == 0)
    def _():
        order_rows(own_ref, basis_ref, ordered_ref, sum(labels, []), -1, share, sizes)

    for f in range(out_ref.shape[0]):
        parts = [ref[:, f] for ref in in_refs]
        row_pass = jnp.concatenate(parts, axis=0).reshape(ordered_ref.shape[0], parts[0].shape[-1])
        total = dot(row_pass, ordered_ref[...], 0, 0)
        if more:
            total = before_ref[0][f] + total
        out_ref[f] = total.astype(out_ref.dtype)


def back_columns(own, shape, pieces, basis, before, kind, share, sizes):
    span, rows, side = shape
    modes = pieces[0][0].shape[2]
    step = 2 if span % 2 == 0 else 1
    frames = pl.BlockSpec((step, rows, side), lambda f: (f, 0, 0))
    work = side // sizes[2] * span * rows
    return pl.pallas_call(
        functools.partial(back_kernel, [labels for _, labels in pieces], len(before), share, sizes),
        grid=(span // step,),
        in_specs=[SMEM]
        + [pl.BlockSpec((len(labels), step, modes, rows), lambda f: (0, f, 0, 0)) for _, labels in pieces]
        + [whole(basis)]
        + [frames] * len(before),
        out_specs=frames,
        out_shape=jax.ShapeDtypeStruct(shape, kind),
        scratch_shapes=[pltpu.VMEM((side // sizes[2], side), BF16)],
        compiler_params=pltpu.CompilerParams(vmem_limit_bytes=24 * MIB),
        cost_estimate=cost(2 * work * side, 2 * work + 6 * span * rows * side + 2 * basis.size),
        name="back_columns",
    )(own, *[array for array, _ in pieces], basis, *before)


def filter_over(taps_b, blocks, span, batch, own):
    tap_count = taps_b.shape[0]
    frames = blocks * span
    place = np.arange(frames)
    source = (place // span ^ own) * span + place % span
    lag = np.arange(frames)[:, None] - source[None, :]
    onehot = lag[:, :, None] == np.arange(tap_count)
    toeplitz = jnp.sum(jnp.where(onehot, taps_b[None, None, :], 0.0), axis=2).astype(BF16)
    index = np.arange(frames * batch)
    spread = (index[:, None] // batch == np.arange(frames)[None, :]).astype(BF16)
    over_rows = dot(spread, toeplitz, 1, 0).astype(BF16)
    over_both = dot(over_rows, spread, 1, 1).astype(BF16)
    same_mode = index[:, None] % batch == index[None, :] % batch
    return jnp.where(same_mode, over_both, jnp.zeros((), BF16))


def on_device(frames, inverse_taps, mode_rate, frame_factor):
    span, rows, side = frames.shape
    blocks, tiles = lax.axis_size("tm"), lax.axis_size("tile")
    own_modes = side // (blocks * tiles)
    batch = min(16, own_modes)
    streams = 2 if own_modes // batch % 2 == 0 else 1
    modes = own_modes // streams
    own_block = lax.axis_index("tm")
    own = jnp.stack([lax.axis_index("tile"), own_block]).astype(jnp.int32)

    basis = jnp.asarray(cosine_matrix(side))
    sizes = (tiles, blocks, streams)
    taps_b = inverse_taps.astype(BF16).astype(F32)
    filter_matrix = filter_over(taps_b, blocks, span, batch, own_block)
    rate = lax.dynamic_slice_in_dim(mode_rate, own_block * own_modes, own_modes, 1).T
    rates = [rate[i * modes:(i + 1) * modes] for i in range(streams)]
    by_tile, by_time = tile_layout(tiles, blocks), time_layout(tiles, blocks)

    def middle(i, pieces, layout, after=()):
        return in_modes(own, pieces, factors, filter_matrix, rates[i], basis, batch, layout, after)

    def short(pieces):
        return [array for e, (array, _) in enumerate(pieces) if e not in (0, tiles // 2)]

    stream_a, *stream_b = forward_columns(own, frames, basis, [by_tile, by_time][:streams], sizes)
    factors = lax.all_gather(held([frame_factor], stream_a[:1])[0], "tm", tiled=True)
    if streams == 1:
        stream_a = over_tiles(stream_a, by_tile)
        stream_a = over_time(arranged(stream_a, by_time), by_time)
        stream_a = over_tiles(middle(0, stream_a, by_tile), by_tile)
        stream_a = over_time(arranged(stream_a, by_time), by_time)
        return back_columns(own, frames.shape, stream_a, basis, [], BF16, 0, sizes)
    stream_a = over_tiles(stream_a, by_tile)
    stream_b = arranged(over_time(stream_b[0], by_time), by_tile, [factors, filter_matrix, *rates, *short(stream_a)])
    stream_a = over_time(arranged(stream_a, by_time, stream_b[:1]), by_time)
    stream_b = over_tiles(stream_b, by_tile)
    stream_a = middle(0, stream_a, by_tile, short(stream_b))
    middle_b = middle(1, stream_b, by_time, stream_a[:1])
    stream_a = over_tiles(stream_a, by_tile)
    stream_b = arranged(over_time(middle_b, by_time), by_tile)
    stream_a = over_time(arranged(stream_a, by_time), by_time)
    stream_b = over_tiles(stream_b, by_tile)
    part = back_columns(own, frames.shape, stream_a, basis, [], F32, 0, sizes)
    return back_columns(own, frames.shape, stream_b, basis, [part], BF16, 1, sizes)


def solution(mesh):
    return jax.shard_map(
        on_device,
        mesh=mesh,
        in_specs=(P(("grp", "tm"), "tile", None), P(), P(None, "tile"), P(("grp", "tm"))),
        out_specs=P(("grp", "tm"), "tile", None),
        check_vma=False,
    )
```
